128 devices in a mesh: dp: 32 (over y, z, x_lo), tensor: 4 (over x_hi, core).
Axes of the slice: x: 4 (x_hi: 2, x_lo: 2; x = x_hi * 2 + x_lo), y: 4, z: 4, core: 2. Of those that a mesh axis runs over, the one named last changes fastest.
Arguments:
- tokens: bfloat16 [16384, 2304], P('dp'), may hold values from -6 to 6
- cotangent: bfloat16 [16384, 2304], P('dp'), may hold values from -320 to 320
- lengths: int32 [256], P('dp'), may hold values from 16 to 64
- gate_weight: bfloat16 [2304, 4608], P(None, 'tensor'), may hold values from -0.125 to 0.125
- up_weight: bfloat16 [2304, 4608], P(None, 'tensor'), may hold values from -1 to 1
- down_weight: bfloat16 [4608, 2304], P('tensor'), may hold values from -1 to 1
Outputs:
- input_grad: bfloat16 [16384, 2304], P('dp', 'tensor')
- norm_ratio: float32 [256], P('dp')
- grad_gate: float32 [2304, 4608], P('dp', 'tensor')
- grad_up: float32 [2304, 4608], P('dp', 'tensor')
- grad_down: float32 [4608, 2304], P('tensor', 'dp')
The draws below stay inside these ranges and needn't reach their ends.
All inputs are finite; a program needn't handle non-finite values.
Results may differ from the reference program's by a relative error of at most 0.005.
Values sent between devices are 32-bit elements; how exact they have to be, the bound alone decides.
No kernel may reach another device: no remote copies, remote signals or barrier semaphores. Data moves between devices by JAX's collectives and lax.ppermute only.
A program may use at most 256 MiB of HBM per device.

```python
import math
import jax
import jax.numpy as jnp
from jax import lax

D = 2304
FFW = 4608
LEN = 64
SEQ_DEV = 8
SEQS = 256
TOKENS = 16384
N_DP = 32


def draw_cotangent(key, part):
    key = jax.random.fold_in(key, 7)
    seq_key, feat_key, tok_key, noise_key = jax.random.split(key, 4)
    seq_scale = jnp.exp(jax.random.uniform(seq_key, (SEQS, 1, 1), jnp.float32, math.log(0.1), math.log(10.0)))
    seq_rise = jnp.exp(math.log(3.0) * (jnp.arange(SEQS, dtype=jnp.float32) / SEQS - 0.5)).reshape(SEQS, 1, 1)
    feat_scale = jnp.exp(jax.random.uniform(feat_key, (1, 1, D), jnp.float32, 0.0, math.log(10.0))) / 4.64
    tok_scale = jnp.exp(jax.random.uniform(tok_key, (SEQS, LEN, 1), jnp.float32, math.log(0.5), math.log(2.0)))
    noise_vals = jnp.clip(jax.random.normal(noise_key, (SEQS, LEN, D), jnp.float32), -4.0, 4.0)
    value_entries = seq_scale * seq_rise * feat_scale * tok_scale * noise_vals
    return value_entries.reshape(SEQS * LEN, D).astype(jnp.bfloat16)


def draw_up_weight(key, part):
    key = jax.random.fold_in(key, 11)
    base_key, rough_key = jax.random.split(key, 2)
    columns = jnp.arange(FFW, dtype=jnp.float32) / FFW - 0.5
    rough_cols = jnp.exp(jax.random.uniform(rough_key, (1, FFW), jnp.float32, math.log(0.7), math.log(1.4)))
    col_rise = jnp.exp(math.log(3.0) * columns)[None, :]
    base_vals = jnp.clip(jax.random.normal(base_key, (D, FFW), jnp.float32), -4.0, 4.0)
    return (base_vals * col_rise * rough_cols / math.sqrt(D)).astype(jnp.bfloat16)


def draw_down_weight(key, part):
    key = jax.random.fold_in(key, 13)
    base_key, rough_key = jax.random.split(key, 2)
    rows = jnp.arange(FFW, dtype=jnp.float32) / FFW - 0.5
    rough_rows = jnp.exp(jax.random.uniform(rough_key, (FFW, 1), jnp.float32, math.log(0.7), math.log(1.4)))
    row_rise = jnp.exp(math.log(4.0) * rows)[:, None]
    base_vals = jnp.clip(jax.random.normal(base_key, (FFW, D), jnp.float32), -4.0, 4.0)
    return (base_vals * row_rise * rough_rows / math.sqrt(FFW)).astype(jnp.bfloat16)


def with_ends(result, key, least, largest):
    dims = result.shape
    spot = [jax.random.randint(jax.random.fold_in(key, axis), (), 0, dims[axis]) for axis in range(len(dims))]
    result = result.at[tuple(spot)].set(least)
    longest = dims.index(max(dims))
    spot[longest] = (spot[longest] + 1) % dims[longest]
    return result.at[tuple(spot)].set(largest)


def raised(drawn, own_key, source, target, blocks, factor):
    owner, partner = [(jnp.arange(drawn.shape[position]) // (drawn.shape[position] // blocks)).reshape([-1 if axis == position else 1 for axis in range(drawn.ndim)]) for position in (source, target)]
    chosen = jax.random.permutation(own_key, blocks)[partner]
    strong = (owner == chosen) | (owner == (partner + blocks // 2) % blocks)
    return jnp.where(strong, factor * drawn, drawn)


def levels(stream_key, shape, shards, least, largest):
    loudness = 1.0
    for dim, parts in shards:
        steps = jax.random.uniform(jax.random.fold_in(jax.random.fold_in(stream_key, 6), dim), (parts,), jnp.float32, least / len(shards), largest / len(shards))
        loudness = loudness * jnp.repeat(jnp.exp(steps), shape[dim] // parts).reshape((-1,) + (1,) * (len(shape) - 1 - dim))
    return loudness


def bell_draw(rng, dims, spread, reach, cuts=(), held_as=jnp.bfloat16):
    result = jax.random.normal(rng, dims, jnp.float32) * spread
    if len(cuts) > 0:
        result = levels(rng, dims, cuts, -0.22, 0.18) * result
    return jnp.clip(result, min=-reach, max=reach).astype(held_as)


def gaussian_with(key, dims, width, most, pieces, heavy, held_as=jnp.bfloat16):
    entries = width * jax.random.normal(key, dims, jnp.float32)
    if pieces:
        entries = entries * levels(key, dims, pieces, -0.22, 0.18)
    return jnp.clip(raised(entries, jax.random.fold_in(key, 3), *heavy), -most, most).astype(held_as)


def setup_inputs(seed: int = 0) -> dict:
    seeds = jax.random.split(jax.random.key(seed), 7)
    return {
        "tokens": gaussian_with(seeds[0], (TOKENS, D), 1.0, 6.0, ((0, 32),), (0, 1, 32, 2.75)),
        "cotangent": draw_cotangent(jax.random.fold_in(seeds[6], 71), 0),
        "lengths": with_ends(jax.random.randint(seeds[2], (SEQS,), LEN // 4, LEN + 1), jax.random.fold_in(seeds[2], 1), LEN // 4, LEN).astype(jnp.int32),
        "gate_weight": bell_draw(seeds[3], (D, FFW), D ** -0.5, 0.125, ((1, 4),)),
        "up_weight": draw_up_weight(jax.random.fold_in(seeds[6], 71), 0),
        "down_weight": draw_down_weight(jax.random.fold_in(seeds[6], 71), 0),
    }


def gelu_parts(pre_act):
    slope_k = math.sqrt(2.0 / math.pi)
    cubed = pre_act * pre_act * pre_act
    tanh_val = jnp.tanh(slope_k * (pre_act + 0.044715 * cubed))
    gelu_value = 0.5 * pre_act * (1.0 + tanh_val)
    gelu_slope = 0.5 * (1.0 + tanh_val) + 0.5 * pre_act * (1.0 - tanh_val * tanh_val) * slope_k * (1.0 + 3.0 * 0.044715 * pre_act * pre_act)
    return (gelu_value, gelu_slope)

def seq_gram(matrix, seq_count):
    block_list = matrix.astype(jnp.float32).reshape(seq_count, LEN, matrix.shape[1])
    return jnp.einsum('aej,avj->aev', block_list, block_list)

def reference(tokens, cotangent, lengths, gate_weight, up_weight, down_weight):
    row_count = SEQ_DEV * LEN
    clip_bound = 0.5 * math.sqrt(D * FFW * LEN)
    positions = jnp.arange(LEN, dtype=jnp.int32)

    def block_step(carry, inputs):
        acc_gate, acc_up, acc_down = carry
        token_block_slice, cot_block, length_block = inputs
        token_mask = (positions[None, :] < length_block[:, None]).reshape(row_count)
        masked = cot_block * token_mask[:, None].astype(cot_block.dtype)
        gate_pre = jnp.dot(token_block_slice, gate_weight, preferred_element_type=jnp.float32)
        up_pre = jnp.dot(token_block_slice, up_weight, preferred_element_type=jnp.float32)
        gelu_value, gelu_slope = gelu_parts(gate_pre)
        hidden_act = (gelu_value * up_pre).astype(jnp.bfloat16)
        d_hidden = jnp.dot(masked, down_weight.T, preferred_element_type=jnp.float32)
        d_gate = (d_hidden * up_pre * gelu_slope).astype(jnp.bfloat16)
        d_up = (d_hidden * gelu_value).astype(jnp.bfloat16)
        token_gram = seq_gram(token_block_slice, SEQ_DEV)
        norm_sq = lax.optimization_barrier(jnp.sum(token_gram * seq_gram(d_gate, SEQ_DEV), axis=(1, 2)))
        norm_sq = norm_sq + lax.optimization_barrier(jnp.sum(token_gram * seq_gram(d_up, SEQ_DEV), axis=(1, 2)))
        norm_sq = norm_sq + lax.optimization_barrier(jnp.sum(seq_gram(hidden_act, SEQ_DEV) * seq_gram(masked, SEQ_DEV), axis=(1, 2)))
        clip_ratio = jnp.sqrt(norm_sq) / clip_bound
        clip_factor = 1.0 / jnp.maximum(1.0, clip_ratio)
        clip_rows = jnp.repeat(clip_factor, LEN)
        raw_input = jnp.dot(d_gate, gate_weight.T, preferred_element_type=jnp.float32)
        raw_input = raw_input + jnp.dot(d_up, up_weight.T, preferred_element_type=jnp.float32)
        input_block = (raw_input * clip_rows[:, None]).astype(jnp.bfloat16)
        weight_row_list = clip_rows / (SEQ_DEV * N_DP)
        scaled_gate = (d_gate * weight_row_list[:, None]).astype(jnp.bfloat16)
        scaled_up = (d_up * weight_row_list[:, None]).astype(jnp.bfloat16)
        scaled_cot = (masked * weight_row_list[:, None]).astype(jnp.bfloat16)
        part_gate = jnp.dot(token_block_slice.T, scaled_gate, preferred_element_type=jnp.float32)
        part_up = jnp.dot(token_block_slice.T, scaled_up, preferred_element_type=jnp.float32)
        part_down = jnp.dot(hidden_act.T, scaled_cot, preferred_element_type=jnp.float32)
        new_carry = (acc_gate + part_gate, acc_up + part_up, acc_down + part_down)
        return (new_carry, (input_block, clip_ratio))
    start_carry = (jnp.zeros((D, FFW), jnp.float32), jnp.zeros((D, FFW), jnp.float32), jnp.zeros((FFW, D), jnp.float32))
    stacked = (tokens.reshape(N_DP, row_count, D), cotangent.reshape(N_DP, row_count, D), lengths.reshape(N_DP, SEQ_DEV).astype(jnp.int32))
    final_carry, outputs = lax.scan(block_step, start_carry, stacked)
    input_blocks, clip_ratio_block_list = outputs
    grad_gate, grad_up, grad_down = final_carry
    return (input_blocks.reshape(N_DP * row_count, D), clip_ratio_block_list.reshape(N_DP * SEQ_DEV), grad_gate, grad_up, grad_down)
```

```python
import math

import jax
import jax.numpy as jnp
from jax import lax
from jax.sharding import PartitionSpec as P

D = 2304
FFW = 4608
LEN = 64
AXES = ("dp", "tensor")


def place(y, z, x, core):
    y, z, x = y % 4, z % 4, x % 4
    return ((y * 4 + z) * 2 + x % 2) * 4 + (x // 2) * 2 + core


def pairs(target):
    return [
        (place(y, z, x, core), place(*target(y, z, x, core)))
        for y in range(4)
        for z in range(4)
        for x in range(4)
        for core in range(2)
    ]


RING_Y = pairs(lambda y, z, x, core: (y + 1 - 2 * core, z, x, core))
RING_Z = pairs(lambda y, z, x, core: (y, z + 1 - 2 * core, x, core))
RING_X = pairs(lambda y, z, x, core: (y, z, x + 1 - 2 * core, core))
CORES = pairs(lambda y, z, x, core: (y, z, x, 1 - core))
X_LO = pairs(lambda y, z, x, core: (y, z, x ^ 1, core))
X_HI = pairs(lambda y, z, x, core: (y, z, x ^ 2, core))


def send(value, route):
    return lax.optimization_barrier(lax.ppermute(lax.optimization_barrier(value), AXES, route))


def gelu_parts(pre_act):
    slope_k = math.sqrt(2.0 / math.pi)
    cubed = pre_act * pre_act * pre_act
    tanh_val = jnp.tanh(slope_k * (pre_act + 0.044715 * cubed))
    gelu_value = 0.5 * pre_act * (1.0 + tanh_val)
    gelu_slope = 0.5 * (1.0 + tanh_val) + 0.5 * pre_act * (1.0 - tanh_val * tanh_val) * slope_k * (
        1.0 + 3.0 * 0.044715 * pre_act * pre_act
    )
    return (gelu_value, gelu_slope)


def seq_gram(matrix, seq_count):
    block_list = matrix.reshape(seq_count, LEN, matrix.shape[1])
    return jnp.einsum("aej,avj->aev", block_list, block_list, preferred_element_type=jnp.float32)


def cross_rows(left, right):
    return lax.dot_general(
        left, right, (((0,), (0,)), ((), ())), preferred_element_type=jnp.float32
    )


def forward(tokens, masked, gate_weight, up_weight, down_weight):
    gate_pre = jnp.dot(tokens, gate_weight, preferred_element_type=jnp.float32)
    up_pre = jnp.dot(tokens, up_weight, preferred_element_type=jnp.float32)
    d_hidden = lax.dot_general(
        masked, down_weight, (((1,), (1,)), ((), ())), preferred_element_type=jnp.float32
    )
    gelu_value, gelu_slope = gelu_parts(gate_pre)
    hidden_act = (gelu_value * up_pre).astype(jnp.bfloat16)
    d_gate = (d_hidden * up_pre * gelu_slope).astype(jnp.bfloat16)
    d_up = (d_hidden * gelu_value).astype(jnp.bfloat16)
    return hidden_act, d_gate, d_up


def ring_sum(take, here, way, route):
    part = take((here + 3 * way) % 4)
    for hops in (2, 1, 0):
        part = send(part, route) + take((here + hops * way) % 4)
    return part


def per_device(tokens, cotangent, lengths, gate_weight, up_weight, down_weight):
    seq_count = lengths.shape[0]
    row_count, width = tokens.shape
    total_seqs = seq_count * lax.axis_size("dp")
    clip_bound = 0.5 * math.sqrt(D * FFW * LEN)
    dp, tensor = lax.axis_index("dp"), lax.axis_index("tensor")
    y, z, x_lo = dp // 8, (dp // 2) % 4, dp % 2
    x_hi, core = tensor // 2, tensor % 2
    way = 1 - 2 * core
    half = row_count // 2
    strip = width // 32

    def far_order(by_seq):
        halves = by_seq.reshape(2, seq_count // 2)
        return jnp.where(core == 0, halves, halves[::-1]).reshape(seq_count)

    positions = jnp.arange(LEN, dtype=jnp.int32)

    def live(seq_lengths):
        return (positions[None, :] < seq_lengths[:, None]).reshape(row_count)[:, None]

    def fetch(rows, far_mask):
        wide = lax.dynamic_slice_in_dim(rows, core * half, half, 0).astype(jnp.float32)
        mine = send(wide, RING_X)
        theirs = send(mine, CORES)
        return (jnp.concatenate([mine, theirs], axis=0) * far_mask).astype(jnp.bfloat16)

    masked = cotangent * live(lengths).astype(jnp.bfloat16)
    far_mask = live(far_order(send(lengths, X_LO))).astype(jnp.float32)
    far_tokens = fetch(tokens, far_mask)
    far_masked = fetch(cotangent, far_mask)

    hidden_act, d_gate, d_up = forward(tokens, masked, gate_weight, up_weight, down_weight)
    token_gram = seq_gram(tokens, seq_count)
    gate_part = jnp.sum(token_gram * seq_gram(d_gate, seq_count), axis=(1, 2))
    up_part = jnp.sum(token_gram * seq_gram(d_up, seq_count), axis=(1, 2))
    down_part = jnp.sum(seq_gram(hidden_act, seq_count) * seq_gram(masked, seq_count), axis=(1, 2))
    norm_sq = lax.psum(gate_part + up_part + down_part, "tensor")
    clip_ratio = jnp.sqrt(norm_sq) / clip_bound
    clip_factor = 1.0 / jnp.maximum(1.0, clip_ratio)
    far_factor = far_order(send(clip_factor, X_LO))

    def scaled(rows, factor):
        return (rows * (jnp.repeat(factor, LEN) / total_seqs)[:, None]).astype(jnp.bfloat16)

    down_full = cross_rows(scaled(masked, clip_factor), hidden_act)
    hidden_units = down_full.shape[1]
    cuts = ((0, 640), (640, hidden_units)) if hidden_units > 640 else ((0, hidden_units),)
    down_full = down_full.reshape(4, 4, 2, strip, hidden_units)

    def sum_y_first(whole, lo, hi):
        def at_y(k):
            return lax.dynamic_index_in_dim(whole, k, 0, keepdims=False)[:, :, lo:hi]

        row = ring_sum(at_y, y, way, RING_Y)
        return ring_sum(
            lambda k: lax.dynamic_index_in_dim(row, k, 0, keepdims=False), z, way, RING_Z
        )

    def sum_z_first(whole, lo, hi):
        def at_z(k):
            return lax.dynamic_index_in_dim(whole, k, 1, keepdims=False)[:, :, lo:hi]

        column = ring_sum(at_z, z, way, RING_Z)
        return ring_sum(
            lambda k: lax.dynamic_index_in_dim(column, k, 0, keepdims=False), y, way, RING_Y
        )

    down_sums = [
        jnp.concatenate([fn(down_full[:, :, side], lo, hi) for lo, hi in cuts], axis=1)
        for side, fn in ((0, sum_y_first), (1, sum_z_first))
    ]

    partial_value = lax.dot_general(
        gate_weight, d_gate, (((1,), (1,)), ((), ())), preferred_element_type=jnp.float32
    ) + lax.dot_general(
        up_weight, d_up, (((1,), (1,)), ((), ())), preferred_element_type=jnp.float32
    )
    partial_value = partial_value * jnp.repeat(clip_factor, LEN)[None, :]
    partial_value = partial_value.reshape(2, 2, width // 4, row_count)
    part = send(lax.dynamic_index_in_dim(partial_value, 1 - core, 1, keepdims=False), CORES)
    part = part + lax.dynamic_index_in_dim(partial_value, core, 1, keepdims=False)
    summed_input = send(lax.dynamic_index_in_dim(part, 1 - x_hi, 0, keepdims=False), X_HI)
    summed_input = summed_input + lax.dynamic_index_in_dim(part, x_hi, 0, keepdims=False)
    input_grad = summed_input.T.astype(jnp.bfloat16)

    column_at = jnp.arange(width // 2, dtype=jnp.int32)
    source = (column_at // strip) * (2 * strip) + x_lo * strip + column_at % strip
    pick = (jnp.arange(width, dtype=jnp.int32)[:, None] == source[None, :]).astype(jnp.bfloat16)

    def picked(rows):
        return jnp.dot(rows, pick, preferred_element_type=jnp.float32).astype(jnp.bfloat16)

    _, far_gate, far_up = forward(far_tokens, far_masked, gate_weight, up_weight, down_weight)
    near_cols, far_cols = picked(tokens), picked(far_tokens)
    gate_half = cross_rows(near_cols, scaled(d_gate, clip_factor))
    gate_half = gate_half + cross_rows(far_cols, scaled(far_gate, far_factor))
    up_half = cross_rows(near_cols, scaled(d_up, clip_factor))
    up_half = up_half + cross_rows(far_cols, scaled(far_up, far_factor))
    gate_half = gate_half.reshape(4, 4, strip, hidden_units)
    up_half = up_half.reshape(4, 4, strip, hidden_units)
    grad_gate = jnp.concatenate([sum_y_first(gate_half, lo, hi) for lo, hi in cuts], axis=1)
    grad_up = jnp.concatenate([sum_z_first(up_half, lo, hi) for lo, hi in cuts], axis=1)

    kept = jnp.where(x_lo == 0, down_sums[0], down_sums[1])
    given = jnp.where(x_lo == 0, down_sums[1], down_sums[0])
    grad_down = (kept + send(given, X_LO)).T
    return (input_grad, clip_ratio, grad_gate, grad_up, grad_down)


def solution(mesh):
    placed = (
        P("dp", None),
        P("dp", None),
        P("dp"),
        P(None, "tensor"),
        P(None, "tensor"),
        P("tensor", None),
    )
    return jax.shard_map(
        per_device,
        mesh=mesh,
        in_specs=placed,
        out_specs=(
            P("dp", "tensor"),
            P("dp"),
            P("dp", "tensor"),
            P("dp", "tensor"),
            P("tensor", "dp"),
        ),
        check_vma=False,
    )
```

```python
import functools
import math

import jax
import jax.numpy as jnp
from jax import lax
from jax.experimental import pallas as pl
from jax.experimental.pallas import tpu as pltpu
from jax.sharding import PartitionSpec as P

D = 2304
FFW = 4608
LEN = 64
AXES = ("dp", "tensor")


def place(y, z, x, core):
    y, z, x = y % 4, z % 4, x % 4
    return ((y * 4 + z) * 2 + x % 2) * 4 + (x // 2) * 2 + core


def pairs(target):
    return [
        (place(y, z, x, core), place(*target(y, z, x, core)))
        for y in range(4)
        for z in range(4)
        for x in range(4)
        for core in range(2)
    ]


RING_YZ = pairs(
    lambda y, z, x, core: (y, z + 1 - 2 * core, x, core) if x % 2 == 0 else (y + 1 - 2 * core, z, x, core)
)
RING_Y = pairs(lambda y, z, x, core: (y + 1 - 2 * core, z, x, core))
RING_Z = pairs(lambda y, z, x, core: (y, z + 1 - 2 * core, x, core))
RING_X = pairs(lambda y, z, x, core: (y, z, x + 1 - 2 * core, core))
CORES = pairs(lambda y, z, x, core: (y, z, x, 1 - core))
X_LO = pairs(lambda y, z, x, core: (y, z, x ^ 1, core))
X_HI = pairs(lambda y, z, x, core: (y, z, x ^ 2, core))


def send(value, route):
    return lax.optimization_barrier(lax.ppermute(lax.optimization_barrier(value), AXES, route))


def nothing(*refs):
    pass


def after(value, *others):
    anywhere = pl.BlockSpec(memory_space=pl.ANY)
    return pl.pallas_call(
        nothing,
        out_shape=jax.ShapeDtypeStruct(value.shape, value.dtype),
        in_specs=[anywhere] * (1 + len(others)),
        out_specs=anywhere,
        input_output_aliases={0: 0},
        cost_estimate=pl.CostEstimate(flops=0, bytes_accessed=0, transcendentals=0),
        compiler_params=pltpu.CompilerParams(vmem_limit_bytes=1 << 20),
    )(value, *others)


def later(index, *others):
    return after(jnp.reshape(index, (1,)), *others)[0]


def gelu_parts(pre_act):
    slope_k = math.sqrt(2.0 / math.pi)
    cubed = pre_act * pre_act * pre_act
    tanh_val = jnp.tanh(slope_k * (pre_act + 0.044715 * cubed))
    gelu_value = 0.5 * pre_act * (1.0 + tanh_val)
    gelu_slope = 0.5 * (1.0 + tanh_val) + 0.5 * pre_act * (1.0 - tanh_val * tanh_val) * slope_k * (
        1.0 + 3.0 * 0.044715 * pre_act * pre_act
    )
    return (gelu_value, gelu_slope)


def cross_rows(left, right):
    return lax.dot_general(
        left, right, (((0,), (0,)), ((), ())), preferred_element_type=jnp.float32
    )


def by_block(rows, width):
    half = rows.shape[0] // 2
    return [
        lax.dot_general(part, part, (((1,), (1,)), ((), ())), preferred_element_type=jnp.float32)
        for part in (rows[:half], rows[half:])
    ]


def block_kernel(near, *refs):
    if near:
        tokens, masked, gate_w, up_w, down_w, hidden, d_gate, d_up, norms = refs[:9]
        tokens_v, masked_v, gate_v, up_v, down_v, pair_gram, hidden_gram, sems = refs[9:]
    else:
        tokens, masked, gate_w, up_w, down_w, hidden, d_gate, d_up = refs[:8]
        tokens_v, masked_v, gate_v, up_v, down_v, sems = refs[8:]
    units = gate_w.shape[1]
    tile = 256
    full, tail = units // tile, units % tile
    spans = [(k * tile, tile) for k in range(full)] + ([(full * tile, tail)] if tail else [])

    def copies(k, start, size):
        cols = pl.ds(start, size)
        return (
            pltpu.make_async_copy(gate_w.at[:, cols], gate_v.at[:, cols], sems.at[0, k]),
            pltpu.make_async_copy(up_w.at[:, cols], up_v.at[:, cols], sems.at[1, k]),
            pltpu.make_async_copy(down_w.at[cols, :], down_v.at[cols, :], sems.at[2, k]),
        )

    rows_in = (
        pltpu.make_async_copy(tokens, tokens_v, sems.at[0, len(spans)]),
        pltpu.make_async_copy(masked, masked_v, sems.at[1, len(spans)]),
    )
    for copy in rows_in:
        copy.start()
    for k, (start, size) in enumerate(spans):
        for copy in copies(k, start, size):
            copy.start()
    for copy in rows_in:
        copy.wait()
    if near:
        pair_gram[...] = jnp.zeros_like(pair_gram)
        hidden_gram[...] = jnp.zeros_like(hidden_gram)

    def work(k, start, size):
        for copy in copies(k, start, size):
            copy.wait()
        cols = pl.ds(start, size)
        gate_pre = jnp.dot(tokens_v[...], gate_v[:, cols], preferred_element_type=jnp.float32)
        up_pre = jnp.dot(tokens_v[...], up_v[:, cols], preferred_element_type=jnp.float32)
        d_hidden = lax.dot_general(
            masked_v[...], down_v[cols, :], (((1,), (1,)), ((), ())), preferred_element_type=jnp.float32
        )
        gelu_value, gelu_slope = gelu_parts(gate_pre)
        gate_rows = (d_hidden * up_pre * gelu_slope).astype(jnp.bfloat16)
        up_rows = (d_hidden * gelu_value).astype(jnp.bfloat16)
        hidden_rows = (gelu_value * up_pre).astype(jnp.bfloat16)
        hidden[:, cols], d_gate[:, cols], d_up[:, cols] = hidden_rows, gate_rows, up_rows
        if near:
            for k, (gate_gram, up_gram, own_gram) in enumerate(
                zip(by_block(gate_rows, size), by_block(up_rows, size), by_block(hidden_rows, size))
            ):
                pair_gram[k] += gate_gram + up_gram
                hidden_gram[k] += own_gram

    if full:
        lax.fori_loop(0, full, lambda k, _: (work(k, pl.multiple_of(k * tile, tile), tile), 0)[1], 0)
    if tail:
        work(full, full * tile, tail)
    if near:
        half = tokens_v.shape[0] // 2
        row_seq = lax.broadcasted_iota(jnp.int32, (half, half), 0) // LEN
        col_seq = lax.broadcasted_iota(jnp.int32, (half, half), 1) // LEN
        token_grams, masked_grams = by_block(tokens_v[...], 0), by_block(masked_v[...], 0)
        for k in range(2):
            total = token_grams[k] * pair_gram[k] + masked_grams[k] * hidden_gram[k]
            for seq in range(half // LEN):
                own = jnp.where((row_seq == seq) & (col_seq == seq), total, 0.0)
                lanes = jnp.sum(own, axis=0, keepdims=True)
                at = k * (half // LEN) + seq
                norms[at : at + 1, :] = jnp.broadcast_to(
                    jnp.sum(lanes, axis=1, keepdims=True), (1, norms.shape[1])
                )


def block(near, tokens, masked, gate_weight, up_weight, down_weight):
    rows, units = tokens.shape[0], gate_weight.shape[1]
    count = units // 256 + (1 if units % 256 else 0)
    anywhere, here = pl.BlockSpec(memory_space=pl.ANY), pl.BlockSpec(memory_space=pltpu.VMEM)
    hidden = jax.ShapeDtypeStruct((rows, units), jnp.bfloat16)
    grams = [pltpu.VMEM((2, rows // 2, rows // 2), jnp.float32)] * 2
    args = (tokens, masked, gate_weight, up_weight, down_weight)
    return pl.pallas_call(
        functools.partial(block_kernel, near),
        out_shape=[hidden] * 3 + [jax.ShapeDtypeStruct((rows // LEN, 128), jnp.float32)] if near else [hidden] * 3,
        in_specs=[anywhere] * 5,
        out_specs=[here] * (4 if near else 3),
        scratch_shapes=[pltpu.VMEM(array.shape, array.dtype) for array in args]
        + (grams if near else [])
        + [pltpu.SemaphoreType.DMA((3, count + 1))],
        compiler_params=pltpu.CompilerParams(vmem_limit_bytes=44 << 20),
        cost_estimate=pl.CostEstimate(flops=0, bytes_accessed=0, transcendentals=0),
    )(*args)


def input_kernel(gate_w, up_w, d_gate, d_up, weight, last, out):
    total = lax.dot_general(gate_w[...], d_gate[...], (((1,), (1,)), ((), ())), preferred_element_type=jnp.float32)
    total += lax.dot_general(up_w[...], d_up[...], (((1,), (1,)), ((), ())), preferred_element_type=jnp.float32)
    out[0] = total * weight[...]


def input_part(gate_weight, up_weight, d_gate, d_up, weight, last):
    width, units = gate_weight.shape
    rows = d_gate.shape[0]
    whole = pl.BlockSpec((rows, units), lambda k: (0, 0))
    part = pl.BlockSpec((width // 4, units), lambda k: (k, 0))
    return pl.pallas_call(
        input_kernel,
        grid=(4,),
        out_shape=jax.ShapeDtypeStruct((4, width // 4, rows), jnp.float32),
        in_specs=[part, part, whole, whole, pl.BlockSpec((1, rows), lambda k: (0, 0)), pl.BlockSpec(memory_space=pl.ANY)],
        out_specs=pl.BlockSpec((1, width // 4, rows), lambda k: (k, 0, 0)),
        compiler_params=pltpu.CompilerParams(vmem_limit_bytes=32 << 20),
        cost_estimate=pl.CostEstimate(flops=0, bytes_accessed=0, transcendentals=0),
    )(gate_weight, up_weight, d_gate, d_up, weight, last)


def ring_sum(take, here, way, route, part=None):
    part = take((here + 3 * way) % 4) if part is None else part
    for hops in (2, 1, 0):
        part = send(part, route) + take((here + hops * way) % 4)
    return part


def product_kernel(scale_left, near_l, near_r, near_w, far_l, far_r, far_w, out, near_v, far_v):
    if scale_left:
        near = (near_l[...].astype(jnp.float32) * near_w[...]).astype(jnp.bfloat16)
        far = (far_l[...].astype(jnp.float32) * far_w[...]).astype(jnp.bfloat16)
        total = jnp.dot(near, near_r[...], preferred_element_type=jnp.float32)
        out[...] = total + jnp.dot(far, far_r[...], preferred_element_type=jnp.float32)
    else:

        @pl.when(pl.program_id(0) == 0)
        def _():
            near_v[...] = (near_r[...].astype(jnp.float32) * near_w[...]).astype(jnp.bfloat16)
            far_v[...] = (far_r[...].astype(jnp.float32) * far_w[...]).astype(jnp.bfloat16)

        total = jnp.dot(near_l[...], near_v[...], preferred_element_type=jnp.float32)
        out[...] = total + jnp.dot(far_l[...], far_v[...], preferred_element_type=jnp.float32)


def product(scale_left, near, far):
    count, rows = near[0].shape
    units = near[1].shape[1]
    tile = count // 4
    left = pl.BlockSpec((tile, rows), lambda k: (k, 0))
    right = pl.BlockSpec((rows, units), lambda k: (0, 0))
    weight = pl.BlockSpec((1, rows) if scale_left else (rows, 1), lambda k: (0, 0))
    scaled = pltpu.VMEM((rows, units), jnp.bfloat16)
    shape = (1, rows) if scale_left else (rows, 1)
    return pl.pallas_call(
        functools.partial(product_kernel, scale_left),
        grid=(4,),
        out_shape=jax.ShapeDtypeStruct((count, units), jnp.float32),
        in_specs=[left, right, weight] * 2,
        out_specs=pl.BlockSpec((tile, units), lambda k: (k, 0)),
        scratch_shapes=[scaled, scaled],
        compiler_params=pltpu.CompilerParams(vmem_limit_bytes=28 << 20),
        cost_estimate=pl.CostEstimate(flops=4 * rows * count * units, bytes_accessed=12 << 20, transcendentals=0),
    )(*(a if a.ndim == 2 else a.reshape(shape) for a in near + far))


def per_device(tokens, cotangent, lengths, gate_weight, up_weight, down_weight):
    seq_count = lengths.shape[0]
    row_count, width = tokens.shape
    total_seqs = seq_count * lax.axis_size("dp")
    clip_bound = 0.5 * math.sqrt(D * FFW * LEN)
    dp, tensor = lax.axis_index("dp"), lax.axis_index("tensor")
    y, z, x_lo = dp // 8, (dp // 2) % 4, dp % 2
    x_hi, core = tensor // 2, tensor % 2
    way = 1 - 2 * core
    half = row_count // 2
    strip = width // 32

    def far_order(by_seq):
        halves = by_seq.reshape(2, seq_count // 2)
        return jnp.where(core == 0, halves, halves[::-1]).reshape(seq_count)

    positions = jnp.arange(LEN, dtype=jnp.int32)

    def live(seq_lengths):
        return (positions[None, :] < seq_lengths[:, None]).reshape(row_count)[:, None]

    def whole(mine, theirs, far_mask):
        return (jnp.concatenate([mine, theirs], axis=0) * far_mask).astype(jnp.bfloat16)

    masked = cotangent * live(lengths).astype(jnp.bfloat16)
    token_half = send(
        jnp.concatenate(
            [
                lax.dynamic_slice_in_dim(tokens, core * half, half, 0).astype(jnp.float32),
                jnp.broadcast_to(lengths.astype(jnp.float32)[:, None], (seq_count, width)),
            ]
        ),
        RING_X,
    )
    cot_half = send(lax.dynamic_slice_in_dim(cotangent, core * half, half, 0).astype(jnp.float32), RING_X)
    hidden_act, d_gate, d_up, norms = block(True, tokens, masked, gate_weight, up_weight, down_weight)

    column_at = jnp.arange(width // 2, dtype=jnp.int32)
    source = (column_at // strip) * (2 * strip) + later(x_lo, norms) * strip + column_at % strip
    pick = (jnp.arange(width, dtype=jnp.int32)[:, None] == source[None, :]).astype(jnp.bfloat16)

    def picked(rows):
        return lax.dot_general(
            pick, rows, (((0,), (1,)), ((), ())), preferred_element_type=jnp.float32
        ).astype(jnp.bfloat16)

    near_tokens, near_cot = picked(tokens), picked(masked)
    norm_sq = lax.psum(after(norms[:, 0], near_tokens, near_cot), "tensor")
    clip_ratio = jnp.sqrt(norm_sq) / clip_bound
    clip_factor = 1.0 / jnp.maximum(1.0, clip_ratio)

    far_mask = live(far_order(token_half[half:, 0])).astype(jnp.float32)
    far_tokens = whole(token_half[:half], send(token_half[:half], CORES), far_mask)
    far_masked = whole(cot_half, send(cot_half, CORES), far_mask)
    far_factor = far_order(send(clip_factor, X_LO))
    far_hidden, far_gate, far_up = block(False, far_tokens, far_masked, gate_weight, up_weight, down_weight)
    far_cols, far_cot = picked(far_tokens), picked(far_masked)

    near_weight = jnp.repeat(clip_factor, LEN) / total_seqs
    far_weight = jnp.repeat(far_factor, LEN) / total_seqs
    gate_half = product(False, (near_tokens, d_gate, near_weight), (far_cols, far_gate, far_weight))
    up_half = product(False, (near_tokens, d_up, near_weight), (far_cols, far_up, far_weight))
    down_half = product(True, (near_cot, hidden_act, near_weight), (far_cot, far_hidden, far_weight))
    units = gate_half.shape[1]
    split = units // 256 * 128 + units % 256

    def by_y(grad, lo, hi):
        grad = grad.reshape(4, 4, strip, units)
        return lambda k: lax.dynamic_slice(grad, (k, 0, 0, lo), (1, 4, strip, hi - lo)).reshape(4, strip, hi - lo)

    def by_z(grad, lo, hi):
        grad = grad.reshape(4, 4, strip, units)
        return lambda k: lax.dynamic_slice(grad, (0, k, 0, lo), (4, 1, strip, hi - lo)).reshape(4, strip, hi - lo)

    def line(rows):
        return lambda k: lax.dynamic_index_in_dim(rows, k, 0, keepdims=False)

    takes = [
        (by_y(gate_half, 0, units), y, RING_Y, z, RING_Z),
        (by_z(up_half, 0, units), z, RING_Z, y, RING_Y),
        (by_y(down_half, 0, split), y, RING_Y, z, RING_Z),
        (by_z(down_half, split, units), z, RING_Z, y, RING_Y),
    ]
    parts = [take((here + 3 * way) % 4) for take, here, _, _, _ in takes]
    partial_value = input_part(
        gate_weight, up_weight, d_gate, d_up, jnp.repeat(clip_factor, LEN)[None, :], parts[3]
    )
    partial_value = partial_value.reshape(2, 2, width // 4, row_count)
    part = send(lax.dynamic_index_in_dim(partial_value, 1 - core, 1, keepdims=False), CORES)
    part = part + lax.dynamic_index_in_dim(partial_value, core, 1, keepdims=False)
    summed_input = send(lax.dynamic_index_in_dim(part, 1 - x_hi, 0, keepdims=False), X_HI)
    summed_input = summed_input + lax.dynamic_index_in_dim(part, x_hi, 0, keepdims=False)
    input_grad = summed_input.T.astype(jnp.bfloat16)

    rows = [ring_sum(take, here, way, route, part) for (take, here, route, _, _), part in zip(takes, parts)]
    sums = [ring_sum(line(row), here, way, route) for row, (_, _, _, here, route) in zip(rows, takes)]
    grad_gate, grad_up = sums[0], sums[1]
    grad_down = jnp.concatenate(sums[2:], axis=1).T
    return (input_grad, clip_ratio, grad_gate, grad_up, grad_down)


def solution(mesh):
    placed = (
        P("dp", None),
        P("dp", None),
        P("dp"),
        P(None, "tensor"),
        P(None, "tensor"),
        P("tensor", None),
    )
    return jax.shard_map(
        per_device,
        mesh=mesh,
        in_specs=placed,
        out_specs=(
            P("dp", "tensor"),
            P("dp"),
            P("dp", "tensor"),
            P("dp", "tensor"),
            P("tensor", "dp"),
        ),
        check_vma=False,
    )
```

```python
import functools
import math

import jax
import jax.numpy as jnp
from jax import lax
from jax.experimental import pallas as pl
from jax.experimental.pallas import tpu as pltpu
from jax.sharding import PartitionSpec as P

D = 2304
FFW = 4608
LEN = 64
AXES = ("dp", "tensor")


def place(y, z, x, core):
    y, z, x = y % 4, z % 4, x % 4
    return ((y * 4 + z) * 2 + x % 2) * 4 + (x // 2) * 2 + core


def pairs(target):
    return [
        (place(y, z, x, core), place(*target(y, z, x, core)))
        for y in range(4)
        for z in range(4)
        for x in range(4)
        for core in range(2)
    ]


RING_YZ = pairs(
    lambda y, z, x, core: (y, z + 1 - 2 * core, x, core) if x % 2 == 0 else (y + 1 - 2 * core, z, x, core)
)
RING_Y = pairs(lambda y, z, x, core: (y + 1 - 2 * core, z, x, core))
RING_Z = pairs(lambda y, z, x, core: (y, z + 1 - 2 * core, x, core))
RING_X = pairs(lambda y, z, x, core: (y, z, x + 1 - 2 * core, core))
CORES = pairs(lambda y, z, x, core: (y, z, x, 1 - core))
X_LO = pairs(lambda y, z, x, core: (y, z, x ^ 1, core))
X_HI = pairs(lambda y, z, x, core: (y, z, x ^ 2, core))


def send(value, route):
    return lax.optimization_barrier(lax.ppermute(lax.optimization_barrier(value), AXES, route))


def nothing(*refs):
    pass


def after(value, *others):
    anywhere = pl.BlockSpec(memory_space=pl.ANY)
    return pl.pallas_call(
        nothing,
        out_shape=jax.ShapeDtypeStruct(value.shape, value.dtype),
        in_specs=[anywhere] * (1 + len(others)),
        out_specs=anywhere,
        input_output_aliases={0: 0},
        cost_estimate=pl.CostEstimate(flops=0, bytes_accessed=0, transcendentals=0),
        compiler_params=pltpu.CompilerParams(vmem_limit_bytes=1 << 20),
    )(value, *others)


def together(*values):
    anywhere = pl.BlockSpec(memory_space=pl.ANY)
    return pl.pallas_call(
        nothing,
        out_shape=[jax.ShapeDtypeStruct(value.shape, value.dtype) for value in values],
        in_specs=[anywhere] * len(values),
        out_specs=[anywhere] * len(values),
        input_output_aliases={k: k for k in range(len(values))},
        cost_estimate=pl.CostEstimate(flops=0, bytes_accessed=0, transcendentals=0),
        compiler_params=pltpu.CompilerParams(vmem_limit_bytes=1 << 20),
    )(*values)


def later(index, *others):
    return after(jnp.reshape(index, (1,)), *others)[0]


def gelu_parts(pre_act):
    slope_k = math.sqrt(2.0 / math.pi)
    cubed = pre_act * pre_act * pre_act
    tanh_val = jnp.tanh(slope_k * (pre_act + 0.044715 * cubed))
    gelu_value = 0.5 * pre_act * (1.0 + tanh_val)
    gelu_slope = 0.5 * (1.0 + tanh_val) + 0.5 * pre_act * (1.0 - tanh_val * tanh_val) * slope_k * (
        1.0 + 3.0 * 0.044715 * pre_act * pre_act
    )
    return (gelu_value, gelu_slope)


def cross_rows(left, right):
    return lax.dot_general(
        left, right, (((0,), (0,)), ((), ())), preferred_element_type=jnp.float32
    )


def by_block(rows, width):
    half = rows.shape[0] // 2
    return [
        lax.dot_general(part, part, (((1,), (1,)), ((), ())), preferred_element_type=jnp.float32)
        for part in (rows[:half], rows[half:])
    ]


def block_kernel(near, *refs):
    if near:
        tokens, masked, gate_w, up_w, down_w, hidden, d_gate, d_up, norms = refs[:9]
        tokens_v, masked_v, gate_v, up_v, down_v, pair_gram, hidden_gram, sems = refs[9:]
    else:
        tokens, masked, gate_w, up_w, down_w, hidden, d_gate, d_up = refs[:8]
        tokens_v, masked_v, gate_v, up_v, down_v, sems = refs[8:]
    units = gate_w.shape[1]
    tile = 256
    full, tail = units // tile, units % tile
    spans = [(k * tile, tile) for k in range(full)] + ([(full * tile, tail)] if tail else [])

    def copies(k, start, size):
        cols = pl.ds(start, size)
        return (
            pltpu.make_async_copy(gate_w.at[:, cols], gate_v.at[:, cols], sems.at[0, k]),
            pltpu.make_async_copy(up_w.at[:, cols], up_v.at[:, cols], sems.at[1, k]),
            pltpu.make_async_copy(down_w.at[cols, :], down_v.at[cols, :], sems.at[2, k]),
        )

    rows_in = (
        pltpu.make_async_copy(tokens, tokens_v, sems.at[0, len(spans)]),
        pltpu.make_async_copy(masked, masked_v, sems.at[1, len(spans)]),
    )
    for copy in rows_in:
        copy.start()
    for k, (start, size) in enumerate(spans):
        for copy in copies(k, start, size):
            copy.start()
    for copy in rows_in:
        copy.wait()
    if near:
        pair_gram[...] = jnp.zeros_like(pair_gram)
        hidden_gram[...] = jnp.zeros_like(hidden_gram)

    def work(k, start, size):
        for copy in copies(k, start, size):
            copy.wait()
        cols = pl.ds(start, size)
        gate_pre = jnp.dot(tokens_v[...], gate_v[:, cols], preferred_element_type=jnp.float32)
        up_pre = jnp.dot(tokens_v[...], up_v[:, cols], preferred_element_type=jnp.float32)
        d_hidden = lax.dot_general(
            masked_v[...], down_v[cols, :], (((1,), (1,)), ((), ())), preferred_element_type=jnp.float32
        )
        gelu_value, gelu_slope = gelu_parts(gate_pre)
        gate_rows = (d_hidden * up_pre * gelu_slope).astype(jnp.bfloat16)
        up_rows = (d_hidden * gelu_value).astype(jnp.bfloat16)
        hidden_rows = (gelu_value * up_pre).astype(jnp.bfloat16)
        hidden[:, cols], d_gate[:, cols], d_up[:, cols] = hidden_rows, gate_rows, up_rows
        if near:
            for k, (gate_gram, up_gram, own_gram) in enumerate(
                zip(by_block(gate_rows, size), by_block(up_rows, size), by_block(hidden_rows, size))
            ):
                pair_gram[k] += gate_gram + up_gram
                hidden_gram[k] += own_gram

    if full:
        lax.fori_loop(0, full, lambda k, _: (work(k, pl.multiple_of(k * tile, tile), tile), 0)[1], 0)
    if tail:
        work(full, full * tile, tail)
    if near:
        half = tokens_v.shape[0] // 2
        row_seq = lax.broadcasted_iota(jnp.int32, (half, half), 0) // LEN
        col_seq = lax.broadcasted_iota(jnp.int32, (half, half), 1) // LEN
        token_grams, masked_grams = by_block(tokens_v[...], 0), by_block(masked_v[...], 0)
        for k in range(2):
            total = token_grams[k] * pair_gram[k] + masked_grams[k] * hidden_gram[k]
            for seq in range(half // LEN):
                own = jnp.where((row_seq == seq) & (col_seq == seq), total, 0.0)
                lanes = jnp.sum(own, axis=0, keepdims=True)
                at = k * (half // LEN) + seq
                norms[at : at + 1, :] = jnp.broadcast_to(
                    jnp.sum(lanes, axis=1, keepdims=True), (1, norms.shape[1])
                )


def block(tokens, masked, gate_weight, up_weight, down_weight):
    near = True
    rows, units = tokens.shape[0], gate_weight.shape[1]
    count = units // 256 + (1 if units % 256 else 0)
    anywhere, here = pl.BlockSpec(memory_space=pl.ANY), pl.BlockSpec(memory_space=pltpu.VMEM)
    hidden = jax.ShapeDtypeStruct((rows, units), jnp.bfloat16)
    grams = [pltpu.VMEM((2, rows // 2, rows // 2), jnp.float32)] * 2
    args = (tokens, masked, gate_weight, up_weight, down_weight)
    return pl.pallas_call(
        functools.partial(block_kernel, near),
        out_shape=[hidden] * 3 + [jax.ShapeDtypeStruct((rows // LEN, 128), jnp.float32)] if near else [hidden] * 3,
        in_specs=[anywhere] * 5,
        out_specs=[here] * (4 if near else 3),
        scratch_shapes=[pltpu.VMEM(array.shape, array.dtype) for array in args]
        + (grams if near else [])
        + [pltpu.SemaphoreType.DMA((3, count + 1))],
        compiler_params=pltpu.CompilerParams(vmem_limit_bytes=44 << 20),
        cost_estimate=pl.CostEstimate(flops=0, bytes_accessed=0, transcendentals=0),
    )(*args)


def far_gate_kernel(tokens, gate_w, up_w, value, slope_up, hidden, tokens_v, gate_v, up_v, sems):
    units = gate_w.shape[1]
    spans = [(at, min(256, units - at)) for at in range(0, units, 256)]
    rows_in = pltpu.make_async_copy(tokens, tokens_v, sems.at[0, len(spans)])
    rows_in.start()
    weights_in = []
    for k, (start, size) in enumerate(spans):
        cols = pl.ds(start, size)
        weights_in.append(
            (
                pltpu.make_async_copy(gate_w.at[:, cols], gate_v.at[:, cols], sems.at[0, k]),
                pltpu.make_async_copy(up_w.at[:, cols], up_v.at[:, cols], sems.at[1, k]),
            )
        )
        for copy in weights_in[-1]:
            copy.start()
    rows_in.wait()
    for (start, size), both in zip(spans, weights_in):
        for copy in both:
            copy.wait()
        cols = pl.ds(start, size)
        gate_pre = jnp.dot(tokens_v[...], gate_v[:, cols], preferred_element_type=jnp.float32)
        up_pre = jnp.dot(tokens_v[...], up_v[:, cols], preferred_element_type=jnp.float32)
        gelu_value, gelu_slope = gelu_parts(gate_pre)
        value[:, cols] = gelu_value
        slope_up[:, cols] = up_pre * gelu_slope
        hidden[:, cols] = (gelu_value * up_pre).astype(jnp.bfloat16)


def far_gate_part(tokens, gate_weight, up_weight):
    rows, units = tokens.shape[0], gate_weight.shape[1]
    anywhere, here = pl.BlockSpec(memory_space=pl.ANY), pl.BlockSpec(memory_space=pltpu.VMEM)
    shape = (rows, units)
    args = (tokens, gate_weight, up_weight)
    return pl.pallas_call(
        far_gate_kernel,
        out_shape=[
            jax.ShapeDtypeStruct(shape, jnp.float32),
            jax.ShapeDtypeStruct(shape, jnp.float32),
            jax.ShapeDtypeStruct(shape, jnp.bfloat16),
        ],
        in_specs=[anywhere] * 3,
        out_specs=[here] * 3,
        scratch_shapes=[pltpu.VMEM(array.shape, array.dtype) for array in args]
        + [pltpu.SemaphoreType.DMA((2, (units + 255) // 256 + 1))],
        compiler_params=pltpu.CompilerParams(vmem_limit_bytes=40 << 20),
        cost_estimate=pl.CostEstimate(flops=4 * rows * tokens.shape[1] * units, bytes_accessed=18 << 20, transcendentals=0),
    )(*args)


def far_down_kernel(masked, down_w, value, slope_up, d_gate, d_up):
    d_hidden = lax.dot_general(
        masked[...], down_w[...], (((1,), (1,)), ((), ())), preferred_element_type=jnp.float32
    )
    d_gate[...] = (d_hidden * slope_up[...]).astype(jnp.bfloat16)
    d_up[...] = (d_hidden * value[...]).astype(jnp.bfloat16)


def far_down_part(masked, down_weight, value, slope_up):
    rows, units = value.shape
    tile = 384 if units % 384 == 0 else 128
    block_of = pl.BlockSpec((rows, tile), lambda k: (0, k))
    shape = jax.ShapeDtypeStruct((rows, units), jnp.bfloat16)
    return pl.pallas_call(
        far_down_kernel,
        grid=(units // tile,),
        out_shape=[shape, shape],
        in_specs=[
            pl.BlockSpec(masked.shape, lambda k: (0, 0)),
            pl.BlockSpec((tile, masked.shape[1]), lambda k: (k, 0)),
            block_of,
            block_of,
        ],
        out_specs=[block_of, block_of],
        compiler_params=pltpu.CompilerParams(vmem_limit_bytes=28 << 20),
        cost_estimate=pl.CostEstimate(flops=2 * rows * masked.shape[1] * units, bytes_accessed=14 << 20, transcendentals=0),
    )(masked, down_weight, value, slope_up)


def input_kernel(gate_w, up_w, d_gate, d_up, last, out):
    total = lax.dot_general(gate_w[...], d_gate[...], (((1,), (1,)), ((), ())), preferred_element_type=jnp.float32)
    total += lax.dot_general(up_w[...], d_up[...], (((1,), (1,)), ((), ())), preferred_element_type=jnp.float32)
    out[0] = total


def input_part(gate_weight, up_weight, d_gate, d_up, last):
    width, units = gate_weight.shape
    rows = d_gate.shape[0]
    whole = pl.BlockSpec((rows, units), lambda k: (0, 0))
    part = pl.BlockSpec((width // 4, units), lambda k: (k, 0))
    return pl.pallas_call(
        input_kernel,
        grid=(4,),
        out_shape=jax.ShapeDtypeStruct((4, width // 4, rows), jnp.float32),
        in_specs=[part, part, whole, whole, pl.BlockSpec(memory_space=pl.ANY)],
        out_specs=pl.BlockSpec((1, width // 4, rows), lambda k: (k, 0, 0)),
        compiler_params=pltpu.CompilerParams(vmem_limit_bytes=32 << 20),
        cost_estimate=pl.CostEstimate(flops=0, bytes_accessed=0, transcendentals=0),
    )(gate_weight, up_weight, d_gate, d_up, last)


class Ring:
    def __init__(self, take, here, way, route):
        self.take, self.here, self.way, self.route = take, here, way, route
        self.hops = 3
        self.part = take((here + 3 * way) % 4)

    def step(self, *others):
        self.hops -= 1
        part = send(self.part, self.route) + self.take((self.here + self.hops * self.way) % 4)
        self.part = after(part, *others) if others else part


def product_kernel(
    near_t, far_t, near_c, far_c, d_gate, far_gate, d_up, far_up, hidden, far_hidden, near_w, far_w, near_a, far_a,
    out, near_v, far_v,
):
    which, tile = pl.program_id(0), pl.program_id(1)
    for index, near, far in ((0, d_gate, far_gate), (1, d_up, far_up)):

        @pl.when((which == index) & (tile == 0))
        def _(near=near, far=far):
            near_v[...] = (near[...].astype(jnp.float32) * near_w[...]).astype(jnp.bfloat16)
            far_v[...] = (far[...].astype(jnp.float32) * far_w[...]).astype(jnp.bfloat16)

    @pl.when(which < 2)
    def _():
        total = jnp.dot(near_t[...], near_v[...], preferred_element_type=jnp.float32)
        out[...] = total + jnp.dot(far_t[...], far_v[...], preferred_element_type=jnp.float32)

    @pl.when(which == 2)
    def _():
        near = (near_c[...].astype(jnp.float32) * near_a[...]).astype(jnp.bfloat16)
        far = (far_c[...].astype(jnp.float32) * far_a[...]).astype(jnp.bfloat16)
        total = jnp.dot(near, hidden[...], preferred_element_type=jnp.float32)
        out[...] = total + jnp.dot(far, far_hidden[...], preferred_element_type=jnp.float32)


def products(*args):
    count, rows = args[0].shape
    units = args[4].shape[1]
    left = pl.BlockSpec((count // 4, rows), lambda which, tile: (tile, 0))
    right = pl.BlockSpec((rows, units), lambda which, tile: (0, 0))
    column = pl.BlockSpec((rows, 1), lambda which, tile: (0, 0))
    across = pl.BlockSpec((1, rows), lambda which, tile: (0, 0))
    scaled = pltpu.VMEM((rows, units), jnp.bfloat16)
    return pl.pallas_call(
        product_kernel,
        grid=(3, 4),
        out_shape=jax.ShapeDtypeStruct((count, 3 * units), jnp.float32),
        in_specs=[left] * 4 + [right] * 6 + [column] * 2 + [across] * 2,
        out_specs=pl.BlockSpec((count // 4, units), lambda which, tile: (tile, which)),
        scratch_shapes=[scaled, scaled],
        compiler_params=pltpu.CompilerParams(vmem_limit_bytes=36 << 20),
        cost_estimate=pl.CostEstimate(flops=12 * rows * count * units, bytes_accessed=28 << 20, transcendentals=0),
    )(*args)


def per_device(tokens, cotangent, lengths, gate_weight, up_weight, down_weight):
    seq_count = lengths.shape[0]
    row_count, width = tokens.shape
    total_seqs = seq_count * lax.axis_size("dp")
    clip_bound = 0.5 * math.sqrt(D * FFW * LEN)
    dp, tensor = lax.axis_index("dp"), lax.axis_index("tensor")
    y, z, x_lo = dp // 8, (dp // 2) % 4, dp % 2
    x_hi, core = tensor // 2, tensor % 2
    way = 1 - 2 * core
    half = row_count // 2
    strip = width // 32

    positions = jnp.arange(LEN, dtype=jnp.int32)
    live = (positions[None, :] < lengths[:, None]).reshape(row_count)[:, None]
    masked = cotangent * live.astype(jnp.bfloat16)

    def own_half(rows, start):
        return lax.dynamic_slice_in_dim(rows, start, half, 0).astype(jnp.float32)

    lanes = jnp.broadcast_to(live.astype(jnp.bfloat16), (row_count, 128))
    token_half = send(jnp.concatenate([own_half(tokens, core * half), own_half(lanes, core * half)], axis=1), RING_X)

    hidden_act, d_gate, d_up, norms = block(tokens, masked, gate_weight, up_weight, down_weight)

    def joined(mine, theirs, mask_mine, mask_theirs):
        return jnp.concatenate(
            [(mine * mask_mine).astype(jnp.bfloat16), (theirs * mask_theirs).astype(jnp.bfloat16)], axis=0
        )

    token_half = after(token_half, norms)
    token_rest = send(token_half, CORES)
    norm_sq = lax.psum(after(norms[:, 0], token_half), "tensor")
    clip_ratio = jnp.sqrt(norm_sq) / clip_bound
    clip_factor = 1.0 / jnp.maximum(1.0, clip_ratio)
    known = after(jnp.stack([core * half, x_lo]), clip_factor, token_rest)
    cot_half = send(own_half(cotangent, known[0]), RING_X)

    column_at = jnp.arange(width // 2, dtype=jnp.int32)
    source = (column_at // strip) * (2 * strip) + known[1] * strip + column_at % strip
    pick = (jnp.arange(width, dtype=jnp.int32)[:, None] == source[None, :]).astype(jnp.bfloat16)

    def picked(rows):
        return lax.dot_general(
            pick, rows, (((0,), (1,)), ((), ())), preferred_element_type=jnp.float32
        ).astype(jnp.bfloat16)

    near_tokens, near_cot = picked(tokens), picked(masked)
    masks = token_half[:, width : width + 1], token_rest[:, width : width + 1]
    far_tokens = joined(token_half[:, :width], token_rest[:, :width], *masks)
    value, slope_up, far_hidden = far_gate_part(far_tokens, gate_weight, up_weight)
    far_cols = picked(far_tokens)
    cot_half = after(cot_half, far_cols, far_hidden, near_tokens, near_cot)
    far_masked = joined(cot_half, send(cot_half, CORES), *masks)
    far_gate, far_up = far_down_part(far_masked, down_weight, value, slope_up)
    far_cot = picked(far_masked)

    def row_weight(by_seq, shift, axis):
        row_seq = (jnp.arange(row_count, dtype=jnp.int32) // LEN + shift) % seq_count
        seqs = jnp.arange(seq_count, dtype=jnp.int32)
        spread = jnp.expand_dims(row_seq, axis) == jnp.expand_dims(seqs, 1 - axis)
        return jnp.sum(jnp.where(spread, jnp.expand_dims(by_seq, 1 - axis), 0.0), axis=axis, keepdims=True)

    near_mean = clip_factor / total_seqs
    far_mean = send(after(clip_factor / total_seqs, cot_half), X_LO)
    shift = core * (seq_count // 2)
    near_weight, far_weight = row_weight(near_mean, 0, 1), row_weight(far_mean, shift, 1)
    near_across, far_across = row_weight(near_mean, 0, 0), row_weight(far_mean, shift, 0)

    grads = products(
        near_tokens, far_cols, near_cot, far_cot, d_gate, far_gate, d_up, far_up, hidden_act, far_hidden,
        near_weight, far_weight, near_across, far_across,
    )
    units = d_gate.shape[1]
    grads = grads.reshape(4, 4, strip, 3 * units)

    def by_y(lo, hi):
        return lambda k: lax.dynamic_slice(grads, (k, 0, 0, lo), (1, 4, strip, hi - lo)).reshape(4, strip, hi - lo)

    def by_z(lo, hi):
        return lambda k: lax.dynamic_slice(grads, (0, k, 0, lo), (4, 1, strip, hi - lo)).reshape(4, strip, hi - lo)

    def line(rows):
        return lambda k: lax.dynamic_index_in_dim(rows, k, 0, keepdims=False)

    tiles = 3 * units // 128
    ends = [0] + [(tiles * share // 27) * 128 for share in (7, 16, 22)] + [3 * units]
    flows = []
    for k in range(4):
        if k % 2 == 0:
            flows.append((by_y(ends[k], ends[k + 1]), y, RING_Y, z, RING_Z))
        else:
            flows.append((by_z(ends[k], ends[k + 1]), z, RING_Z, y, RING_Y))
    rings = [Ring(take, here, way, route) for take, here, route, _, _ in flows]

    partial_value = input_part(gate_weight, up_weight, d_gate, d_up, rings[3].part)
    partial_value = partial_value.reshape(2, 2, width // 4, row_count)
    part = send(lax.dynamic_index_in_dim(partial_value, 1 - core, 1, keepdims=False), CORES)
    part = part + lax.dynamic_index_in_dim(partial_value, core, 1, keepdims=False)
    summed_input = send(lax.dynamic_index_in_dim(part, 1 - x_hi, 0, keepdims=False), X_HI)
    summed_input = summed_input + lax.dynamic_index_in_dim(part, x_hi, 0, keepdims=False)
    input_grad = (summed_input * row_weight(clip_factor, 0, 0)).T.astype(jnp.bfloat16)

    for _ in range(3):
        for ring in rings:
            ring.step()
    rows = together(*[ring.part for ring in rings])
    rings = [Ring(line(row), here, way, route) for row, (_, _, _, here, route) in zip(rows, flows)]
    for _ in range(3):
        for ring in rings:
            ring.step()
    sums = jnp.concatenate([ring.part for ring in rings], axis=1)
    grad_gate, grad_up = sums[:, :units], sums[:, units : 2 * units]
    grad_down = sums[:, 2 * units :].T
    return (input_grad, clip_ratio, grad_gate, grad_up, grad_down)


def solution(mesh):
    placed = (
        P("dp", None),
        P("dp", None),
        P("dp"),
        P(None, "tensor"),
        P(None, "tensor"),
        P("tensor", None),
    )
    return jax.shard_map(
        per_device,
        mesh=mesh,
        in_specs=placed,
        out_specs=(
            P("dp", "tensor"),
            P("dp"),
            P("dp", "tensor"),
            P("dp", "tensor"),
            P("tensor", "dp"),
        ),
        check_vma=False,
    )
```

```python
import functools
import math

import jax
import jax.numpy as jnp
from jax import lax
from jax.experimental import pallas as pl
from jax.experimental.pallas import tpu as pltpu
from jax.sharding import PartitionSpec as P

D = 2304
FFW = 4608
LEN = 64
AXES = ("dp", "tensor")


def place(y, z, x, core):
    y, z, x = y % 4, z % 4, x % 4
    return ((y * 4 + z) * 2 + x % 2) * 4 + (x // 2) * 2 + core


def pairs(target):
    return [
        (place(y, z, x, core), place(*target(y, z, x, core)))
        for y in range(4)
        for z in range(4)
        for x in range(4)
        for core in range(2)
    ]


RING_YZ = pairs(
    lambda y, z, x, core: (y, z + 1 - 2 * core, x, core) if x % 2 == 0 else (y + 1 - 2 * core, z, x, core)
)
RING_Y = pairs(lambda y, z, x, core: (y + 1 - 2 * core, z, x, core))
RING_Z = pairs(lambda y, z, x, core: (y, z + 1 - 2 * core, x, core))
RING_X = pairs(lambda y, z, x, core: (y, z, x + 1 - 2 * core, core))
CORES = pairs(lambda y, z, x, core: (y, z, x, 1 - core))
X_LO = pairs(lambda y, z, x, core: (y, z, x ^ 1, core))
X_HI = pairs(lambda y, z, x, core: (y, z, x ^ 2, core))


def send(value, route):
    return lax.optimization_barrier(lax.ppermute(lax.optimization_barrier(value), AXES, route))


def nothing(*refs):
    pass


def after(value, *others):
    anywhere = pl.BlockSpec(memory_space=pl.ANY)
    return pl.pallas_call(
        nothing,
        out_shape=jax.ShapeDtypeStruct(value.shape, value.dtype),
        in_specs=[anywhere] * (1 + len(others)),
        out_specs=anywhere,
        input_output_aliases={0: 0},
        cost_estimate=pl.CostEstimate(flops=0, bytes_accessed=0, transcendentals=0),
        compiler_params=pltpu.CompilerParams(vmem_limit_bytes=1 << 20),
    )(value, *others)


def together(*values):
    anywhere = pl.BlockSpec(memory_space=pl.ANY)
    return pl.pallas_call(
        nothing,
        out_shape=[jax.ShapeDtypeStruct(value.shape, value.dtype) for value in values],
        in_specs=[anywhere] * len(values),
        out_specs=[anywhere] * len(values),
        input_output_aliases={k: k for k in range(len(values))},
        cost_estimate=pl.CostEstimate(flops=0, bytes_accessed=0, transcendentals=0),
        compiler_params=pltpu.CompilerParams(vmem_limit_bytes=1 << 20),
    )(*values)


def later(index, *others):
    return after(jnp.reshape(index, (1,)), *others)[0]


def gelu_parts(pre_act):
    slope_k = math.sqrt(2.0 / math.pi)
    cubed = pre_act * pre_act * pre_act
    tanh_val = jnp.tanh(slope_k * (pre_act + 0.044715 * cubed))
    gelu_value = 0.5 * pre_act * (1.0 + tanh_val)
    gelu_slope = 0.5 * (1.0 + tanh_val) + 0.5 * pre_act * (1.0 - tanh_val * tanh_val) * slope_k * (
        1.0 + 3.0 * 0.044715 * pre_act * pre_act
    )
    return (gelu_value, gelu_slope)


def cross_rows(left, right):
    return lax.dot_general(
        left, right, (((0,), (0,)), ((), ())), preferred_element_type=jnp.float32
    )


def by_block(rows, width):
    half = rows.shape[0] // 2
    return [
        lax.dot_general(part, part, (((1,), (1,)), ((), ())), preferred_element_type=jnp.float32)
        for part in (rows[:half], rows[half:])
    ]


def block_kernel(near, *refs):
    if near:
        tokens, masked, gate_w, up_w, down_w, hidden, d_gate, d_up, norms = refs[:9]
        tokens_v, masked_v, gate_v, up_v, down_v, pair_gram, hidden_gram, sems = refs[9:]
    else:
        tokens, masked, gate_w, up_w, down_w, hidden, d_gate, d_up = refs[:8]
        tokens_v, masked_v, gate_v, up_v, down_v, sems = refs[8:]
    units = gate_w.shape[1]
    tile = 256
    full, tail = units // tile, units % tile
    spans = [(k * tile, tile) for k in range(full)] + ([(full * tile, tail)] if tail else [])

    def copies(k, start, size):
        cols = pl.ds(start, size)
        return (
            pltpu.make_async_copy(gate_w.at[:, cols], gate_v.at[:, cols], sems.at[0, k]),
            pltpu.make_async_copy(up_w.at[:, cols], up_v.at[:, cols], sems.at[1, k]),
            pltpu.make_async_copy(down_w.at[cols, :], down_v.at[cols, :], sems.at[2, k]),
        )

    rows_in = (
        pltpu.make_async_copy(tokens, tokens_v, sems.at[0, len(spans)]),
        pltpu.make_async_copy(masked, masked_v, sems.at[1, len(spans)]),
    )
    for copy in rows_in:
        copy.start()
    for k, (start, size) in enumerate(spans):
        for copy in copies(k, start, size):
            copy.start()
    for copy in rows_in:
        copy.wait()
    if near:
        pair_gram[...] = jnp.zeros_like(pair_gram)
        hidden_gram[...] = jnp.zeros_like(hidden_gram)

    def work(k, start, size):
        for copy in copies(k, start, size):
            copy.wait()
        cols = pl.ds(start, size)
        gate_pre = jnp.dot(tokens_v[...], gate_v[:, cols], preferred_element_type=jnp.float32)
        up_pre = jnp.dot(tokens_v[...], up_v[:, cols], preferred_element_type=jnp.float32)
        d_hidden = lax.dot_general(
            masked_v[...], down_v[cols, :], (((1,), (1,)), ((), ())), preferred_element_type=jnp.float32
        )
        gelu_value, gelu_slope = gelu_parts(gate_pre)
        gate_rows = (d_hidden * up_pre * gelu_slope).astype(jnp.bfloat16)
        up_rows = (d_hidden * gelu_value).astype(jnp.bfloat16)
        hidden_rows = (gelu_value * up_pre).astype(jnp.bfloat16)
        hidden[:, cols], d_gate[:, cols], d_up[:, cols] = hidden_rows, gate_rows, up_rows
        if near:
            for k, (gate_gram, up_gram, own_gram) in enumerate(
                zip(by_block(gate_rows, size), by_block(up_rows, size), by_block(hidden_rows, size))
            ):
                pair_gram[k] += gate_gram + up_gram
                hidden_gram[k] += own_gram

    if full:
        lax.fori_loop(0, full, lambda k, _: (work(k, pl.multiple_of(k * tile, tile), tile), 0)[1], 0)
    if tail:
        work(full, full * tile, tail)
    if near:
        half = tokens_v.shape[0] // 2
        row_seq = lax.broadcasted_iota(jnp.int32, (half, half), 0) // LEN
        col_seq = lax.broadcasted_iota(jnp.int32, (half, half), 1) // LEN
        token_grams, masked_grams = by_block(tokens_v[...], 0), by_block(masked_v[...], 0)
        for k in range(2):
            total = token_grams[k] * pair_gram[k] + masked_grams[k] * hidden_gram[k]
            for seq in range(half // LEN):
                own = jnp.where((row_seq == seq) & (col_seq == seq), total, 0.0)
                lanes = jnp.sum(own, axis=0, keepdims=True)
                at = k * (half // LEN) + seq
                norms[at : at + 1, :] = jnp.broadcast_to(
                    jnp.sum(lanes, axis=1, keepdims=True), (1, norms.shape[1])
                )


def block(tokens, masked, gate_weight, up_weight, down_weight):
    near = True
    rows, units = tokens.shape[0], gate_weight.shape[1]
    count = units // 256 + (1 if units % 256 else 0)
    anywhere, here = pl.BlockSpec(memory_space=pl.ANY), pl.BlockSpec(memory_space=pltpu.VMEM)
    hidden = jax.ShapeDtypeStruct((rows, units), jnp.bfloat16)
    grams = [pltpu.VMEM((2, rows // 2, rows // 2), jnp.float32)] * 2
    args = (tokens, masked, gate_weight, up_weight, down_weight)
    return pl.pallas_call(
        functools.partial(block_kernel, near),
        out_shape=[hidden] * 3 + [jax.ShapeDtypeStruct((rows // LEN, 128), jnp.float32)] if near else [hidden] * 3,
        in_specs=[anywhere] * 5,
        out_specs=[here] * (4 if near else 3),
        scratch_shapes=[pltpu.VMEM(array.shape, array.dtype) for array in args]
        + (grams if near else [])
        + [pltpu.SemaphoreType.DMA((3, count + 1))],
        compiler_params=pltpu.CompilerParams(vmem_limit_bytes=44 << 20),
        cost_estimate=pl.CostEstimate(flops=0, bytes_accessed=0, transcendentals=0),
    )(*args)


def far_gate_kernel(tokens, gate_w, up_w, value, slope_up, hidden, tokens_v, gate_v, up_v, sems):
    units = gate_w.shape[1]
    spans = [(at, min(256, units - at)) for at in range(0, units, 256)]
    rows_in = pltpu.make_async_copy(tokens, tokens_v, sems.at[0, len(spans)])
    rows_in.start()
    weights_in = []
    for k, (start, size) in enumerate(spans):
        cols = pl.ds(start, size)
        weights_in.append(
            (
                pltpu.make_async_copy(gate_w.at[:, cols], gate_v.at[:, cols], sems.at[0, k]),
                pltpu.make_async_copy(up_w.at[:, cols], up_v.at[:, cols], sems.at[1, k]),
            )
        )
        for copy in weights_in[-1]:
            copy.start()
    rows_in.wait()
    for (start, size), both in zip(spans, weights_in):
        for copy in both:
            copy.wait()
        cols = pl.ds(start, size)
        gate_pre = jnp.dot(tokens_v[...], gate_v[:, cols], preferred_element_type=jnp.float32)
        up_pre = jnp.dot(tokens_v[...], up_v[:, cols], preferred_element_type=jnp.float32)
        gelu_value, gelu_slope = gelu_parts(gate_pre)
        value[:, cols] = gelu_value
        slope_up[:, cols] = up_pre * gelu_slope
        hidden[:, cols] = (gelu_value * up_pre).astype(jnp.bfloat16)


def far_gate_part(tokens, gate_weight, up_weight):
    rows, units = tokens.shape[0], gate_weight.shape[1]
    anywhere, here = pl.BlockSpec(memory_space=pl.ANY), pl.BlockSpec(memory_space=pltpu.VMEM)
    shape = (rows, units)
    args = (tokens, gate_weight, up_weight)
    return pl.pallas_call(
        far_gate_kernel,
        out_shape=[
            jax.ShapeDtypeStruct(shape, jnp.float32),
            jax.ShapeDtypeStruct(shape, jnp.float32),
            jax.ShapeDtypeStruct(shape, jnp.bfloat16),
        ],
        in_specs=[anywhere] * 3,
        out_specs=[here] * 3,
        scratch_shapes=[pltpu.VMEM(array.shape, array.dtype) for array in args]
        + [pltpu.SemaphoreType.DMA((2, (units + 255) // 256 + 1))],
        compiler_params=pltpu.CompilerParams(vmem_limit_bytes=40 << 20),
        cost_estimate=pl.CostEstimate(flops=4 * rows * tokens.shape[1] * units, bytes_accessed=18 << 20, transcendentals=0),
    )(*args)


def far_down_kernel(masked, down_w, value, slope_up, d_gate, d_up):
    d_hidden = lax.dot_general(
        masked[...], down_w[...], (((1,), (1,)), ((), ())), preferred_element_type=jnp.float32
    )
    d_gate[...] = (d_hidden * slope_up[...]).astype(jnp.bfloat16)
    d_up[...] = (d_hidden * value[...]).astype(jnp.bfloat16)


def far_down_part(masked, down_weight, value, slope_up):
    rows, units = value.shape
    tile = 384 if units % 384 == 0 else 128
    block_of = pl.BlockSpec((rows, tile), lambda k: (0, k))
    shape = jax.ShapeDtypeStruct((rows, units), jnp.bfloat16)
    return pl.pallas_call(
        far_down_kernel,
        grid=(units // tile,),
        out_shape=[shape, shape],
        in_specs=[
            pl.BlockSpec(masked.shape, lambda k: (0, 0)),
            pl.BlockSpec((tile, masked.shape[1]), lambda k: (k, 0)),
            block_of,
            block_of,
        ],
        out_specs=[block_of, block_of],
        compiler_params=pltpu.CompilerParams(vmem_limit_bytes=28 << 20),
        cost_estimate=pl.CostEstimate(flops=2 * rows * masked.shape[1] * units, bytes_accessed=14 << 20, transcendentals=0),
    )(masked, down_weight, value, slope_up)


def input_kernel(gate_w, up_w, d_gate, d_up, last, out):
    total = lax.dot_general(gate_w[...], d_gate[...], (((1,), (1,)), ((), ())), preferred_element_type=jnp.float32)
    total += lax.dot_general(up_w[...], d_up[...], (((1,), (1,)), ((), ())), preferred_element_type=jnp.float32)
    out[0] = total


def input_part(gate_weight, up_weight, d_gate, d_up, last):
    width, units = gate_weight.shape
    rows = d_gate.shape[0]
    whole = pl.BlockSpec((rows, units), lambda k: (0, 0))
    part = pl.BlockSpec((width // 4, units), lambda k: (k, 0))
    return pl.pallas_call(
        input_kernel,
        grid=(4,),
        out_shape=jax.ShapeDtypeStruct((4, width // 4, rows), jnp.float32),
        in_specs=[part, part, whole, whole, pl.BlockSpec(memory_space=pl.ANY)],
        out_specs=pl.BlockSpec((1, width // 4, rows), lambda k: (k, 0, 0)),
        compiler_params=pltpu.CompilerParams(vmem_limit_bytes=32 << 20),
        cost_estimate=pl.CostEstimate(flops=0, bytes_accessed=0, transcendentals=0),
    )(gate_weight, up_weight, d_gate, d_up, last)


class Ring:
    def __init__(self, take, here, way, route):
        self.take, self.here, self.way, self.route = take, here, way, route
        self.hops = 3
        self.part = take((here + 3 * way) % 4)

    def step(self, *others):
        self.hops -= 1
        part = send(self.part, self.route) + self.take((self.here + self.hops * self.way) % 4)
        self.part = after(part, *others) if others else part


def product_kernel(
    near_t, far_t, near_c, far_c, d_gate, far_gate, d_up, far_up, hidden, far_hidden, near_w, far_w, near_a, far_a,
    out, near_v, far_v,
):
    which, tile = pl.program_id(0), pl.program_id(1)
    for index, near, far in ((0, d_gate, far_gate), (1, d_up, far_up)):

        @pl.when((which == index) & (tile == 0))
        def _(near=near, far=far):
            near_v[...] = (near[...].astype(jnp.float32) * near_w[...]).astype(jnp.bfloat16)
            far_v[...] = (far[...].astype(jnp.float32) * far_w[...]).astype(jnp.bfloat16)

    @pl.when(which < 2)
    def _():
        total = jnp.dot(near_t[...], near_v[...], preferred_element_type=jnp.float32)
        out[...] = total + jnp.dot(far_t[...], far_v[...], preferred_element_type=jnp.float32)

    @pl.when(which == 2)
    def _():
        near = (near_c[...].astype(jnp.float32) * near_a[...]).astype(jnp.bfloat16)
        far = (far_c[...].astype(jnp.float32) * far_a[...]).astype(jnp.bfloat16)
        total = jnp.dot(near, hidden[...], preferred_element_type=jnp.float32)
        out[...] = total + jnp.dot(far, far_hidden[...], preferred_element_type=jnp.float32)


def products(*args):
    count, rows = args[0].shape
    units = args[4].shape[1]
    left = pl.BlockSpec((count // 4, rows), lambda which, tile: (tile, 0))
    right = pl.BlockSpec((rows, units), lambda which, tile: (0, 0))
    column = pl.BlockSpec((rows, 1), lambda which, tile: (0, 0))
    across = pl.BlockSpec((1, rows), lambda which, tile: (0, 0))
    scaled = pltpu.VMEM((rows, units), jnp.bfloat16)
    return pl.pallas_call(
        product_kernel,
        grid=(3, 4),
        out_shape=jax.ShapeDtypeStruct((count, 3 * units), jnp.float32),
        in_specs=[left] * 4 + [right] * 6 + [column] * 2 + [across] * 2,
        out_specs=pl.BlockSpec((count // 4, units), lambda which, tile: (tile, which)),
        scratch_shapes=[scaled, scaled],
        compiler_params=pltpu.CompilerParams(vmem_limit_bytes=36 << 20),
        cost_estimate=pl.CostEstimate(flops=12 * rows * count * units, bytes_accessed=28 << 20, transcendentals=0),
    )(*args)


def per_device(tokens, cotangent, lengths, gate_weight, up_weight, down_weight):
    seq_count = lengths.shape[0]
    row_count, width = tokens.shape
    total_seqs = seq_count * lax.axis_size("dp")
    clip_bound = 0.5 * math.sqrt(D * FFW * LEN)
    dp, tensor = lax.axis_index("dp"), lax.axis_index("tensor")
    y, z, x_lo = dp // 8, (dp // 2) % 4, dp % 2
    x_hi, core = tensor // 2, tensor % 2
    way = 1 - 2 * core
    half = row_count // 2
    strip = width // 32

    positions = jnp.arange(LEN, dtype=jnp.int32)
    live = (positions[None, :] < lengths[:, None]).reshape(row_count)[:, None]
    masked = cotangent * live.astype(jnp.bfloat16)

    def own_half(rows, start):
        return lax.dynamic_slice_in_dim(rows, start, half, 0).astype(jnp.float32)

    lanes = jnp.broadcast_to(live.astype(jnp.bfloat16), (row_count, 128))
    token_half = send(jnp.concatenate([own_half(tokens, core * half), own_half(lanes, core * half)], axis=1), RING_X)

    hidden_act, d_gate, d_up, norms = block(tokens, masked, gate_weight, up_weight, down_weight)

    def joined(mine, theirs, mask_mine, mask_theirs):
        return jnp.concatenate(
            [(mine * mask_mine).astype(jnp.bfloat16), (theirs * mask_theirs).astype(jnp.bfloat16)], axis=0
        )

    partial_value = input_part(gate_weight, up_weight, d_gate, d_up, norms)
    token_half = after(token_half, norms, partial_value)
    token_rest = send(token_half, CORES)
    norm_sq = lax.psum(after(norms[:, 0], token_half), "tensor")
    clip_ratio = jnp.sqrt(norm_sq) / clip_bound
    clip_factor = 1.0 / jnp.maximum(1.0, clip_ratio)
    cot_half = send(after(own_half(cotangent, core * half), clip_factor, token_rest), RING_X)

    column_at = jnp.arange(width // 2, dtype=jnp.int32)
    source = (column_at // strip) * (2 * strip) + later(x_lo, clip_factor, token_rest) * strip + column_at % strip
    pick = (jnp.arange(width, dtype=jnp.int32)[:, None] == source[None, :]).astype(jnp.bfloat16)

    def picked(rows):
        return lax.dot_general(
            pick, rows, (((0,), (1,)), ((), ())), preferred_element_type=jnp.float32
        ).astype(jnp.bfloat16)

    near_tokens, near_cot = picked(tokens), picked(masked)
    masks = token_half[:, width : width + 1], token_rest[:, width : width + 1]
    far_tokens = joined(token_half[:, :width], token_rest[:, :width], *masks)
    value, slope_up, far_hidden = far_gate_part(far_tokens, gate_weight, up_weight)
    far_cols = picked(far_tokens)
    cot_half = after(cot_half, far_cols, far_hidden, near_tokens, near_cot)
    far_masked = joined(cot_half, send(cot_half, CORES), *masks)
    far_gate, far_up = far_down_part(far_masked, down_weight, value, slope_up)
    far_cot = picked(far_masked)

    def row_weight(by_seq, shift, axis):
        row_seq = (jnp.arange(row_count, dtype=jnp.int32) // LEN + shift) % seq_count
        seqs = jnp.arange(seq_count, dtype=jnp.int32)
        spread = jnp.expand_dims(row_seq, axis) == jnp.expand_dims(seqs, 1 - axis)
        return jnp.sum(jnp.where(spread, jnp.expand_dims(by_seq, 1 - axis), 0.0), axis=axis, keepdims=True)

    near_mean = clip_factor / total_seqs
    far_mean = send(after(clip_factor / total_seqs, cot_half), X_LO)
    shift = core * (seq_count // 2)
    near_weight, far_weight = row_weight(near_mean, 0, 1), row_weight(far_mean, shift, 1)
    near_across, far_across = row_weight(near_mean, 0, 0), row_weight(far_mean, shift, 0)

    grads = products(
        near_tokens, far_cols, near_cot, far_cot, d_gate, far_gate, d_up, far_up, hidden_act, far_hidden,
        near_weight, far_weight, near_across, far_across,
    )
    units = d_gate.shape[1]
    grads = grads.reshape(4, 4, strip, 3 * units)

    def by_y(lo, hi):
        return lambda k: lax.dynamic_slice(grads, (k, 0, 0, lo), (1, 4, strip, hi - lo)).reshape(4, strip, hi - lo)

    def by_z(lo, hi):
        return lambda k: lax.dynamic_slice(grads, (0, k, 0, lo), (4, 1, strip, hi - lo)).reshape(4, strip, hi - lo)

    def line(rows):
        return lambda k: lax.dynamic_index_in_dim(rows, k, 0, keepdims=False)

    tiles = 3 * units // 128
    ends = [0] + [(tiles * share // 27) * 128 for share in (7, 16, 22)] + [3 * units]
    flows = []
    for k in range(4):
        if k % 2 == 0:
            flows.append((by_y(ends[k], ends[k + 1]), y, RING_Y, z, RING_Z))
        else:
            flows.append((by_z(ends[k], ends[k + 1]), z, RING_Z, y, RING_Y))
    rings = [Ring(take, here, way, route) for take, here, route, _, _ in flows]

    partial_value = partial_value.reshape(2, 2, width // 4, row_count)
    part = send(lax.dynamic_index_in_dim(partial_value, 1 - core, 1, keepdims=False), CORES)
    part = part + lax.dynamic_index_in_dim(partial_value, core, 1, keepdims=False)
    across = after(lax.dynamic_index_in_dim(part, 1 - x_hi, 0, keepdims=False), far_gate)
    summed_input = send(across, X_HI)
    summed_input = summed_input + lax.dynamic_index_in_dim(part, x_hi, 0, keepdims=False)
    for _ in range(3):
        for ring in rings:
            ring.step()
    rows = together(*[ring.part for ring in rings])
    rings = [Ring(line(row), here, way, route) for row, (_, _, _, here, route) in zip(rows, flows)]
    for _ in range(3):
        for ring in rings:
            ring.step()
    clip_late = after(clip_factor, *[ring.part for ring in rings])
    input_grad = (summed_input * row_weight(clip_late, 0, 0)).T.astype(jnp.bfloat16)
    sums = jnp.concatenate([ring.part for ring in rings], axis=1)
    grad_gate, grad_up = sums[:, :units], sums[:, units : 2 * units]
    grad_down = sums[:, 2 * units :].T
    return (input_grad, clip_ratio, grad_gate, grad_up, grad_down)


def solution(mesh):
    placed = (
        P("dp", None),
        P("dp", None),
        P("dp"),
        P(None, "tensor"),
        P(None, "tensor"),
        P("tensor", None),
    )
    return jax.shard_map(
        per_device,
        mesh=mesh,
        in_specs=placed,
        out_specs=(
            P("dp", "tensor"),
            P("dp"),
            P("dp", "tensor"),
            P("dp", "tensor"),
            P("tensor", "dp"),
        ),
        check_vma=False,
    )
```

```python
import functools
import math

import jax
import jax.numpy as jnp
from jax import lax
from jax.experimental import pallas as pl
from jax.experimental.pallas import tpu as pltpu
from jax.sharding import PartitionSpec as P

D = 2304
FFW = 4608
LEN = 64
AXES = ("dp", "tensor")


def place(y, z, x, core):
    y, z, x = y % 4, z % 4, x % 4
    return ((y * 4 + z) * 2 + x % 2) * 4 + (x // 2) * 2 + core


def pairs(target):
    return [
        (place(y, z, x, core), place(*target(y, z, x, core)))
        for y in range(4)
        for z in range(4)
        for x in range(4)
        for core in range(2)
    ]


RING_YZ = pairs(
    lambda y, z, x, core: (y, z + 1 - 2 * core, x, core) if x % 2 == 0 else (y + 1 - 2 * core, z, x, core)
)
RING_Y = pairs(lambda y, z, x, core: (y + 1 - 2 * core, z, x, core))
RING_Z = pairs(lambda y, z, x, core: (y, z + 1 - 2 * core, x, core))
RING_X = pairs(lambda y, z, x, core: (y, z, x + 1 - 2 * core, core))
CORES = pairs(lambda y, z, x, core: (y, z, x, 1 - core))
X_LO = pairs(lambda y, z, x, core: (y, z, x ^ 1, core))
X_HI = pairs(lambda y, z, x, core: (y, z, x ^ 2, core))


def send(value, route):
    return lax.optimization_barrier(lax.ppermute(lax.optimization_barrier(value), AXES, route))


def nothing(*refs):
    pass


def after(value, *others):
    anywhere = pl.BlockSpec(memory_space=pl.ANY)
    return pl.pallas_call(
        nothing,
        out_shape=jax.ShapeDtypeStruct(value.shape, value.dtype),
        in_specs=[anywhere] * (1 + len(others)),
        out_specs=anywhere,
        input_output_aliases={0: 0},
        cost_estimate=pl.CostEstimate(flops=0, bytes_accessed=0, transcendentals=0),
        compiler_params=pltpu.CompilerParams(vmem_limit_bytes=1 << 20),
    )(value, *others)


def together(*values):
    anywhere = pl.BlockSpec(memory_space=pl.ANY)
    return pl.pallas_call(
        nothing,
        out_shape=[jax.ShapeDtypeStruct(value.shape, value.dtype) for value in values],
        in_specs=[anywhere] * len(values),
        out_specs=[anywhere] * len(values),
        input_output_aliases={k: k for k in range(len(values))},
        cost_estimate=pl.CostEstimate(flops=0, bytes_accessed=0, transcendentals=0),
        compiler_params=pltpu.CompilerParams(vmem_limit_bytes=1 << 20),
    )(*values)


def later(index, *others):
    return after(jnp.reshape(index, (1,)), *others)[0]


def gelu_parts(pre_act):
    slope_k = math.sqrt(2.0 / math.pi)
    cubed = pre_act * pre_act * pre_act
    tanh_val = jnp.tanh(slope_k * (pre_act + 0.044715 * cubed))
    gelu_value = 0.5 * pre_act * (1.0 + tanh_val)
    gelu_slope = 0.5 * (1.0 + tanh_val) + 0.5 * pre_act * (1.0 - tanh_val * tanh_val) * slope_k * (
        1.0 + 3.0 * 0.044715 * pre_act * pre_act
    )
    return (gelu_value, gelu_slope)


def cross_rows(left, right):
    return lax.dot_general(
        left, right, (((0,), (0,)), ((), ())), preferred_element_type=jnp.float32
    )


def by_block(rows, width):
    half = rows.shape[0] // 2
    return [
        lax.dot_general(part, part, (((1,), (1,)), ((), ())), preferred_element_type=jnp.float32)
        for part in (rows[:half], rows[half:])
    ]


def block_kernel(near, *refs):
    if near:
        tokens, masked, gate_w, up_w, down_w, hidden, d_gate, d_up, norms = refs[:9]
        tokens_v, masked_v, gate_v, up_v, down_v, pair_gram, hidden_gram, sems = refs[9:]
    else:
        tokens, masked, gate_w, up_w, down_w, hidden, d_gate, d_up = refs[:8]
        tokens_v, masked_v, gate_v, up_v, down_v, sems = refs[8:]
    units = gate_w.shape[1]
    tile = 256
    full, tail = units // tile, units % tile
    spans = [(k * tile, tile) for k in range(full)] + ([(full * tile, tail)] if tail else [])

    def copies(k, start, size):
        cols = pl.ds(start, size)
        return (
            pltpu.make_async_copy(gate_w.at[:, cols], gate_v.at[:, cols], sems.at[0, k]),
            pltpu.make_async_copy(up_w.at[:, cols], up_v.at[:, cols], sems.at[1, k]),
            pltpu.make_async_copy(down_w.at[cols, :], down_v.at[cols, :], sems.at[2, k]),
        )

    rows_in = (
        pltpu.make_async_copy(tokens, tokens_v, sems.at[0, len(spans)]),
        pltpu.make_async_copy(masked, masked_v, sems.at[1, len(spans)]),
    )
    for copy in rows_in:
        copy.start()
    for k, (start, size) in enumerate(spans):
        for copy in copies(k, start, size):
            copy.start()
    for copy in rows_in:
        copy.wait()
    if near:
        pair_gram[...] = jnp.zeros_like(pair_gram)
        hidden_gram[...] = jnp.zeros_like(hidden_gram)

    def work(k, start, size):
        for copy in copies(k, start, size):
            copy.wait()
        cols = pl.ds(start, size)
        gate_pre = jnp.dot(tokens_v[...], gate_v[:, cols], preferred_element_type=jnp.float32)
        up_pre = jnp.dot(tokens_v[...], up_v[:, cols], preferred_element_type=jnp.float32)
        d_hidden = lax.dot_general(
            masked_v[...], down_v[cols, :], (((1,), (1,)), ((), ())), preferred_element_type=jnp.float32
        )
        gelu_value, gelu_slope = gelu_parts(gate_pre)
        gate_rows = (d_hidden * up_pre * gelu_slope).astype(jnp.bfloat16)
        up_rows = (d_hidden * gelu_value).astype(jnp.bfloat16)
        hidden_rows = (gelu_value * up_pre).astype(jnp.bfloat16)
        hidden[:, cols], d_gate[:, cols], d_up[:, cols] = hidden_rows, gate_rows, up_rows
        if near:
            for k, (gate_gram, up_gram, own_gram) in enumerate(
                zip(by_block(gate_rows, size), by_block(up_rows, size), by_block(hidden_rows, size))
            ):
                pair_gram[k] += gate_gram + up_gram
                hidden_gram[k] += own_gram

    if full:
        lax.fori_loop(0, full, lambda k, _: (work(k, pl.multiple_of(k * tile, tile), tile), 0)[1], 0)
    if tail:
        work(full, full * tile, tail)
    if near:
        half = tokens_v.shape[0] // 2
        row_seq = lax.broadcasted_iota(jnp.int32, (half, half), 0) // LEN
        col_seq = lax.broadcasted_iota(jnp.int32, (half, half), 1) // LEN
        token_grams, masked_grams = by_block(tokens_v[...], 0), by_block(masked_v[...], 0)
        for k in range(2):
            total = token_grams[k] * pair_gram[k] + masked_grams[k] * hidden_gram[k]
            for seq in range(half // LEN):
                own = jnp.where((row_seq == seq) & (col_seq == seq), total, 0.0)
                lanes = jnp.sum(own, axis=0, keepdims=True)
                at = k * (half // LEN) + seq
                norms[at : at + 1, :] = jnp.broadcast_to(
                    jnp.sum(lanes, axis=1, keepdims=True), (1, norms.shape[1])
                )


def block(near, tokens, masked, gate_weight, up_weight, down_weight):
    rows, units = tokens.shape[0], gate_weight.shape[1]
    count = units // 256 + (1 if units % 256 else 0)
    anywhere, here = pl.BlockSpec(memory_space=pl.ANY), pl.BlockSpec(memory_space=pltpu.VMEM)
    hidden = jax.ShapeDtypeStruct((rows, units), jnp.bfloat16)
    grams = [pltpu.VMEM((2, rows // 2, rows // 2), jnp.float32)] * 2
    args = (tokens, masked, gate_weight, up_weight, down_weight)
    return pl.pallas_call(
        functools.partial(block_kernel, near),
        out_shape=[hidden] * 3 + [jax.ShapeDtypeStruct((rows // LEN, 128), jnp.float32)] if near else [hidden] * 3,
        in_specs=[anywhere] * 5,
        out_specs=[here] * (4 if near else 3),
        scratch_shapes=[pltpu.VMEM(array.shape, array.dtype) for array in args]
        + (grams if near else [])
        + [pltpu.SemaphoreType.DMA((3, count + 1))],
        compiler_params=pltpu.CompilerParams(vmem_limit_bytes=44 << 20),
        cost_estimate=pl.CostEstimate(flops=0, bytes_accessed=0, transcendentals=0),
    )(*args)


def input_kernel(gate_w, up_w, d_gate, d_up, last, out):
    total = lax.dot_general(gate_w[...], d_gate[...], (((1,), (1,)), ((), ())), preferred_element_type=jnp.float32)
    total += lax.dot_general(up_w[...], d_up[...], (((1,), (1,)), ((), ())), preferred_element_type=jnp.float32)
    out[0] = total


def input_part(gate_weight, up_weight, d_gate, d_up, last):
    width, units = gate_weight.shape
    rows = d_gate.shape[0]
    whole = pl.BlockSpec((rows, units), lambda k: (0, 0))
    part = pl.BlockSpec((width // 4, units), lambda k: (k, 0))
    return pl.pallas_call(
        input_kernel,
        grid=(4,),
        out_shape=jax.ShapeDtypeStruct((4, width // 4, rows), jnp.float32),
        in_specs=[part, part, whole, whole, pl.BlockSpec(memory_space=pl.ANY)],
        out_specs=pl.BlockSpec((1, width // 4, rows), lambda k: (k, 0, 0)),
        compiler_params=pltpu.CompilerParams(vmem_limit_bytes=32 << 20),
        cost_estimate=pl.CostEstimate(flops=0, bytes_accessed=0, transcendentals=0),
    )(gate_weight, up_weight, d_gate, d_up, last)


class Ring:
    def __init__(self, take, here, way, route):
        self.take, self.here, self.way, self.route = take, here, way, route
        self.hops = 3
        self.part = take((here + 3 * way) % 4)

    def step(self, *others):
        self.hops -= 1
        part = send(self.part, self.route) + self.take((self.here + self.hops * self.way) % 4)
        self.part = after(part, *others) if others else part


def flow_widths(units):
    tiles = 3 * units // 128
    return [(tiles + 3 - k) // 4 * 128 for k in range(4)]


def product_kernel(
    near_t, far_t, near_c, far_c, d_gate, far_gate, d_up, far_up, hidden, far_hidden, near_w, far_w, near_a, far_a,
    *refs,
):
    outs, scaled = refs[:4], refs[4:]

    @pl.when(pl.program_id(0) == 0)
    def _():
        for rows, weight, into in zip((d_gate, far_gate, d_up, far_up), (near_w, far_w) * 2, scaled):
            into[...] = (rows[...].astype(jnp.float32) * weight[...]).astype(jnp.bfloat16)

    near_cot = (near_c[...].astype(jnp.float32) * near_a[...]).astype(jnp.bfloat16)
    far_cot = (far_c[...].astype(jnp.float32) * far_a[...]).astype(jnp.bfloat16)
    units = hidden.shape[1]
    parts = []
    for lefts, rights in (
        ((near_t[...], far_t[...]), scaled[:2]),
        ((near_t[...], far_t[...]), scaled[2:]),
        ((near_cot, far_cot), (hidden, far_hidden)),
    ):
        total = jnp.dot(lefts[0], rights[0][...], preferred_element_type=jnp.float32)
        parts.append(total + jnp.dot(lefts[1], rights[1][...], preferred_element_type=jnp.float32))
    start = 0
    for out in outs:
        width = out.shape[1]
        for k, part in enumerate(parts):
            low, high = max(start, k * units), min(start + width, (k + 1) * units)
            if low < high:
                out[:, low - start : high - start] = part[:, low - k * units : high - k * units]
        start += width


def products(*args):
    count, rows = args[0].shape
    units = args[4].shape[1]
    left = pl.BlockSpec((count // 4, rows), lambda tile: (tile, 0))
    right = pl.BlockSpec((rows, units), lambda tile: (0, 0))
    column = pl.BlockSpec((rows, 1), lambda tile: (0, 0))
    across = pl.BlockSpec((1, rows), lambda tile: (0, 0))
    widths = flow_widths(units)
    return pl.pallas_call(
        product_kernel,
        grid=(4,),
        out_shape=[jax.ShapeDtypeStruct((count, width), jnp.float32) for width in widths],
        in_specs=[left] * 4 + [right] * 6 + [column] * 2 + [across] * 2,
        out_specs=[pl.BlockSpec((count // 4, width), lambda tile: (tile, 0)) for width in widths],
        scratch_shapes=[pltpu.VMEM((rows, units), jnp.bfloat16)] * 4,
        compiler_params=pltpu.CompilerParams(vmem_limit_bytes=44 << 20),
        cost_estimate=pl.CostEstimate(flops=12 * rows * count * units, bytes_accessed=28 << 20, transcendentals=0),
    )(*args)


def per_device(tokens, cotangent, lengths, gate_weight, up_weight, down_weight):
    seq_count = lengths.shape[0]
    row_count, width = tokens.shape
    total_seqs = seq_count * lax.axis_size("dp")
    clip_bound = 0.5 * math.sqrt(D * FFW * LEN)
    dp, tensor = lax.axis_index("dp"), lax.axis_index("tensor")
    y, z, x_lo = dp // 8, (dp // 2) % 4, dp % 2
    x_hi, core = tensor // 2, tensor % 2
    way = 1 - 2 * core
    half = row_count // 2
    strip = width // 32

    positions = jnp.arange(LEN, dtype=jnp.int32)
    live = (positions[None, :] < lengths[:, None]).reshape(row_count)[:, None]
    masked = cotangent * live.astype(jnp.bfloat16)

    def own_half(rows, start):
        return lax.dynamic_slice_in_dim(rows, start, half, 0).astype(jnp.float32)

    lanes = jnp.broadcast_to(live.astype(jnp.bfloat16), (row_count, 128))
    token_half = send(jnp.concatenate([own_half(tokens, core * half), own_half(lanes, core * half)], axis=1), RING_X)

    cot_half = send(own_half(cotangent, core * half), RING_X)

    hidden_act, d_gate, d_up, norms = block(True, tokens, masked, gate_weight, up_weight, down_weight)
    partial_value = input_part(gate_weight, up_weight, d_gate, d_up, norms).reshape(2, 2, width // 4, row_count)

    column_at = jnp.arange(width // 2, dtype=jnp.int32)
    source = (column_at // strip) * (2 * strip) + later(x_lo, norms) * strip + column_at % strip
    pick = (jnp.arange(width, dtype=jnp.int32)[:, None] == source[None, :]).astype(jnp.bfloat16)

    def picked(rows):
        return lax.dot_general(
            pick, rows, (((0,), (1,)), ((), ())), preferred_element_type=jnp.float32
        ).astype(jnp.bfloat16)

    near_tokens, near_cot = picked(tokens), picked(masked)

    def joined(mine, theirs, mask_mine, mask_theirs):
        return jnp.concatenate(
            [(mine * mask_mine).astype(jnp.bfloat16), (theirs * mask_theirs).astype(jnp.bfloat16)], axis=0
        )

    token_half = after(token_half, near_tokens, near_cot, partial_value)
    cot_half = after(cot_half, near_tokens, near_cot, partial_value)
    norm_sq = lax.psum(after(norms[:, 0], token_half, cot_half), "tensor")
    clip_ratio = jnp.sqrt(norm_sq) / clip_bound
    clip_factor = 1.0 / jnp.maximum(1.0, clip_ratio)
    token_rest, cot_rest = send(token_half, CORES), send(cot_half, CORES)
    masks = token_half[:, width : width + 1], token_rest[:, width : width + 1]
    far_tokens = joined(token_half[:, :width], token_rest[:, :width], *masks)
    far_masked = joined(cot_half, cot_rest, *masks)
    far_hidden, far_gate, far_up = block(False, far_tokens, far_masked, gate_weight, up_weight, down_weight)
    far_cols, far_cot = picked(far_tokens), picked(far_masked)

    def row_weight(by_seq, shift, axis):
        row_seq = (jnp.arange(row_count, dtype=jnp.int32) // LEN + shift) % seq_count
        seqs = jnp.arange(seq_count, dtype=jnp.int32)
        spread = jnp.expand_dims(row_seq, axis) == jnp.expand_dims(seqs, 1 - axis)
        return jnp.sum(jnp.where(spread, jnp.expand_dims(by_seq, 1 - axis), 0.0), axis=axis, keepdims=True)

    near_mean = clip_factor / total_seqs
    far_mean = send(after(clip_factor / total_seqs, cot_half), X_LO)
    shift = core * (seq_count // 2)
    near_weight, far_weight = row_weight(near_mean, 0, 1), row_weight(far_mean, shift, 1)
    near_across, far_across = row_weight(near_mean, 0, 0), row_weight(far_mean, shift, 0)

    grads = products(
        near_tokens, far_cols, near_cot, far_cot, d_gate, far_gate, d_up, far_up, hidden_act, far_hidden,
        near_weight, far_weight, near_across, far_across,
    )
    units = d_gate.shape[1]
    grads = [grad.reshape(4, 4, strip, grad.shape[1]) for grad in grads]

    def line(rows, axis=0):
        return lambda k: lax.dynamic_index_in_dim(rows, k, axis, keepdims=False)

    flows = [
        (line(grad, 0), y, RING_Y, z, RING_Z) if k % 2 == 0 else (line(grad, 1), z, RING_Z, y, RING_Y)
        for k, grad in enumerate(grads)
    ]
    rings = [Ring(take, here, way, route) for take, here, route, _, _ in flows]

    part = send(lax.dynamic_index_in_dim(partial_value, 1 - core, 1, keepdims=False), CORES)
    part = part + lax.dynamic_index_in_dim(partial_value, core, 1, keepdims=False)
    across = after(lax.dynamic_index_in_dim(part, 1 - x_hi, 0, keepdims=False), clip_factor)
    summed_input = send(across, X_HI)
    summed_input = summed_input + lax.dynamic_index_in_dim(part, x_hi, 0, keepdims=False)
    for _ in range(3):
        for ring in rings:
            ring.step()
    rows = together(*[ring.part for ring in rings])
    rings = [Ring(line(row), here, way, route) for row, (_, _, _, here, route) in zip(rows, flows)]
    for _ in range(3):
        for ring in rings:
            ring.step()
    clip_late = after(clip_factor, *[ring.part for ring in rings])
    input_grad = (summed_input * row_weight(clip_late, 0, 0)).T.astype(jnp.bfloat16)
    sums = jnp.concatenate([ring.part for ring in rings], axis=1)
    grad_gate, grad_up = sums[:, :units], sums[:, units : 2 * units]
    grad_down = sums[:, 2 * units :].T
    return (input_grad, clip_ratio, grad_gate, grad_up, grad_down)


def solution(mesh):
    placed = (
        P("dp", None),
        P("dp", None),
        P("dp"),
        P(None, "tensor"),
        P(None, "tensor"),
        P("tensor", None),
    )
    return jax.shard_map(
        per_device,
        mesh=mesh,
        in_specs=placed,
        out_specs=(
            P("dp", "tensor"),
            P("dp"),
            P("dp", "tensor"),
            P("dp", "tensor"),
            P("tensor", "dp"),
        ),
        check_vma=False,
    )
```

```python
import functools
import math

import jax
import jax.numpy as jnp
from jax import lax
from jax.experimental import pallas as pl
from jax.experimental.pallas import tpu as pltpu
from jax.sharding import PartitionSpec as P

D = 2304
FFW = 4608
LEN = 64
AXES = ("dp", "tensor")


def place(y, z, x, core):
    y, z, x = y % 4, z % 4, x % 4
    return ((y * 4 + z) * 2 + x % 2) * 4 + (x // 2) * 2 + core


def pairs(target):
    return [
        (place(y, z, x, core), place(*target(y, z, x, core)))
        for y in range(4)
        for z in range(4)
        for x in range(4)
        for core in range(2)
    ]


RING_YZ = pairs(
    lambda y, z, x, core: (y, z + 1 - 2 * core, x, core) if x % 2 == 0 else (y + 1 - 2 * core, z, x, core)
)
RING_Y = pairs(lambda y, z, x, core: (y + 1 - 2 * core, z, x, core))
RING_Z = pairs(lambda y, z, x, core: (y, z + 1 - 2 * core, x, core))
RING_X = pairs(lambda y, z, x, core: (y, z, x + 1 - 2 * core, core))
CORES = pairs(lambda y, z, x, core: (y, z, x, 1 - core))
X_LO = pairs(lambda y, z, x, core: (y, z, x ^ 1, core))
X_HI = pairs(lambda y, z, x, core: (y, z, x ^ 2, core))


def send(value, route):
    return lax.optimization_barrier(lax.ppermute(lax.optimization_barrier(value), AXES, route))


def nothing(*refs):
    pass


def after(value, *others):
    anywhere = pl.BlockSpec(memory_space=pl.ANY)
    return pl.pallas_call(
        nothing,
        out_shape=jax.ShapeDtypeStruct(value.shape, value.dtype),
        in_specs=[anywhere] * (1 + len(others)),
        out_specs=anywhere,
        input_output_aliases={0: 0},
        cost_estimate=pl.CostEstimate(flops=0, bytes_accessed=0, transcendentals=0),
        compiler_params=pltpu.CompilerParams(vmem_limit_bytes=1 << 20),
    )(value, *others)


def together(*values):
    anywhere = pl.BlockSpec(memory_space=pl.ANY)
    return pl.pallas_call(
        nothing,
        out_shape=[jax.ShapeDtypeStruct(value.shape, value.dtype) for value in values],
        in_specs=[anywhere] * len(values),
        out_specs=[anywhere] * len(values),
        input_output_aliases={k: k for k in range(len(values))},
        cost_estimate=pl.CostEstimate(flops=0, bytes_accessed=0, transcendentals=0),
        compiler_params=pltpu.CompilerParams(vmem_limit_bytes=1 << 20),
    )(*values)


def later(index, *others):
    return after(jnp.reshape(index, (1,)), *others)[0]


def gelu_parts(pre_act):
    slope_k = math.sqrt(2.0 / math.pi)
    cubed = pre_act * pre_act * pre_act
    tanh_val = jnp.tanh(slope_k * (pre_act + 0.044715 * cubed))
    gelu_value = 0.5 * pre_act * (1.0 + tanh_val)
    gelu_slope = 0.5 * (1.0 + tanh_val) + 0.5 * pre_act * (1.0 - tanh_val * tanh_val) * slope_k * (
        1.0 + 3.0 * 0.044715 * pre_act * pre_act
    )
    return (gelu_value, gelu_slope)


def cross_rows(left, right):
    return lax.dot_general(
        left, right, (((0,), (0,)), ((), ())), preferred_element_type=jnp.float32
    )


def by_block(rows, width):
    half = rows.shape[0] // 2
    return [
        lax.dot_general(part, part, (((1,), (1,)), ((), ())), preferred_element_type=jnp.float32)
        for part in (rows[:half], rows[half:])
    ]


def block_kernel(near, *refs):
    if near:
        tokens, masked, gate_w, up_w, down_w, hidden, d_gate, d_up, norms = refs[:9]
        tokens_v, masked_v, gate_v, up_v, down_v, pair_gram, hidden_gram, sems = refs[9:]
    else:
        tokens, masked, gate_w, up_w, down_w, hidden, d_gate, d_up = refs[:8]
        tokens_v, masked_v, gate_v, up_v, down_v, sems = refs[8:]
    units = gate_w.shape[1]
    tile = 256
    full, tail = units // tile, units % tile
    spans = [(k * tile, tile) for k in range(full)] + ([(full * tile, tail)] if tail else [])

    def copies(k, start, size):
        cols = pl.ds(start, size)
        return (
            pltpu.make_async_copy(gate_w.at[:, cols], gate_v.at[:, cols], sems.at[0, k]),
            pltpu.make_async_copy(up_w.at[:, cols], up_v.at[:, cols], sems.at[1, k]),
            pltpu.make_async_copy(down_w.at[cols, :], down_v.at[cols, :], sems.at[2, k]),
        )

    rows_in = (
        pltpu.make_async_copy(tokens, tokens_v, sems.at[0, len(spans)]),
        pltpu.make_async_copy(masked, masked_v, sems.at[1, len(spans)]),
    )
    for copy in rows_in:
        copy.start()
    for k, (start, size) in enumerate(spans):
        for copy in copies(k, start, size):
            copy.start()
    for copy in rows_in:
        copy.wait()
    if near:
        pair_gram[...] = jnp.zeros_like(pair_gram)
        hidden_gram[...] = jnp.zeros_like(hidden_gram)

    def work(k, start, size):
        for copy in copies(k, start, size):
            copy.wait()
        cols = pl.ds(start, size)
        gate_pre = jnp.dot(tokens_v[...], gate_v[:, cols], preferred_element_type=jnp.float32)
        up_pre = jnp.dot(tokens_v[...], up_v[:, cols], preferred_element_type=jnp.float32)
        d_hidden = lax.dot_general(
            masked_v[...], down_v[cols, :], (((1,), (1,)), ((), ())), preferred_element_type=jnp.float32
        )
        gelu_value, gelu_slope = gelu_parts(gate_pre)
        gate_rows = (d_hidden * up_pre * gelu_slope).astype(jnp.bfloat16)
        up_rows = (d_hidden * gelu_value).astype(jnp.bfloat16)
        hidden_rows = (gelu_value * up_pre).astype(jnp.bfloat16)
        hidden[:, cols], d_gate[:, cols], d_up[:, cols] = hidden_rows, gate_rows, up_rows
        if near:
            for k, (gate_gram, up_gram, own_gram) in enumerate(
                zip(by_block(gate_rows, size), by_block(up_rows, size), by_block(hidden_rows, size))
            ):
                pair_gram[k] += gate_gram + up_gram
                hidden_gram[k] += own_gram

    if full:
        lax.fori_loop(0, full, lambda k, _: (work(k, pl.multiple_of(k * tile, tile), tile), 0)[1], 0)
    if tail:
        work(full, full * tile, tail)
    if near:
        half = tokens_v.shape[0] // 2
        row_seq = lax.broadcasted_iota(jnp.int32, (half, half), 0) // LEN
        col_seq = lax.broadcasted_iota(jnp.int32, (half, half), 1) // LEN
        token_grams, masked_grams = by_block(tokens_v[...], 0), by_block(masked_v[...], 0)
        for k in range(2):
            total = token_grams[k] * pair_gram[k] + masked_grams[k] * hidden_gram[k]
            for seq in range(half // LEN):
                own = jnp.where((row_seq == seq) & (col_seq == seq), total, 0.0)
                lanes = jnp.sum(own, axis=0, keepdims=True)
                at = k * (half // LEN) + seq
                norms[at : at + 1, :] = jnp.broadcast_to(
                    jnp.sum(lanes, axis=1, keepdims=True), (1, norms.shape[1])
                )


def block(near, tokens, masked, gate_weight, up_weight, down_weight):
    rows, units = tokens.shape[0], gate_weight.shape[1]
    count = units // 256 + (1 if units % 256 else 0)
    anywhere, here = pl.BlockSpec(memory_space=pl.ANY), pl.BlockSpec(memory_space=pltpu.VMEM)
    hidden = jax.ShapeDtypeStruct((rows, units), jnp.bfloat16)
    grams = [pltpu.VMEM((2, rows // 2, rows // 2), jnp.float32)] * 2
    args = (tokens, masked, gate_weight, up_weight, down_weight)
    return pl.pallas_call(
        functools.partial(block_kernel, near),
        out_shape=[hidden] * 3 + [jax.ShapeDtypeStruct((rows // LEN, 128), jnp.float32)] if near else [hidden] * 3,
        in_specs=[anywhere] * 5,
        out_specs=[here] * (4 if near else 3),
        scratch_shapes=[pltpu.VMEM(array.shape, array.dtype) for array in args]
        + (grams if near else [])
        + [pltpu.SemaphoreType.DMA((3, count + 1))],
        compiler_params=pltpu.CompilerParams(vmem_limit_bytes=44 << 20),
        cost_estimate=pl.CostEstimate(flops=0, bytes_accessed=0, transcendentals=0),
    )(*args)


def input_kernel(core, gate_w, up_w, d_gate, d_up, last, own, other):
    total = lax.dot_general(gate_w[...], d_gate[...], (((1,), (1,)), ((), ())), preferred_element_type=jnp.float32)
    total += lax.dot_general(up_w[...], d_up[...], (((1,), (1,)), ((), ())), preferred_element_type=jnp.float32)

    @pl.when(pl.program_id(1) == 0)
    def _():
        own[0] = total

    @pl.when(pl.program_id(1) == 1)
    def _():
        other[0] = total


def input_part(core, gate_weight, up_weight, d_gate, d_up, last):
    width, units = gate_weight.shape
    rows = d_gate.shape[0]
    whole = pl.BlockSpec((rows, units), lambda x, turn, core: (0, 0))
    part = pl.BlockSpec((width // 4, units), lambda x, turn, core: (x * 2 + lax.rem(turn + core[0], 2), 0))
    out = pl.BlockSpec((1, width // 4, rows), lambda x, turn, core: (x, 0, 0))
    shape = jax.ShapeDtypeStruct((2, width // 4, rows), jnp.float32)
    return pl.pallas_call(
        input_kernel,
        grid_spec=pltpu.PrefetchScalarGridSpec(
            num_scalar_prefetch=1,
            grid=(2, 2),
            in_specs=[part, part, whole, whole, pl.BlockSpec(memory_space=pl.ANY)],
            out_specs=[out, out],
        ),
        out_shape=[shape, shape],
        compiler_params=pltpu.CompilerParams(vmem_limit_bytes=32 << 20),
        cost_estimate=pl.CostEstimate(flops=0, bytes_accessed=0, transcendentals=0),
    )(core.reshape(1).astype(jnp.int32), gate_weight, up_weight, d_gate, d_up, last)


class Ring:
    def __init__(self, take, here, way, route):
        self.take, self.here, self.way, self.route = take, here, way, route
        self.hops = 3
        self.part = take((here + 3 * way) % 4)

    def step(self, *others):
        self.hops -= 1
        part = send(self.part, self.route) + self.take((self.here + self.hops * self.way) % 4)
        self.part = after(part, *others) if others else part


def flow_widths(units):
    tiles = 3 * units // 128
    return [(tiles + 3 - k) // 4 * 128 for k in range(4)]


def product_kernel(
    near_t, far_t, near_c, far_c, d_gate, far_gate, d_up, far_up, hidden, far_hidden, near_w, far_w, near_a, far_a,
    *refs,
):
    outs, scaled = refs[:4], refs[4:]

    @pl.when(pl.program_id(0) == 0)
    def _():
        for rows, weight, into in zip((d_gate, far_gate, d_up, far_up), (near_w, far_w) * 2, scaled):
            into[...] = (rows[...].astype(jnp.float32) * weight[...]).astype(jnp.bfloat16)

    near_cot = (near_c[...].astype(jnp.float32) * near_a[...]).astype(jnp.bfloat16)
    far_cot = (far_c[...].astype(jnp.float32) * far_a[...]).astype(jnp.bfloat16)
    units = hidden.shape[1]
    parts = []
    for lefts, rights in (
        ((near_t[...], far_t[...]), scaled[:2]),
        ((near_t[...], far_t[...]), scaled[2:]),
        ((near_cot, far_cot), (hidden, far_hidden)),
    ):
        total = jnp.dot(lefts[0], rights[0][...], preferred_element_type=jnp.float32)
        parts.append(total + jnp.dot(lefts[1], rights[1][...], preferred_element_type=jnp.float32))
    start = 0
    for out in outs:
        width = out.shape[1]
        for k, part in enumerate(parts):
            low, high = max(start, k * units), min(start + width, (k + 1) * units)
            if low < high:
                out[:, low - start : high - start] = part[:, low - k * units : high - k * units]
        start += width


def products(*args):
    count, rows = args[0].shape
    units = args[4].shape[1]
    left = pl.BlockSpec((count // 4, rows), lambda tile: (tile, 0))
    right = pl.BlockSpec((rows, units), lambda tile: (0, 0))
    column = pl.BlockSpec((rows, 1), lambda tile: (0, 0))
    across = pl.BlockSpec((1, rows), lambda tile: (0, 0))
    widths = flow_widths(units)
    return pl.pallas_call(
        product_kernel,
        grid=(4,),
        out_shape=[jax.ShapeDtypeStruct((count, width), jnp.float32) for width in widths],
        in_specs=[left] * 4 + [right] * 6 + [column] * 2 + [across] * 2,
        out_specs=[pl.BlockSpec((count // 4, width), lambda tile: (tile, 0)) for width in widths],
        scratch_shapes=[pltpu.VMEM((rows, units), jnp.bfloat16)] * 4,
        compiler_params=pltpu.CompilerParams(vmem_limit_bytes=44 << 20),
        cost_estimate=pl.CostEstimate(flops=12 * rows * count * units, bytes_accessed=28 << 20, transcendentals=0),
    )(*args)


def per_device(tokens, cotangent, lengths, gate_weight, up_weight, down_weight):
    seq_count = lengths.shape[0]
    row_count, width = tokens.shape
    total_seqs = seq_count * lax.axis_size("dp")
    clip_bound = 0.5 * math.sqrt(D * FFW * LEN)
    dp, tensor = lax.axis_index("dp"), lax.axis_index("tensor")
    y, z, x_lo = dp // 8, (dp // 2) % 4, dp % 2
    x_hi, core = tensor // 2, tensor % 2
    way = 1 - 2 * core
    half = row_count // 2
    strip = width // 32

    positions = jnp.arange(LEN, dtype=jnp.int32)
    live = (positions[None, :] < lengths[:, None]).reshape(row_count)[:, None]
    masked = cotangent * live.astype(jnp.bfloat16)

    def own_half(rows, start):
        return lax.dynamic_slice_in_dim(rows, start, half, 0).astype(jnp.float32)

    lanes = jnp.broadcast_to(live.astype(jnp.bfloat16), (row_count, 128))
    token_half = send(jnp.concatenate([own_half(tokens, core * half), own_half(lanes, core * half)], axis=1), RING_X)

    cot_half = send(own_half(cotangent, core * half), RING_X)

    hidden_act, d_gate, d_up, norms = block(True, tokens, masked, gate_weight, up_weight, down_weight)
    own_input, other_input = input_part(core, gate_weight, up_weight, d_gate, d_up, norms)
    norm_pair = norms[:, 0] + send(norms[:, 0], CORES)

    column_at = jnp.arange(width // 2, dtype=jnp.int32)
    source = (column_at // strip) * (2 * strip) + later(x_lo, norms) * strip + column_at % strip
    pick = (jnp.arange(width, dtype=jnp.int32)[:, None] == source[None, :]).astype(jnp.bfloat16)

    def picked(rows):
        return lax.dot_general(
            pick, rows, (((0,), (1,)), ((), ())), preferred_element_type=jnp.float32
        ).astype(jnp.bfloat16)

    near_tokens, near_cot = picked(tokens), picked(masked)

    def joined(mine, theirs, mask_mine, mask_theirs):
        return jnp.concatenate(
            [(mine * mask_mine).astype(jnp.bfloat16), (theirs * mask_theirs).astype(jnp.bfloat16)], axis=0
        )

    token_half = after(token_half, near_tokens, near_cot, own_input)
    cot_half = after(cot_half, near_tokens, near_cot, own_input)
    norm_pair = after(norm_pair, token_half, cot_half)
    norm_sq = norm_pair + send(norm_pair, X_HI)
    clip_ratio = jnp.sqrt(norm_sq) / clip_bound
    clip_factor = 1.0 / jnp.maximum(1.0, clip_ratio)
    token_rest, cot_rest = send(token_half, CORES), send(cot_half, CORES)
    masks = token_half[:, width : width + 1], token_rest[:, width : width + 1]
    far_tokens = joined(token_half[:, :width], token_rest[:, :width], *masks)
    far_masked = joined(cot_half, cot_rest, *masks)
    far_hidden, far_gate, far_up = block(False, far_tokens, far_masked, gate_weight, up_weight, down_weight)
    far_cols, far_cot = picked(far_tokens), picked(far_masked)

    def row_weight(by_seq, shift, axis):
        row_seq = (jnp.arange(row_count, dtype=jnp.int32) // LEN + shift) % seq_count
        seqs = jnp.arange(seq_count, dtype=jnp.int32)
        spread = jnp.expand_dims(row_seq, axis) == jnp.expand_dims(seqs, 1 - axis)
        return jnp.sum(jnp.where(spread, jnp.expand_dims(by_seq, 1 - axis), 0.0), axis=axis, keepdims=True)

    near_mean = clip_factor / total_seqs
    far_mean = send(near_mean, X_LO)
    shift = core * (seq_count // 2)
    near_weight, far_weight = row_weight(near_mean, 0, 1), row_weight(far_mean, shift, 1)
    near_across, far_across = row_weight(near_mean, 0, 0), row_weight(far_mean, shift, 0)

    grads = products(
        near_tokens, far_cols, near_cot, far_cot, d_gate, far_gate, d_up, far_up, hidden_act, far_hidden,
        near_weight, far_weight, near_across, far_across,
    )
    units = d_gate.shape[1]
    grads = [grad.reshape(4, 4, strip, grad.shape[1]) for grad in grads]

    def line(rows, axis=0):
        return lambda k: lax.dynamic_index_in_dim(rows, k, axis, keepdims=False)

    flows = [
        (line(grad, 0), y, RING_Y, z, RING_Z) if k % 2 == 0 else (line(grad, 1), z, RING_Z, y, RING_Y)
        for k, grad in enumerate(grads)
    ]
    rings = [Ring(take, here, way, route) for take, here, route, _, _ in flows]

    part = own_input + send(other_input, CORES)
    across = after(lax.dynamic_index_in_dim(part, 1 - x_hi, 0, keepdims=False), far_mean)
    summed_input = send(across, X_HI)
    summed_input = summed_input + lax.dynamic_index_in_dim(part, x_hi, 0, keepdims=False)
    for _ in range(3):
        for ring in rings:
            ring.step()
    rows = together(*[ring.part for ring in rings])
    rings = [Ring(line(row), here, way, route) for row, (_, _, _, here, route) in zip(rows, flows)]
    for turn in range(3):
        for ring in rings:
            ring.step()
        if turn == 0:
            clip_late = after(clip_factor, *[ring.part for ring in rings])
    input_grad = (summed_input * row_weight(clip_late, 0, 0)).T.astype(jnp.bfloat16)
    sums = jnp.concatenate([ring.part for ring in rings], axis=1)
    grad_gate, grad_up = sums[:, :units], sums[:, units : 2 * units]
    grad_down = sums[:, 2 * units :].T
    return (input_grad, clip_ratio, grad_gate, grad_up, grad_down)


def solution(mesh):
    placed = (
        P("dp", None),
        P("dp", None),
        P("dp"),
        P(None, "tensor"),
        P(None, "tensor"),
        P("tensor", None),
    )
    return jax.shard_map(
        per_device,
        mesh=mesh,
        in_specs=placed,
        out_specs=(
            P("dp", "tensor"),
            P("dp"),
            P("dp", "tensor"),
            P("dp", "tensor"),
            P("tensor", "dp"),
        ),
        check_vma=False,
    )
```

```python
import functools
import math

import jax
import jax.numpy as jnp
from jax import lax
from jax.experimental import pallas as pl
from jax.experimental.pallas import tpu as pltpu
from jax.sharding import PartitionSpec as P

D = 2304
FFW = 4608
LEN = 64
AXES = ("dp", "tensor")


def place(y, z, x, core):
    y, z, x = y % 4, z % 4, x % 4
    return ((y * 4 + z) * 2 + x % 2) * 4 + (x // 2) * 2 + core


def pairs(target):
    return [
        (place(y, z, x, core), place(*target(y, z, x, core)))
        for y in range(4)
        for z in range(4)
        for x in range(4)
        for core in range(2)
    ]


RING_YZ = pairs(
    lambda y, z, x, core: (y, z + 1 - 2 * core, x, core) if x % 2 == 0 else (y + 1 - 2 * core, z, x, core)
)
RING_Y = pairs(lambda y, z, x, core: (y + 1 - 2 * core, z, x, core))
RING_Z = pairs(lambda y, z, x, core: (y, z + 1 - 2 * core, x, core))
RING_X = pairs(lambda y, z, x, core: (y, z, x + 1 - 2 * core, core))
CORES = pairs(lambda y, z, x, core: (y, z, x, 1 - core))
X_LO = pairs(lambda y, z, x, core: (y, z, x ^ 1, core))
X_HI = pairs(lambda y, z, x, core: (y, z, x ^ 2, core))


def send(value, route):
    return lax.optimization_barrier(lax.ppermute(lax.optimization_barrier(value), AXES, route))


def nothing(*refs):
    pass


def after(value, *others):
    anywhere = pl.BlockSpec(memory_space=pl.ANY)
    return pl.pallas_call(
        nothing,
        out_shape=jax.ShapeDtypeStruct(value.shape, value.dtype),
        in_specs=[anywhere] * (1 + len(others)),
        out_specs=anywhere,
        input_output_aliases={0: 0},
        cost_estimate=pl.CostEstimate(flops=0, bytes_accessed=0, transcendentals=0),
        compiler_params=pltpu.CompilerParams(vmem_limit_bytes=1 << 20),
    )(value, *others)


def together(*values):
    anywhere = pl.BlockSpec(memory_space=pl.ANY)
    return pl.pallas_call(
        nothing,
        out_shape=[jax.ShapeDtypeStruct(value.shape, value.dtype) for value in values],
        in_specs=[anywhere] * len(values),
        out_specs=[anywhere] * len(values),
        input_output_aliases={k: k for k in range(len(values))},
        cost_estimate=pl.CostEstimate(flops=0, bytes_accessed=0, transcendentals=0),
        compiler_params=pltpu.CompilerParams(vmem_limit_bytes=1 << 20),
    )(*values)


def later(index, *others):
    return after(jnp.reshape(index, (1,)), *others)[0]


def gelu_parts(pre_act):
    slope_k = math.sqrt(2.0 / math.pi)
    cubed = pre_act * pre_act * pre_act
    tanh_val = jnp.tanh(slope_k * (pre_act + 0.044715 * cubed))
    gelu_value = 0.5 * pre_act * (1.0 + tanh_val)
    gelu_slope = 0.5 * (1.0 + tanh_val) + 0.5 * pre_act * (1.0 - tanh_val * tanh_val) * slope_k * (
        1.0 + 3.0 * 0.044715 * pre_act * pre_act
    )
    return (gelu_value, gelu_slope)


def cross_rows(left, right):
    return lax.dot_general(
        left, right, (((0,), (0,)), ((), ())), preferred_element_type=jnp.float32
    )


def by_block(rows, width):
    half = rows.shape[0] // 2
    return [
        lax.dot_general(part, part, (((1,), (1,)), ((), ())), preferred_element_type=jnp.float32)
        for part in (rows[:half], rows[half:])
    ]


def block_kernel(near, *refs):
    if near:
        tokens, masked, gate_w, up_w, down_w, hidden, d_gate, d_up, norms = refs[:9]
        tokens_v, masked_v, gate_v, up_v, down_v, pair_gram, hidden_gram, sems = refs[9:]
    else:
        fetched, (gate_w, up_w, down_w, hidden, d_gate, d_up, tokens_v, masked_v) = refs[:4], refs[4:12]
        wide, (gate_v, up_v, down_v, sems) = refs[12:16], refs[16:]
    units = gate_w.shape[1]
    tile = 256
    full, tail = units // tile, units % tile
    spans = [(k * tile, tile) for k in range(full)] + ([(full * tile, tail)] if tail else [])

    def copies(k, start, size):
        cols = pl.ds(start, size)
        return (
            pltpu.make_async_copy(gate_w.at[:, cols], gate_v.at[:, cols], sems.at[0, k]),
            pltpu.make_async_copy(up_w.at[:, cols], up_v.at[:, cols], sems.at[1, k]),
            pltpu.make_async_copy(down_w.at[cols, :], down_v.at[cols, :], sems.at[2, k]),
        )

    moves = ((tokens, tokens_v), (masked, masked_v)) if near else zip(fetched, wide)
    rows_in = [
        pltpu.make_async_copy(source, target, sems.at[k % 3, len(spans) + k // 3])
        for k, (source, target) in enumerate(moves)
    ]
    for copy in rows_in:
        copy.start()
    for k, (start, size) in enumerate(spans):
        for copy in copies(k, start, size):
            copy.start()
    for copy in rows_in:
        copy.wait()
    if not near:
        half, width = tokens_v.shape[0] // 2, tokens_v.shape[1]
        for k in range(2):
            rows, mask = slice(k * half, (k + 1) * half), wide[k][:, width : width + 1]
            tokens_v[rows, :] = (wide[k][:, :width] * mask).astype(jnp.bfloat16)
            masked_v[rows, :] = (wide[2 + k][...] * mask).astype(jnp.bfloat16)
    if near:
        pair_gram[...] = jnp.zeros_like(pair_gram)
        hidden_gram[...] = jnp.zeros_like(hidden_gram)

    def work(k, start, size):
        for copy in copies(k, start, size):
            copy.wait()
        cols = pl.ds(start, size)
        gate_pre = jnp.dot(tokens_v[...], gate_v[:, cols], preferred_element_type=jnp.float32)
        up_pre = jnp.dot(tokens_v[...], up_v[:, cols], preferred_element_type=jnp.float32)
        d_hidden = lax.dot_general(
            masked_v[...], down_v[cols, :], (((1,), (1,)), ((), ())), preferred_element_type=jnp.float32
        )
        gelu_value, gelu_slope = gelu_parts(gate_pre)
        gate_rows = (d_hidden * up_pre * gelu_slope).astype(jnp.bfloat16)
        up_rows = (d_hidden * gelu_value).astype(jnp.bfloat16)
        hidden_rows = (gelu_value * up_pre).astype(jnp.bfloat16)
        hidden[:, cols], d_gate[:, cols], d_up[:, cols] = hidden_rows, gate_rows, up_rows
        if near:
            for k, (gate_gram, up_gram, own_gram) in enumerate(
                zip(by_block(gate_rows, size), by_block(up_rows, size), by_block(hidden_rows, size))
            ):
                pair_gram[k] += gate_gram + up_gram
                hidden_gram[k] += own_gram

    if full:
        lax.fori_loop(0, full, lambda k, _: (work(k, pl.multiple_of(k * tile, tile), tile), 0)[1], 0)
    if tail:
        work(full, full * tile, tail)
    if near:
        half = tokens_v.shape[0] // 2
        row_seq = lax.broadcasted_iota(jnp.int32, (half, half), 0) // LEN
        col_seq = lax.broadcasted_iota(jnp.int32, (half, half), 1) // LEN
        token_grams, masked_grams = by_block(tokens_v[...], 0), by_block(masked_v[...], 0)
        for k in range(2):
            total = token_grams[k] * pair_gram[k] + masked_grams[k] * hidden_gram[k]
            for seq in range(half // LEN):
                own = jnp.where((row_seq == seq) & (col_seq == seq), total, 0.0)
                lanes = jnp.sum(own, axis=0, keepdims=True)
                at = k * (half // LEN) + seq
                norms[at : at + 1, :] = jnp.broadcast_to(
                    jnp.sum(lanes, axis=1, keepdims=True), (1, norms.shape[1])
                )


def block(near, rows_in, gate_weight, up_weight, down_weight):
    units, width = down_weight.shape
    rows = rows_in[0].shape[0] * (1 if near else 2)
    count = units // 256 + (1 if units % 256 else 0)
    anywhere, here = pl.BlockSpec(memory_space=pl.ANY), pl.BlockSpec(memory_space=pltpu.VMEM)
    hidden = jax.ShapeDtypeStruct((rows, units), jnp.bfloat16)
    whole = jax.ShapeDtypeStruct((rows, width), jnp.bfloat16)
    grams = [pltpu.VMEM((2, rows // 2, rows // 2), jnp.float32)] * 2
    args = (*rows_in, gate_weight, up_weight, down_weight)
    more = [jax.ShapeDtypeStruct((rows // LEN, 128), jnp.float32)] if near else [whole] * 2
    return pl.pallas_call(
        functools.partial(block_kernel, near),
        out_shape=[hidden] * 3 + more,
        in_specs=[anywhere] * len(args),
        out_specs=[here] * (3 + len(more)),
        scratch_shapes=[pltpu.VMEM(array.shape, array.dtype) for array in args]
        + (grams if near else [])
        + [pltpu.SemaphoreType.DMA((3, count + 2))],
        compiler_params=pltpu.CompilerParams(vmem_limit_bytes=(44 if near else 50) << 20),
        cost_estimate=pl.CostEstimate(flops=0, bytes_accessed=0, transcendentals=0),
    )(*args)


def input_kernel(core, gate_w, up_w, d_gate, d_up, last, own, other):
    total = lax.dot_general(gate_w[...], d_gate[...], (((1,), (1,)), ((), ())), preferred_element_type=jnp.float32)
    total += lax.dot_general(up_w[...], d_up[...], (((1,), (1,)), ((), ())), preferred_element_type=jnp.float32)

    @pl.when(pl.program_id(1) == 0)
    def _():
        own[0] = total

    @pl.when(pl.program_id(1) == 1)
    def _():
        other[0] = total


def input_part(core, gate_weight, up_weight, d_gate, d_up, last):
    width, units = gate_weight.shape
    rows = d_gate.shape[0]
    whole = pl.BlockSpec((rows, units), lambda x, turn, core: (0, 0))
    part = pl.BlockSpec((width // 4, units), lambda x, turn, core: (x * 2 + lax.rem(turn + core[0], 2), 0))
    out = pl.BlockSpec((1, width // 4, rows), lambda x, turn, core: (x, 0, 0))
    shape = jax.ShapeDtypeStruct((2, width // 4, rows), jnp.float32)
    return pl.pallas_call(
        input_kernel,
        grid_spec=pltpu.PrefetchScalarGridSpec(
            num_scalar_prefetch=1,
            grid=(2, 2),
            in_specs=[part, part, whole, whole, pl.BlockSpec(memory_space=pl.ANY)],
            out_specs=[out, out],
        ),
        out_shape=[shape, shape],
        compiler_params=pltpu.CompilerParams(vmem_limit_bytes=32 << 20),
        cost_estimate=pl.CostEstimate(flops=0, bytes_accessed=0, transcendentals=0),
    )(core.reshape(1).astype(jnp.int32), gate_weight, up_weight, d_gate, d_up, last)


class Ring:
    def __init__(self, take, here, way, route):
        self.take, self.here, self.way, self.route = take, here, way, route
        self.hops = 3
        self.part = take((here + 3 * way) % 4)

    def step(self, *others):
        self.hops -= 1
        part = send(self.part, self.route) + self.take((self.here + self.hops * self.way) % 4)
        self.part = after(part, *others) if others else part


def flow_widths(units):
    tiles = 3 * units // 128
    return [(tiles + 3 - k) // 4 * 128 for k in range(4)]


def product_kernel(
    near_t, far_t, near_c, far_c, d_gate, far_gate, d_up, far_up, hidden, far_hidden, near_s, far_s, shift, *refs
):
    outs, scaled = refs[:4], refs[4:]
    rows = hidden.shape[0]
    seq_count = rows // LEN

    def spread(by_seq, shift_by, axis):
        shape = (rows, 1) if axis == 0 else (1, rows)
        row_seq = lax.broadcasted_iota(jnp.int32, shape, axis) // LEN + shift_by
        row_seq = jnp.where(row_seq >= seq_count, row_seq - seq_count, row_seq)
        weight = jnp.zeros(shape, jnp.float32)
        for seq in range(seq_count):
            weight = jnp.where(row_seq == seq, by_seq[seq], weight)
        return weight

    @pl.when(pl.program_id(0) == 0)
    def _():
        weights = [spread(near_s, 0, 0), spread(far_s, shift[0], 0)]
        for rows_of, weight, into in zip((d_gate, far_gate, d_up, far_up), weights * 2, scaled):
            into[...] = (rows_of[...].astype(jnp.float32) * weight).astype(jnp.bfloat16)

    near_cot = (near_c[...].astype(jnp.float32) * spread(near_s, 0, 1)).astype(jnp.bfloat16)
    far_cot = (far_c[...].astype(jnp.float32) * spread(far_s, shift[0], 1)).astype(jnp.bfloat16)
    units = hidden.shape[1]
    parts = []
    for lefts, rights in (
        ((near_t[...], far_t[...]), scaled[:2]),
        ((near_t[...], far_t[...]), scaled[2:]),
        ((near_cot, far_cot), (hidden, far_hidden)),
    ):
        total = jnp.dot(lefts[0], rights[0][...], preferred_element_type=jnp.float32)
        parts.append(total + jnp.dot(lefts[1], rights[1][...], preferred_element_type=jnp.float32))
    start = 0
    for out in outs:
        width = out.shape[1]
        for k, part in enumerate(parts):
            low, high = max(start, k * units), min(start + width, (k + 1) * units)
            if low < high:
                out[:, low - start : high - start] = part[:, low - k * units : high - k * units]
        start += width


def products(*args):
    count, rows = args[0].shape
    units = args[4].shape[1]
    left = pl.BlockSpec((count // 4, rows), lambda tile: (tile, 0))
    right = pl.BlockSpec((rows, units), lambda tile: (0, 0))
    scalars = pl.BlockSpec(memory_space=pltpu.SMEM)
    widths = flow_widths(units)
    return pl.pallas_call(
        product_kernel,
        grid=(4,),
        out_shape=[jax.ShapeDtypeStruct((count, width), jnp.float32) for width in widths],
        in_specs=[left] * 4 + [right] * 6 + [scalars] * 3,
        out_specs=[pl.BlockSpec((count // 4, width), lambda tile: (tile, 0)) for width in widths],
        scratch_shapes=[pltpu.VMEM((rows, units), jnp.bfloat16)] * 4,
        compiler_params=pltpu.CompilerParams(vmem_limit_bytes=44 << 20),
        cost_estimate=pl.CostEstimate(flops=12 * rows * count * units, bytes_accessed=28 << 20, transcendentals=0),
    )(*args)


def per_device(tokens, cotangent, lengths, gate_weight, up_weight, down_weight):
    seq_count = lengths.shape[0]
    row_count, width = tokens.shape
    total_seqs = seq_count * lax.axis_size("dp")
    clip_bound = 0.5 * math.sqrt(D * FFW * LEN)
    dp, tensor = lax.axis_index("dp"), lax.axis_index("tensor")
    y, z, x_lo = dp // 8, (dp // 2) % 4, dp % 2
    x_hi, core = tensor // 2, tensor % 2
    way = 1 - 2 * core
    half = row_count // 2
    strip = width // 32

    positions = jnp.arange(LEN, dtype=jnp.int32)
    live = (positions[None, :] < lengths[:, None]).reshape(row_count)[:, None]
    masked = cotangent * live.astype(jnp.bfloat16)

    def own_half(rows, start):
        return lax.dynamic_slice_in_dim(rows, start, half, 0).astype(jnp.float32)

    lanes = jnp.broadcast_to(live.astype(jnp.bfloat16), (row_count, 128))
    token_half = send(jnp.concatenate([own_half(tokens, core * half), own_half(lanes, core * half)], axis=1), RING_X)

    cot_half = send(own_half(cotangent, core * half), RING_X)

    hidden_act, d_gate, d_up, norms = block(True, (tokens, masked), gate_weight, up_weight, down_weight)
    own_input, other_input = input_part(core, gate_weight, up_weight, d_gate, d_up, norms)
    norm_pair = norms[:, 0] + send(norms[:, 0], CORES)

    column_at = jnp.arange(width // 2, dtype=jnp.int32)
    source = (column_at // strip) * (2 * strip) + later(x_lo, norms) * strip + column_at % strip
    pick = (jnp.arange(width, dtype=jnp.int32)[:, None] == source[None, :]).astype(jnp.bfloat16)

    def picked(rows):
        return lax.dot_general(
            pick, rows, (((0,), (1,)), ((), ())), preferred_element_type=jnp.float32
        ).astype(jnp.bfloat16)

    near_tokens, near_cot = picked(tokens), picked(masked)

    token_half = after(token_half, near_tokens, near_cot, own_input)
    cot_half = after(cot_half, near_tokens, near_cot, own_input)
    norm_pair = after(norm_pair, token_half, cot_half)
    norm_sq = norm_pair + send(norm_pair, X_HI)
    clip_ratio = jnp.sqrt(norm_sq) / clip_bound
    clip_factor = 1.0 / jnp.maximum(1.0, clip_ratio)
    token_rest, cot_rest = send(token_half, CORES), send(cot_half, CORES)
    far_hidden, far_gate, far_up, far_tokens, far_masked = block(
        False, (token_half, token_rest, cot_half, cot_rest), gate_weight, up_weight, down_weight
    )
    far_cols, far_cot = picked(far_tokens), picked(far_masked)

    def row_weight(by_seq, shift, axis):
        row_seq = (jnp.arange(row_count, dtype=jnp.int32) // LEN + shift) % seq_count
        seqs = jnp.arange(seq_count, dtype=jnp.int32)
        spread = jnp.expand_dims(row_seq, axis) == jnp.expand_dims(seqs, 1 - axis)
        return jnp.sum(jnp.where(spread, jnp.expand_dims(by_seq, 1 - axis), 0.0), axis=axis, keepdims=True)

    near_mean = clip_factor / total_seqs
    far_mean = send(near_mean, X_LO)
    shift = core * (seq_count // 2)
    grads = products(
        near_tokens, far_cols, near_cot, far_cot, d_gate, far_gate, d_up, far_up, hidden_act, far_hidden,
        near_mean, far_mean, shift.reshape(1),
    )
    units = d_gate.shape[1]
    grads = [grad.reshape(4, 4, strip, grad.shape[1]) for grad in grads]

    def line(rows, axis=0):
        return lambda k: lax.dynamic_index_in_dim(rows, k, axis, keepdims=False)

    flows = [
        (line(grad, 0), y, RING_Y, z, RING_Z) if k % 2 == 0 else (line(grad, 1), z, RING_Z, y, RING_Y)
        for k, grad in enumerate(grads)
    ]
    rings = [Ring(take, here, way, route) for take, here, route, _, _ in flows]

    part = own_input + send(other_input, CORES)
    across = after(lax.dynamic_index_in_dim(part, 1 - x_hi, 0, keepdims=False), far_mean)
    summed_input = send(across, X_HI)
    summed_input = summed_input + lax.dynamic_index_in_dim(part, x_hi, 0, keepdims=False)
    for _ in range(3):
        for ring in rings:
            ring.step()
    rows = together(*[ring.part for ring in rings])
    rings = [Ring(line(row), here, way, route) for row, (_, _, _, here, route) in zip(rows, flows)]
    for turn in range(3):
        for ring in rings:
            ring.step()
        if turn == 0:
            clip_late = after(clip_factor, *[ring.part for ring in rings])
    input_grad = (summed_input * row_weight(clip_late, 0, 0)).T.astype(jnp.bfloat16)
    sums = jnp.concatenate([ring.part for ring in rings], axis=1)
    grad_gate, grad_up = sums[:, :units], sums[:, units : 2 * units]
    grad_down = sums[:, 2 * units :].T
    return (input_grad, clip_ratio, grad_gate, grad_up, grad_down)


def solution(mesh):
    placed = (
        P("dp", None),
        P("dp", None),
        P("dp"),
        P(None, "tensor"),
        P(None, "tensor"),
        P("tensor", None),
    )
    return jax.shard_map(
        per_device,
        mesh=mesh,
        in_specs=placed,
        out_specs=(
            P("dp", "tensor"),
            P("dp"),
            P("dp", "tensor"),
            P("dp", "tensor"),
            P("tensor", "dp"),
        ),
        check_vma=False,
    )
```

```python
import functools
import math

import jax
import jax.numpy as jnp
from jax import lax
from jax.experimental import pallas as pl
from jax.experimental.pallas import tpu as pltpu
from jax.sharding import PartitionSpec as P

D = 2304
FFW = 4608
LEN = 64
AXES = ("dp", "tensor")


def place(y, z, x, core):
    y, z, x = y % 4, z % 4, x % 4
    return ((y * 4 + z) * 2 + x % 2) * 4 + (x // 2) * 2 + core


def pairs(target):
    return [
        (place(y, z, x, core), place(*target(y, z, x, core)))
        for y in range(4)
        for z in range(4)
        for x in range(4)
        for core in range(2)
    ]


RING_YZ = pairs(
    lambda y, z, x, core: (y, z + 1 - 2 * core, x, core) if x % 2 == 0 else (y + 1 - 2 * core, z, x, core)
)
RING_Y = pairs(lambda y, z, x, core: (y + 1 - 2 * core, z, x, core))
RING_Z = pairs(lambda y, z, x, core: (y, z + 1 - 2 * core, x, core))
RING_X = pairs(lambda y, z, x, core: (y, z, x + 1 - 2 * core, core))
CORES = pairs(lambda y, z, x, core: (y, z, x, 1 - core))
X_LO = pairs(lambda y, z, x, core: (y, z, x ^ 1, core))
X_HI = pairs(lambda y, z, x, core: (y, z, x ^ 2, core))


def send(value, route):
    return lax.optimization_barrier(lax.ppermute(lax.optimization_barrier(value), AXES, route))


def nothing(*refs):
    pass


def after(value, *others):
    anywhere = pl.BlockSpec(memory_space=pl.ANY)
    return pl.pallas_call(
        nothing,
        out_shape=jax.ShapeDtypeStruct(value.shape, value.dtype),
        in_specs=[anywhere] * (1 + len(others)),
        out_specs=anywhere,
        input_output_aliases={0: 0},
        cost_estimate=pl.CostEstimate(flops=0, bytes_accessed=0, transcendentals=0),
        compiler_params=pltpu.CompilerParams(vmem_limit_bytes=1 << 20),
    )(value, *others)


def together(*values):
    anywhere = pl.BlockSpec(memory_space=pl.ANY)
    return pl.pallas_call(
        nothing,
        out_shape=[jax.ShapeDtypeStruct(value.shape, value.dtype) for value in values],
        in_specs=[anywhere] * len(values),
        out_specs=[anywhere] * len(values),
        input_output_aliases={k: k for k in range(len(values))},
        cost_estimate=pl.CostEstimate(flops=0, bytes_accessed=0, transcendentals=0),
        compiler_params=pltpu.CompilerParams(vmem_limit_bytes=1 << 20),
    )(*values)


def later(index, *others):
    return after(jnp.reshape(index, (1,)), *others)[0]


def gelu_parts(pre_act):
    slope_k = math.sqrt(2.0 / math.pi)
    cubed = pre_act * pre_act * pre_act
    tanh_val = jnp.tanh(slope_k * (pre_act + 0.044715 * cubed))
    gelu_value = 0.5 * pre_act * (1.0 + tanh_val)
    gelu_slope = 0.5 * (1.0 + tanh_val) + 0.5 * pre_act * (1.0 - tanh_val * tanh_val) * slope_k * (
        1.0 + 3.0 * 0.044715 * pre_act * pre_act
    )
    return (gelu_value, gelu_slope)


def cross_rows(left, right):
    return lax.dot_general(
        left, right, (((0,), (0,)), ((), ())), preferred_element_type=jnp.float32
    )


def by_block(rows, width):
    half = rows.shape[0] // 2
    return [
        lax.dot_general(part, part, (((1,), (1,)), ((), ())), preferred_element_type=jnp.float32)
        for part in (rows[:half], rows[half:])
    ]


def block_kernel(near, *refs):
    if near:
        tokens, masked, gate_w, up_w, down_w, hidden, d_gate, d_up, norms = refs[:9]
        tokens_v, masked_v, gate_v, up_v, down_v, pair_gram, hidden_gram, sems = refs[9:]
    else:
        fetched, (gate_w, up_w, down_w, hidden, d_gate, d_up, tokens_v, masked_v) = refs[:4], refs[4:12]
        wide, (gate_v, up_v, down_v, sems) = refs[12:16], refs[16:]
    units = gate_w.shape[1]
    tile = 256
    full, tail = units // tile, units % tile
    spans = [(k * tile, tile) for k in range(full)] + ([(full * tile, tail)] if tail else [])

    def copies(k, start, size):
        cols = pl.ds(start, size)
        return (
            pltpu.make_async_copy(gate_w.at[:, cols], gate_v.at[:, cols], sems.at[0, k]),
            pltpu.make_async_copy(up_w.at[:, cols], up_v.at[:, cols], sems.at[1, k]),
            pltpu.make_async_copy(down_w.at[cols, :], down_v.at[cols, :], sems.at[2, k]),
        )

    moves = ((tokens, tokens_v), (masked, masked_v)) if near else zip(fetched, wide)
    rows_in = [
        pltpu.make_async_copy(source, target, sems.at[k % 3, len(spans) + k // 3])
        for k, (source, target) in enumerate(moves)
    ]
    for copy in rows_in:
        copy.start()
    for k, (start, size) in enumerate(spans):
        for copy in copies(k, start, size):
            copy.start()
    for copy in rows_in:
        copy.wait()
    if not near:
        half, width = tokens_v.shape[0] // 2, tokens_v.shape[1]
        for k in range(2):
            rows, mask = slice(k * half, (k + 1) * half), wide[k][:, width : width + 1]
            tokens_v[rows, :] = (wide[k][:, :width] * mask).astype(jnp.bfloat16)
            masked_v[rows, :] = (wide[2 + k][...] * mask).astype(jnp.bfloat16)
    if near:
        pair_gram[...] = jnp.zeros_like(pair_gram)
        hidden_gram[...] = jnp.zeros_like(hidden_gram)

    def work(k, start, size):
        for copy in copies(k, start, size):
            copy.wait()
        cols = pl.ds(start, size)
        gate_pre = jnp.dot(tokens_v[...], gate_v[:, cols], preferred_element_type=jnp.float32)
        up_pre = jnp.dot(tokens_v[...], up_v[:, cols], preferred_element_type=jnp.float32)
        d_hidden = lax.dot_general(
            masked_v[...], down_v[cols, :], (((1,), (1,)), ((), ())), preferred_element_type=jnp.float32
        )
        gelu_value, gelu_slope = gelu_parts(gate_pre)
        gate_rows = (d_hidden * up_pre * gelu_slope).astype(jnp.bfloat16)
        up_rows = (d_hidden * gelu_value).astype(jnp.bfloat16)
        hidden_rows = (gelu_value * up_pre).astype(jnp.bfloat16)
        hidden[:, cols], d_gate[:, cols], d_up[:, cols] = hidden_rows, gate_rows, up_rows
        if near:
            for k, (gate_gram, up_gram, own_gram) in enumerate(
                zip(by_block(gate_rows, size), by_block(up_rows, size), by_block(hidden_rows, size))
            ):
                pair_gram[k] += gate_gram + up_gram
                hidden_gram[k] += own_gram

    if full:
        lax.fori_loop(0, full, lambda k, _: (work(k, pl.multiple_of(k * tile, tile), tile), 0)[1], 0)
    if tail:
        work(full, full * tile, tail)
    if near:
        half = tokens_v.shape[0] // 2
        row_seq = lax.broadcasted_iota(jnp.int32, (half, half), 0) // LEN
        col_seq = lax.broadcasted_iota(jnp.int32, (half, half), 1) // LEN
        token_grams, masked_grams = by_block(tokens_v[...], 0), by_block(masked_v[...], 0)
        for k in range(2):
            total = token_grams[k] * pair_gram[k] + masked_grams[k] * hidden_gram[k]
            for seq in range(half // LEN):
                own = jnp.where((row_seq == seq) & (col_seq == seq), total, 0.0)
                lanes = jnp.sum(own, axis=0, keepdims=True)
                at = k * (half // LEN) + seq
                norms[at : at + 1, :] = jnp.broadcast_to(
                    jnp.sum(lanes, axis=1, keepdims=True), (1, norms.shape[1])
                )


def block(near, rows_in, gate_weight, up_weight, down_weight):
    units, width = down_weight.shape
    rows = rows_in[0].shape[0] * (1 if near else 2)
    count = units // 256 + (1 if units % 256 else 0)
    anywhere, here = pl.BlockSpec(memory_space=pl.ANY), pl.BlockSpec(memory_space=pltpu.VMEM)
    hidden = jax.ShapeDtypeStruct((rows, units), jnp.bfloat16)
    whole = jax.ShapeDtypeStruct((rows, width), jnp.bfloat16)
    grams = [pltpu.VMEM((2, rows // 2, rows // 2), jnp.float32)] * 2
    args = (*rows_in, gate_weight, up_weight, down_weight)
    more = [jax.ShapeDtypeStruct((rows // LEN, 128), jnp.float32)] if near else [whole] * 2
    return pl.pallas_call(
        functools.partial(block_kernel, near),
        out_shape=[hidden] * 3 + more,
        in_specs=[anywhere] * len(args),
        out_specs=[here] * (3 + len(more)),
        scratch_shapes=[pltpu.VMEM(array.shape, array.dtype) for array in args]
        + (grams if near else [])
        + [pltpu.SemaphoreType.DMA((3, count + 2))],
        compiler_params=pltpu.CompilerParams(vmem_limit_bytes=(44 if near else 50) << 20),
        cost_estimate=pl.CostEstimate(flops=0, bytes_accessed=0, transcendentals=0),
    )(*args)


def input_kernel(core, gate_w, up_w, d_gate, d_up, last, own, other):
    total = lax.dot_general(gate_w[...], d_gate[...], (((1,), (1,)), ((), ())), preferred_element_type=jnp.float32)
    total += lax.dot_general(up_w[...], d_up[...], (((1,), (1,)), ((), ())), preferred_element_type=jnp.float32)

    @pl.when(pl.program_id(1) == 0)
    def _():
        own[0] = total

    @pl.when(pl.program_id(1) == 1)
    def _():
        other[0] = total


def input_part(core, gate_weight, up_weight, d_gate, d_up, last):
    width, units = gate_weight.shape
    rows = d_gate.shape[0]
    whole = pl.BlockSpec((rows, units), lambda x, turn, core: (0, 0))
    part = pl.BlockSpec((width // 4, units), lambda x, turn, core: (x * 2 + lax.rem(turn + core[0], 2), 0))
    out = pl.BlockSpec((1, width // 4, rows), lambda x, turn, core: (x, 0, 0))
    shape = jax.ShapeDtypeStruct((2, width // 4, rows), jnp.float32)
    return pl.pallas_call(
        input_kernel,
        grid_spec=pltpu.PrefetchScalarGridSpec(
            num_scalar_prefetch=1,
            grid=(2, 2),
            in_specs=[part, part, whole, whole, pl.BlockSpec(memory_space=pl.ANY)],
            out_specs=[out, out],
        ),
        out_shape=[shape, shape],
        compiler_params=pltpu.CompilerParams(vmem_limit_bytes=32 << 20),
        cost_estimate=pl.CostEstimate(flops=0, bytes_accessed=0, transcendentals=0),
    )(core.reshape(1).astype(jnp.int32), gate_weight, up_weight, d_gate, d_up, last)


class Ring:
    def __init__(self, take, here, way, route):
        self.take, self.here, self.way, self.route = take, here, way, route
        self.hops = 3
        self.part = take((here + 3 * way) % 4)

    def step(self, *others):
        self.hops -= 1
        part = send(self.part, self.route) + self.take((self.here + self.hops * self.way) % 4)
        self.part = after(part, *others) if others else part


def flow_widths(units):
    tiles = 3 * units // 128
    return [(tiles + 3 - k) // 4 * 128 for k in range(4)]


def product_kernel(
    near_t, far_t, near_c, far_c, d_gate, far_gate, d_up, far_up, hidden, far_hidden, near_s, far_s, shift, *refs
):
    outs, scaled = refs[:4], refs[4:]
    rows = hidden.shape[0]
    seq_count = rows // LEN

    def spread(by_seq, shift_by, axis):
        shape = (rows, 1) if axis == 0 else (1, rows)
        row_seq = lax.broadcasted_iota(jnp.int32, shape, axis) // LEN + shift_by
        row_seq = jnp.where(row_seq >= seq_count, row_seq - seq_count, row_seq)
        weight = jnp.zeros(shape, jnp.float32)
        for seq in range(seq_count):
            weight = jnp.where(row_seq == seq, by_seq[seq], weight)
        return weight

    @pl.when(pl.program_id(0) == 0)
    def _():
        weights = [spread(near_s, 0, 0), spread(far_s, shift[0], 0)]
        for rows_of, weight, into in zip((d_gate, far_gate, d_up, far_up), weights * 2, scaled):
            into[...] = (rows_of[...].astype(jnp.float32) * weight).astype(jnp.bfloat16)

    near_cot = (near_c[...].astype(jnp.float32) * spread(near_s, 0, 1)).astype(jnp.bfloat16)
    far_cot = (far_c[...].astype(jnp.float32) * spread(far_s, shift[0], 1)).astype(jnp.bfloat16)
    units = hidden.shape[1]
    parts = []
    for lefts, rights in (
        ((near_t[...], far_t[...]), scaled[:2]),
        ((near_t[...], far_t[...]), scaled[2:]),
        ((near_cot, far_cot), (hidden, far_hidden)),
    ):
        total = jnp.dot(lefts[0], rights[0][...], preferred_element_type=jnp.float32)
        parts.append(total + jnp.dot(lefts[1], rights[1][...], preferred_element_type=jnp.float32))
    start = 0
    for out in outs:
        width = out.shape[1]
        for k, part in enumerate(parts):
            low, high = max(start, k * units), min(start + width, (k + 1) * units)
            if low < high:
                out[:, low - start : high - start] = part[:, low - k * units : high - k * units]
        start += width


def products(*args):
    count, rows = args[0].shape
    units = args[4].shape[1]
    left = pl.BlockSpec((count // 4, rows), lambda tile: (tile, 0))
    right = pl.BlockSpec((rows, units), lambda tile: (0, 0))
    scalars = pl.BlockSpec(memory_space=pltpu.SMEM)
    widths = flow_widths(units)
    return pl.pallas_call(
        product_kernel,
        grid=(4,),
        out_shape=[jax.ShapeDtypeStruct((count, width), jnp.float32) for width in widths],
        in_specs=[left] * 4 + [right] * 6 + [scalars] * 3,
        out_specs=[pl.BlockSpec((count // 4, width), lambda tile: (tile, 0)) for width in widths],
        scratch_shapes=[pltpu.VMEM((rows, units), jnp.bfloat16)] * 4,
        compiler_params=pltpu.CompilerParams(vmem_limit_bytes=44 << 20),
        cost_estimate=pl.CostEstimate(flops=12 * rows * count * units, bytes_accessed=28 << 20, transcendentals=0),
    )(*args)


def per_device(tokens, cotangent, lengths, gate_weight, up_weight, down_weight):
    seq_count = lengths.shape[0]
    row_count, width = tokens.shape
    total_seqs = seq_count * lax.axis_size("dp")
    clip_bound = 0.5 * math.sqrt(D * FFW * LEN)
    dp, tensor = lax.axis_index("dp"), lax.axis_index("tensor")
    y, z, x_lo = dp // 8, (dp // 2) % 4, dp % 2
    x_hi, core = tensor // 2, tensor % 2
    way = 1 - 2 * core
    half = row_count // 2
    strip = width // 32

    positions = jnp.arange(LEN, dtype=jnp.int32)
    live = (positions[None, :] < lengths[:, None]).reshape(row_count)[:, None]
    masked = cotangent * live.astype(jnp.bfloat16)

    def own_half(rows, start):
        return lax.dynamic_slice_in_dim(rows, start, half, 0).astype(jnp.float32)

    lanes = jnp.broadcast_to(live.astype(jnp.bfloat16), (row_count, 128))
    token_half = send(jnp.concatenate([own_half(tokens, core * half), own_half(lanes, core * half)], axis=1), RING_X)

    cot_half = send(own_half(cotangent, core * half), RING_X)

    hidden_act, d_gate, d_up, norms = block(True, (tokens, masked), gate_weight, up_weight, down_weight)
    own_input, other_input = input_part(core, gate_weight, up_weight, d_gate, d_up, norms)
    norm_pair = norms[:, 0] + send(norms[:, 0], CORES)

    column_at = jnp.arange(width // 2, dtype=jnp.int32)
    source = (column_at // strip) * (2 * strip) + later(x_lo, norms) * strip + column_at % strip
    pick = (jnp.arange(width, dtype=jnp.int32)[:, None] == source[None, :]).astype(jnp.bfloat16)

    def picked(rows):
        return lax.dot_general(
            pick, rows, (((0,), (1,)), ((), ())), preferred_element_type=jnp.float32
        ).astype(jnp.bfloat16)

    near_tokens, near_cot = picked(tokens), picked(masked)

    token_half = after(token_half, near_tokens, near_cot, own_input)
    cot_half = after(cot_half, near_tokens, near_cot, own_input)
    token_rest, cot_rest = send(token_half, CORES), send(cot_half, CORES)
    far_hidden, far_gate, far_up, far_tokens, far_masked = block(
        False, (token_half, token_rest, cot_half, cot_rest), gate_weight, up_weight, down_weight
    )
    norm_pair = after(norm_pair, far_hidden)
    norm_sq = norm_pair + send(norm_pair, X_HI)
    clip_ratio = jnp.sqrt(norm_sq) / clip_bound
    clip_factor = 1.0 / jnp.maximum(1.0, clip_ratio)
    far_cols, far_cot = picked(far_tokens), picked(far_masked)

    def row_weight(by_seq, shift, axis):
        row_seq = (jnp.arange(row_count, dtype=jnp.int32) // LEN + shift) % seq_count
        seqs = jnp.arange(seq_count, dtype=jnp.int32)
        spread = jnp.expand_dims(row_seq, axis) == jnp.expand_dims(seqs, 1 - axis)
        return jnp.sum(jnp.where(spread, jnp.expand_dims(by_seq, 1 - axis), 0.0), axis=axis, keepdims=True)

    near_mean = clip_factor / total_seqs
    far_mean = send(near_mean, X_LO)
    shift = core * (seq_count // 2)
    grads = products(
        near_tokens, far_cols, near_cot, far_cot, d_gate, far_gate, d_up, far_up, hidden_act, far_hidden,
        near_mean, far_mean, shift.reshape(1),
    )
    units = d_gate.shape[1]
    grads = [grad.reshape(4, 4, strip, grad.shape[1]) for grad in grads]

    def line(rows, axis=0):
        return lambda k: lax.dynamic_index_in_dim(rows, k, axis, keepdims=False)

    flows = [
        (line(grad, 0), y, RING_Y, z, RING_Z) if k % 2 == 0 else (line(grad, 1), z, RING_Z, y, RING_Y)
        for k, grad in enumerate(grads)
    ]
    rings = [Ring(take, here, way, route) for take, here, route, _, _ in flows]

    part = own_input + send(other_input, CORES)
    across = after(lax.dynamic_index_in_dim(part, 1 - x_hi, 0, keepdims=False), far_mean)
    summed_input = send(across, X_HI)
    summed_input = summed_input + lax.dynamic_index_in_dim(part, x_hi, 0, keepdims=False)
    for _ in range(3):
        for ring in rings:
            ring.step()
    rows = together(*[ring.part for ring in rings])
    rings = [Ring(line(row), here, way, route) for row, (_, _, _, here, route) in zip(rows, flows)]
    for turn in range(3):
        for ring in rings:
            ring.step()
        if turn == 0:
            clip_late = after(clip_factor, *[ring.part for ring in rings])
    input_grad = (summed_input * row_weight(clip_late, 0, 0)).T.astype(jnp.bfloat16)
    sums = jnp.concatenate([ring.part for ring in rings], axis=1)
    grad_gate, grad_up = sums[:, :units], sums[:, units : 2 * units]
    grad_down = sums[:, 2 * units :].T
    return (input_grad, clip_ratio, grad_gate, grad_up, grad_down)


def solution(mesh):
    placed = (
        P("dp", None),
        P("dp", None),
        P("dp"),
        P(None, "tensor"),
        P(None, "tensor"),
        P("tensor", None),
    )
    return jax.shard_map(
        per_device,
        mesh=mesh,
        in_specs=placed,
        out_specs=(
            P("dp", "tensor"),
            P("dp"),
            P("dp", "tensor"),
            P("dp", "tensor"),
            P("tensor", "dp"),
        ),
        check_vma=False,
    )
```

```python
import functools
import math

import jax
import jax.numpy as jnp
from jax import lax
from jax.experimental import pallas as pl
from jax.experimental.pallas import tpu as pltpu
from jax.sharding import PartitionSpec as P

D = 2304
FFW = 4608
LEN = 64
AXES = ("dp", "tensor")


def place(y, z, x, core):
    y, z, x = y % 4, z % 4, x % 4
    return ((y * 4 + z) * 2 + x % 2) * 4 + (x // 2) * 2 + core


def pairs(target):
    return [
        (place(y, z, x, core), place(*target(y, z, x, core)))
        for y in range(4)
        for z in range(4)
        for x in range(4)
        for core in range(2)
    ]


RING_YZ = pairs(
    lambda y, z, x, core: (y, z + 1 - 2 * core, x, core) if x % 2 == 0 else (y + 1 - 2 * core, z, x, core)
)
RING_Y = pairs(lambda y, z, x, core: (y + 1 - 2 * core, z, x, core))
RING_Z = pairs(lambda y, z, x, core: (y, z + 1 - 2 * core, x, core))
RING_X = pairs(lambda y, z, x, core: (y, z, x + 1 - 2 * core, core))
CORES = pairs(lambda y, z, x, core: (y, z, x, 1 - core))
X_LO = pairs(lambda y, z, x, core: (y, z, x ^ 1, core))
X_HI = pairs(lambda y, z, x, core: (y, z, x ^ 2, core))


def send(value, route):
    return lax.optimization_barrier(lax.ppermute(lax.optimization_barrier(value), AXES, route))


def nothing(*refs):
    pass


def after(value, *others):
    anywhere = pl.BlockSpec(memory_space=pl.ANY)
    return pl.pallas_call(
        nothing,
        out_shape=jax.ShapeDtypeStruct(value.shape, value.dtype),
        in_specs=[anywhere] * (1 + len(others)),
        out_specs=anywhere,
        input_output_aliases={0: 0},
        cost_estimate=pl.CostEstimate(flops=0, bytes_accessed=0, transcendentals=0),
        compiler_params=pltpu.CompilerParams(vmem_limit_bytes=1 << 20),
    )(value, *others)


def together(*values):
    anywhere = pl.BlockSpec(memory_space=pl.ANY)
    return pl.pallas_call(
        nothing,
        out_shape=[jax.ShapeDtypeStruct(value.shape, value.dtype) for value in values],
        in_specs=[anywhere] * len(values),
        out_specs=[anywhere] * len(values),
        input_output_aliases={k: k for k in range(len(values))},
        cost_estimate=pl.CostEstimate(flops=0, bytes_accessed=0, transcendentals=0),
        compiler_params=pltpu.CompilerParams(vmem_limit_bytes=1 << 20),
    )(*values)


def later(index, *others):
    return after(jnp.reshape(index, (1,)), *others)[0]


def gelu_parts(pre_act):
    slope_k = math.sqrt(2.0 / math.pi)
    cubed = pre_act * pre_act * pre_act
    tanh_val = jnp.tanh(slope_k * (pre_act + 0.044715 * cubed))
    gelu_value = 0.5 * pre_act * (1.0 + tanh_val)
    gelu_slope = 0.5 * (1.0 + tanh_val) + 0.5 * pre_act * (1.0 - tanh_val * tanh_val) * slope_k * (
        1.0 + 3.0 * 0.044715 * pre_act * pre_act
    )
    return (gelu_value, gelu_slope)


def cross_rows(left, right):
    return lax.dot_general(
        left, right, (((0,), (0,)), ((), ())), preferred_element_type=jnp.float32
    )


def by_block(rows, width):
    half = rows.shape[0] // 2
    return [
        lax.dot_general(part, part, (((1,), (1,)), ((), ())), preferred_element_type=jnp.float32)
        for part in (rows[:half], rows[half:])
    ]


def block_kernel(near, *refs):
    if near:
        tokens, masked, gate_w, up_w, down_w, hidden, d_gate, d_up, norms = refs[:9]
        tokens_v, masked_v, gate_v, up_v, down_v, pair_gram, hidden_gram, sems = refs[9:]
    else:
        fetched, (gate_w, up_w, down_w, hidden, d_gate, d_up, tokens_v, masked_v) = refs[:4], refs[4:12]
        wide, (gate_v, up_v, down_v, sems) = refs[12:16], refs[16:]
    units = gate_w.shape[1]
    tile = 256
    full, tail = units // tile, units % tile
    spans = [(k * tile, tile) for k in range(full)] + ([(full * tile, tail)] if tail else [])

    def copies(k, start, size):
        cols = pl.ds(start, size)
        return (
            pltpu.make_async_copy(gate_w.at[:, cols], gate_v.at[:, cols], sems.at[0, k]),
            pltpu.make_async_copy(up_w.at[:, cols], up_v.at[:, cols], sems.at[1, k]),
            pltpu.make_async_copy(down_w.at[cols, :], down_v.at[cols, :], sems.at[2, k]),
        )

    moves = ((tokens, tokens_v), (masked, masked_v)) if near else zip(fetched, wide)
    rows_in = [
        pltpu.make_async_copy(source, target, sems.at[k % 3, len(spans) + k // 3])
        for k, (source, target) in enumerate(moves)
    ]
    for copy in rows_in:
        copy.start()
    for k, (start, size) in enumerate(spans):
        for copy in copies(k, start, size):
            copy.start()
    for copy in rows_in:
        copy.wait()
    if not near:
        half, width = tokens_v.shape[0] // 2, tokens_v.shape[1]
        for k in range(2):
            rows, mask = slice(k * half, (k + 1) * half), wide[k][:, width : width + 1]
            tokens_v[rows, :] = (wide[k][:, :width] * mask).astype(jnp.bfloat16)
            masked_v[rows, :] = (wide[2 + k][...] * mask).astype(jnp.bfloat16)
    if near:
        pair_gram[...] = jnp.zeros_like(pair_gram)
        hidden_gram[...] = jnp.zeros_like(hidden_gram)

    def work(k, start, size):
        for copy in copies(k, start, size):
            copy.wait()
        cols = pl.ds(start, size)
        gate_pre = jnp.dot(tokens_v[...], gate_v[:, cols], preferred_element_type=jnp.float32)
        up_pre = jnp.dot(tokens_v[...], up_v[:, cols], preferred_element_type=jnp.float32)
        d_hidden = lax.dot_general(
            masked_v[...], down_v[cols, :], (((1,), (1,)), ((), ())), preferred_element_type=jnp.float32
        )
        gelu_value, gelu_slope = gelu_parts(gate_pre)
        gate_rows = (d_hidden * up_pre * gelu_slope).astype(jnp.bfloat16)
        up_rows = (d_hidden * gelu_value).astype(jnp.bfloat16)
        hidden_rows = (gelu_value * up_pre).astype(jnp.bfloat16)
        hidden[:, cols], d_gate[:, cols], d_up[:, cols] = hidden_rows, gate_rows, up_rows
        if near:
            for k, (gate_gram, up_gram, own_gram) in enumerate(
                zip(by_block(gate_rows, size), by_block(up_rows, size), by_block(hidden_rows, size))
            ):
                pair_gram[k] += gate_gram + up_gram
                hidden_gram[k] += own_gram

    if full:
        lax.fori_loop(0, full, lambda k, _: (work(k, pl.multiple_of(k * tile, tile), tile), 0)[1], 0)
    if tail:
        work(full, full * tile, tail)
    if near:
        half = tokens_v.shape[0] // 2
        row_seq = lax.broadcasted_iota(jnp.int32, (half, half), 0) // LEN
        col_seq = lax.broadcasted_iota(jnp.int32, (half, half), 1) // LEN
        token_grams, masked_grams = by_block(tokens_v[...], 0), by_block(masked_v[...], 0)
        for k in range(2):
            total = token_grams[k] * pair_gram[k] + masked_grams[k] * hidden_gram[k]
            for seq in range(half // LEN):
                own = jnp.where((row_seq == seq) & (col_seq == seq), total, 0.0)
                lanes = jnp.sum(own, axis=0, keepdims=True)
                at = k * (half // LEN) + seq
                norms[at : at + 1, :] = jnp.broadcast_to(
                    jnp.sum(lanes, axis=1, keepdims=True), (1, norms.shape[1])
                )


def block(near, rows_in, gate_weight, up_weight, down_weight):
    units, width = down_weight.shape
    rows = rows_in[0].shape[0] * (1 if near else 2)
    count = units // 256 + (1 if units % 256 else 0)
    anywhere, here = pl.BlockSpec(memory_space=pl.ANY), pl.BlockSpec(memory_space=pltpu.VMEM)
    hidden = jax.ShapeDtypeStruct((rows, units), jnp.bfloat16)
    whole = jax.ShapeDtypeStruct((rows, width), jnp.bfloat16)
    grams = [pltpu.VMEM((2, rows // 2, rows // 2), jnp.float32)] * 2
    args = (*rows_in, gate_weight, up_weight, down_weight)
    more = [jax.ShapeDtypeStruct((rows // LEN, 128), jnp.float32)] if near else [whole] * 2
    return pl.pallas_call(
        functools.partial(block_kernel, near),
        out_shape=[hidden] * 3 + more,
        in_specs=[anywhere] * len(args),
        out_specs=[here] * (3 + len(more)),
        scratch_shapes=[pltpu.VMEM(array.shape, array.dtype) for array in args]
        + (grams if near else [])
        + [pltpu.SemaphoreType.DMA((3, count + 2))],
        compiler_params=pltpu.CompilerParams(vmem_limit_bytes=(44 if near else 50) << 20),
        cost_estimate=pl.CostEstimate(flops=0, bytes_accessed=0, transcendentals=0),
    )(*args)


def input_kernel(core, gate_w, up_w, d_gate, d_up, last, own, other):
    total = lax.dot_general(gate_w[...], d_gate[...], (((1,), (1,)), ((), ())), preferred_element_type=jnp.float32)
    total += lax.dot_general(up_w[...], d_up[...], (((1,), (1,)), ((), ())), preferred_element_type=jnp.float32)

    @pl.when(pl.program_id(1) == 0)
    def _():
        own[0] = total

    @pl.when(pl.program_id(1) == 1)
    def _():
        other[0] = total


def input_part(core, gate_weight, up_weight, d_gate, d_up, last):
    width, units = gate_weight.shape
    rows = d_gate.shape[0]
    whole = pl.BlockSpec((rows, units), lambda x, turn, core: (0, 0))
    part = pl.BlockSpec((width // 4, units), lambda x, turn, core: (x * 2 + lax.rem(turn + core[0], 2), 0))
    out = pl.BlockSpec((1, width // 4, rows), lambda x, turn, core: (x, 0, 0))
    shape = jax.ShapeDtypeStruct((2, width // 4, rows), jnp.float32)
    return pl.pallas_call(
        input_kernel,
        grid_spec=pltpu.PrefetchScalarGridSpec(
            num_scalar_prefetch=1,
            grid=(2, 2),
            in_specs=[part, part, whole, whole, pl.BlockSpec(memory_space=pl.ANY)],
            out_specs=[out, out],
        ),
        out_shape=[shape, shape],
        compiler_params=pltpu.CompilerParams(vmem_limit_bytes=32 << 20),
        cost_estimate=pl.CostEstimate(flops=0, bytes_accessed=0, transcendentals=0),
    )(core.reshape(1).astype(jnp.int32), gate_weight, up_weight, d_gate, d_up, last)


class Ring:
    def __init__(self, take, here, way, route, part=None):
        self.take, self.here, self.way, self.route = take, here, way, route
        self.hops = 3
        self.part = take((here + 3 * way) % 4) if part is None else part

    def step(self, *others):
        self.hops -= 1
        part = send(self.part, self.route) + self.take((self.here + self.hops * self.way) % 4)
        self.part = after(part, *others) if others else part


def flow_widths(units):
    tiles = 3 * units // 128
    return [(tiles + 3 - k) // 4 * 128 for k in range(4)]


def product_kernel(
    near_t, far_t, near_c, far_c, d_gate, far_gate, d_up, far_up, hidden, far_hidden, near_s, far_s, place_of, *refs
):
    outs, firsts, scaled = refs[:4], refs[4:8], refs[8:]
    rows = hidden.shape[0]
    seq_count = rows // LEN

    def spread(by_seq, shift_by, axis):
        shape = (rows, 1) if axis == 0 else (1, rows)
        row_seq = lax.broadcasted_iota(jnp.int32, shape, axis) // LEN + shift_by
        row_seq = jnp.where(row_seq >= seq_count, row_seq - seq_count, row_seq)
        weight = jnp.zeros(shape, jnp.float32)
        for seq in range(seq_count):
            weight = jnp.where(row_seq == seq, by_seq[seq], weight)
        return weight

    @pl.when(pl.program_id(0) == 0)
    def _():
        weights = [spread(near_s, 0, 0), spread(far_s, place_of[0], 0)]
        for rows_of, weight, into in zip((d_gate, far_gate, d_up, far_up), weights * 2, scaled):
            into[...] = (rows_of[...].astype(jnp.float32) * weight).astype(jnp.bfloat16)

    near_cot = (near_c[...].astype(jnp.float32) * spread(near_s, 0, 1)).astype(jnp.bfloat16)
    far_cot = (far_c[...].astype(jnp.float32) * spread(far_s, place_of[0], 1)).astype(jnp.bfloat16)
    units = hidden.shape[1]
    parts = []
    for lefts, rights in (
        ((near_t[...], far_t[...]), scaled[:2]),
        ((near_t[...], far_t[...]), scaled[2:]),
        ((near_cot, far_cot), (hidden, far_hidden)),
    ):
        total = jnp.dot(lefts[0], rights[0][...], preferred_element_type=jnp.float32)
        parts.append(total + jnp.dot(lefts[1], rights[1][...], preferred_element_type=jnp.float32))
    start = 0
    for out in outs:
        width = out.shape[1]
        for k, part in enumerate(parts):
            low, high = max(start, k * units), min(start + width, (k + 1) * units)
            if low < high:
                out[:, low - start : high - start] = part[:, low - k * units : high - k * units]
        start += width
    for out, first in ((outs[0], firsts[0]), (outs[2], firsts[2])):

        @pl.when(pl.program_id(0) == place_of[1])
        def _(out=out, first=first):
            first[...] = out[...]

    strip = outs[0].shape[0] // 4
    at_z = pl.ds(pl.multiple_of(place_of[2] * strip, strip), strip)
    for out, first in ((outs[1], firsts[1]), (outs[3], firsts[3])):
        first[...] = out[at_z, :]


def products(*args):
    count, rows = args[0].shape
    units = args[4].shape[1]
    left = pl.BlockSpec((count // 4, rows), lambda tile: (tile, 0))
    right = pl.BlockSpec((rows, units), lambda tile: (0, 0))
    scalars = pl.BlockSpec(memory_space=pltpu.SMEM)
    widths = flow_widths(units)
    return pl.pallas_call(
        product_kernel,
        grid=(4,),
        out_shape=[jax.ShapeDtypeStruct((count, width), jnp.float32) for width in widths]
        + [jax.ShapeDtypeStruct((count // 4, width), jnp.float32) for width in widths],
        in_specs=[left] * 4 + [right] * 6 + [scalars] * 3,
        out_specs=[pl.BlockSpec((count // 4, width), lambda tile: (tile, 0)) for width in widths]
        + [
            pl.BlockSpec((count // 4, width), lambda tile: (0, 0))
            if k % 2 == 0
            else pl.BlockSpec((count // 16, width), lambda tile: (tile, 0))
            for k, width in enumerate(widths)
        ],
        scratch_shapes=[pltpu.VMEM((rows, units), jnp.bfloat16)] * 4,
        compiler_params=pltpu.CompilerParams(vmem_limit_bytes=44 << 20),
        cost_estimate=pl.CostEstimate(flops=12 * rows * count * units, bytes_accessed=28 << 20, transcendentals=0),
    )(*args)


def per_device(tokens, cotangent, lengths, gate_weight, up_weight, down_weight):
    seq_count = lengths.shape[0]
    row_count, width = tokens.shape
    total_seqs = seq_count * lax.axis_size("dp")
    clip_bound = 0.5 * math.sqrt(D * FFW * LEN)
    dp, tensor = lax.axis_index("dp"), lax.axis_index("tensor")
    y, z, x_lo = dp // 8, (dp // 2) % 4, dp % 2
    x_hi, core = tensor // 2, tensor % 2
    way = 1 - 2 * core
    half = row_count // 2
    strip = width // 32

    positions = jnp.arange(LEN, dtype=jnp.int32)
    live = (positions[None, :] < lengths[:, None]).reshape(row_count)[:, None]
    masked = cotangent * live.astype(jnp.bfloat16)

    def own_half(rows, start):
        return lax.dynamic_slice_in_dim(rows, start, half, 0).astype(jnp.float32)

    lanes = jnp.broadcast_to(live.astype(jnp.bfloat16), (row_count, 128))
    token_half = send(jnp.concatenate([own_half(tokens, core * half), own_half(lanes, core * half)], axis=1), RING_X)

    cot_half = send(own_half(cotangent, core * half), RING_X)

    hidden_act, d_gate, d_up, norms = block(True, (tokens, masked), gate_weight, up_weight, down_weight)
    own_input, other_input = input_part(core, gate_weight, up_weight, d_gate, d_up, norms)
    norm_pair = norms[:, 0] + send(norms[:, 0], CORES)

    column_at = jnp.arange(width // 2, dtype=jnp.int32)
    source = (column_at // strip) * (2 * strip) + later(x_lo, norms) * strip + column_at % strip
    pick = (jnp.arange(width, dtype=jnp.int32)[:, None] == source[None, :]).astype(jnp.bfloat16)

    def picked(rows):
        return lax.dot_general(
            pick, rows, (((0,), (1,)), ((), ())), preferred_element_type=jnp.float32
        ).astype(jnp.bfloat16)

    near_tokens, near_cot = picked(tokens), picked(masked)

    token_half = after(token_half, near_tokens, near_cot, own_input)
    cot_half = after(cot_half, near_tokens, near_cot, own_input)
    token_rest, cot_rest = send(token_half, CORES), send(cot_half, CORES)
    far_hidden, far_gate, far_up, far_tokens, far_masked = block(
        False, (token_half, token_rest, cot_half, cot_rest), gate_weight, up_weight, down_weight
    )
    norm_pair = after(norm_pair, far_hidden)
    norm_sq = norm_pair + send(norm_pair, X_HI)
    clip_ratio = jnp.sqrt(norm_sq) / clip_bound
    clip_factor = 1.0 / jnp.maximum(1.0, clip_ratio)
    far_cols, far_cot = picked(far_tokens), picked(far_masked)

    def row_weight(by_seq, shift, axis):
        row_seq = (jnp.arange(row_count, dtype=jnp.int32) // LEN + shift) % seq_count
        seqs = jnp.arange(seq_count, dtype=jnp.int32)
        spread = jnp.expand_dims(row_seq, axis) == jnp.expand_dims(seqs, 1 - axis)
        return jnp.sum(jnp.where(spread, jnp.expand_dims(by_seq, 1 - axis), 0.0), axis=axis, keepdims=True)

    near_mean = clip_factor / total_seqs
    far_mean = send(near_mean, X_LO)
    shift = core * (seq_count // 2)
    grads = products(
        near_tokens, far_cols, near_cot, far_cot, d_gate, far_gate, d_up, far_up, hidden_act, far_hidden,
        near_mean, far_mean, jnp.stack([shift, (y + 3 * way) % 4, (z + 3 * way) % 4]),
    )
    units = d_gate.shape[1]
    parts = [first.reshape(4, strip, first.shape[1]) for first in grads[4:]]
    grads = [grad.reshape(4, 4, strip, grad.shape[1]) for grad in grads[:4]]

    def line(rows, axis=0):
        return lambda k: lax.dynamic_index_in_dim(rows, k, axis, keepdims=False)

    flows = [
        (line(grad, 0), y, RING_Y, z, RING_Z) if k % 2 == 0 else (line(grad, 1), z, RING_Z, y, RING_Y)
        for k, grad in enumerate(grads)
    ]
    rings = [Ring(take, here, way, route, part) for (take, here, route, _, _), part in zip(flows, parts)]

    part = own_input + send(other_input, CORES)
    across = after(lax.dynamic_index_in_dim(part, 1 - x_hi, 0, keepdims=False), far_mean)
    summed_input = send(across, X_HI)
    summed_input = summed_input + lax.dynamic_index_in_dim(part, x_hi, 0, keepdims=False)
    for _ in range(3):
        for ring in rings:
            ring.step()
    rows = together(*[ring.part for ring in rings])
    rings = [Ring(line(row), here, way, route) for row, (_, _, _, here, route) in zip(rows, flows)]
    for turn in range(3):
        for ring in rings:
            ring.step()
        if turn == 0:
            clip_late = after(clip_factor, *[ring.part for ring in rings])
    input_grad = (summed_input * row_weight(clip_late, 0, 0)).T.astype(jnp.bfloat16)
    sums = jnp.concatenate([ring.part for ring in rings], axis=1)
    grad_gate, grad_up = sums[:, :units], sums[:, units : 2 * units]
    grad_down = sums[:, 2 * units :].T
    return (input_grad, clip_ratio, grad_gate, grad_up, grad_down)


def solution(mesh):
    placed = (
        P("dp", None),
        P("dp", None),
        P("dp"),
        P(None, "tensor"),
        P(None, "tensor"),
        P("tensor", None),
    )
    return jax.shard_map(
        per_device,
        mesh=mesh,
        in_specs=placed,
        out_specs=(
            P("dp", "tensor"),
            P("dp"),
            P("dp", "tensor"),
            P("dp", "tensor"),
            P("tensor", "dp"),
        ),
        check_vma=False,
    )
```

```python
import functools
import math

import jax
import jax.numpy as jnp
from jax import lax
from jax.experimental import pallas as pl
from jax.experimental.pallas import tpu as pltpu
from jax.sharding import PartitionSpec as P

D = 2304
FFW = 4608
LEN = 64
AXES = ("dp", "tensor")


def place(y, z, x, core):
    y, z, x = y % 4, z % 4, x % 4
    return ((y * 4 + z) * 2 + x % 2) * 4 + (x // 2) * 2 + core


def pairs(target):
    return [
        (place(y, z, x, core), place(*target(y, z, x, core)))
        for y in range(4)
        for z in range(4)
        for x in range(4)
        for core in range(2)
    ]


RING_YZ = pairs(
    lambda y, z, x, core: (y, z + 1 - 2 * core, x, core) if x % 2 == 0 else (y + 1 - 2 * core, z, x, core)
)
RING_Y = pairs(lambda y, z, x, core: (y + 1 - 2 * core, z, x, core))
RING_Z = pairs(lambda y, z, x, core: (y, z + 1 - 2 * core, x, core))
RING_X = pairs(lambda y, z, x, core: (y, z, x + 1 - 2 * core, core))
CORES = pairs(lambda y, z, x, core: (y, z, x, 1 - core))
X_LO = pairs(lambda y, z, x, core: (y, z, x ^ 1, core))
X_HI = pairs(lambda y, z, x, core: (y, z, x ^ 2, core))


def send(value, route):
    return lax.optimization_barrier(lax.ppermute(lax.optimization_barrier(value), AXES, route))


def nothing(*refs):
    pass


def after(value, *others):
    anywhere = pl.BlockSpec(memory_space=pl.ANY)
    return pl.pallas_call(
        nothing,
        out_shape=jax.ShapeDtypeStruct(value.shape, value.dtype),
        in_specs=[anywhere] * (1 + len(others)),
        out_specs=anywhere,
        input_output_aliases={0: 0},
        cost_estimate=pl.CostEstimate(flops=0, bytes_accessed=0, transcendentals=0),
        compiler_params=pltpu.CompilerParams(vmem_limit_bytes=1 << 20),
    )(value, *others)


def together(*values):
    anywhere = pl.BlockSpec(memory_space=pl.ANY)
    return pl.pallas_call(
        nothing,
        out_shape=[jax.ShapeDtypeStruct(value.shape, value.dtype) for value in values],
        in_specs=[anywhere] * len(values),
        out_specs=[anywhere] * len(values),
        input_output_aliases={k: k for k in range(len(values))},
        cost_estimate=pl.CostEstimate(flops=0, bytes_accessed=0, transcendentals=0),
        compiler_params=pltpu.CompilerParams(vmem_limit_bytes=1 << 20),
    )(*values)


def later(index, *others):
    return after(jnp.reshape(index, (1,)), *others)[0]


def gelu_parts(pre_act):
    slope_k = math.sqrt(2.0 / math.pi)
    cubed = pre_act * pre_act * pre_act
    tanh_val = jnp.tanh(slope_k * (pre_act + 0.044715 * cubed))
    gelu_value = 0.5 * pre_act * (1.0 + tanh_val)
    gelu_slope = 0.5 * (1.0 + tanh_val) + 0.5 * pre_act * (1.0 - tanh_val * tanh_val) * slope_k * (
        1.0 + 3.0 * 0.044715 * pre_act * pre_act
    )
    return (gelu_value, gelu_slope)


def cross_rows(left, right):
    return lax.dot_general(
        left, right, (((0,), (0,)), ((), ())), preferred_element_type=jnp.float32
    )


def by_block(rows, width):
    half = rows.shape[0] // 2
    return [
        lax.dot_general(part, part, (((1,), (1,)), ((), ())), preferred_element_type=jnp.float32)
        for part in (rows[:half], rows[half:])
    ]


def block_kernel(near, *refs):
    if near:
        tokens, masked, gate_w, up_w, down_w, hidden, d_gate, d_up, norms = refs[:9]
        tokens_v, masked_v, gate_v, up_v, down_v, pair_gram, hidden_gram, sems = refs[9:]
    else:
        fetched, (gate_w, up_w, down_w, hidden, d_gate, d_up, tokens_v, masked_v) = refs[:4], refs[4:12]
        wide, (gate_v, up_v, down_v, sems) = refs[12:16], refs[16:]
    units = gate_w.shape[1]
    tile = 256
    full, tail = units // tile, units % tile
    spans = [(k * tile, tile) for k in range(full)] + ([(full * tile, tail)] if tail else [])

    def copies(k, start, size):
        cols = pl.ds(start, size)
        return (
            pltpu.make_async_copy(gate_w.at[:, cols], gate_v.at[:, cols], sems.at[0, k]),
            pltpu.make_async_copy(up_w.at[:, cols], up_v.at[:, cols], sems.at[1, k]),
            pltpu.make_async_copy(down_w.at[cols, :], down_v.at[cols, :], sems.at[2, k]),
        )

    moves = ((tokens, tokens_v), (masked, masked_v)) if near else zip(fetched, wide)
    rows_in = [
        pltpu.make_async_copy(source, target, sems.at[k % 3, len(spans) + k // 3])
        for k, (source, target) in enumerate(moves)
    ]
    for copy in rows_in:
        copy.start()
    for k, (start, size) in enumerate(spans):
        for copy in copies(k, start, size):
            copy.start()
    for copy in rows_in:
        copy.wait()
    if not near:
        half, width = tokens_v.shape[0] // 2, tokens_v.shape[1]
        for k in range(2):
            rows, mask = slice(k * half, (k + 1) * half), wide[k][:, width : width + 1]
            tokens_v[rows, :] = (wide[k][:, :width] * mask).astype(jnp.bfloat16)
            masked_v[rows, :] = (wide[2 + k][...] * mask).astype(jnp.bfloat16)
    if near:
        pair_gram[...] = jnp.zeros_like(pair_gram)
        hidden_gram[...] = jnp.zeros_like(hidden_gram)

    def work(k, start, size):
        for copy in copies(k, start, size):
            copy.wait()
        cols = pl.ds(start, size)
        gate_pre = jnp.dot(tokens_v[...], gate_v[:, cols], preferred_element_type=jnp.float32)
        up_pre = jnp.dot(tokens_v[...], up_v[:, cols], preferred_element_type=jnp.float32)
        d_hidden = lax.dot_general(
            masked_v[...], down_v[cols, :], (((1,), (1,)), ((), ())), preferred_element_type=jnp.float32
        )
        gelu_value, gelu_slope = gelu_parts(gate_pre)
        gate_rows = (d_hidden * up_pre * gelu_slope).astype(jnp.bfloat16)
        up_rows = (d_hidden * gelu_value).astype(jnp.bfloat16)
        hidden_rows = (gelu_value * up_pre).astype(jnp.bfloat16)
        hidden[:, cols], d_gate[:, cols], d_up[:, cols] = hidden_rows, gate_rows, up_rows
        if near:
            for k, (gate_gram, up_gram, own_gram) in enumerate(
                zip(by_block(gate_rows, size), by_block(up_rows, size), by_block(hidden_rows, size))
            ):
                pair_gram[k] += gate_gram + up_gram
                hidden_gram[k] += own_gram

    if full:
        lax.fori_loop(0, full, lambda k, _: (work(k, pl.multiple_of(k * tile, tile), tile), 0)[1], 0)
    if tail:
        work(full, full * tile, tail)
    if near:
        half = tokens_v.shape[0] // 2
        row_seq = lax.broadcasted_iota(jnp.int32, (half, half), 0) // LEN
        col_seq = lax.broadcasted_iota(jnp.int32, (half, half), 1) // LEN
        token_grams, masked_grams = by_block(tokens_v[...], 0), by_block(masked_v[...], 0)
        for k in range(2):
            total = token_grams[k] * pair_gram[k] + masked_grams[k] * hidden_gram[k]
            for seq in range(half // LEN):
                own = jnp.where((row_seq == seq) & (col_seq == seq), total, 0.0)
                lanes = jnp.sum(own, axis=0, keepdims=True)
                at = k * (half // LEN) + seq
                norms[at : at + 1, :] = jnp.broadcast_to(
                    jnp.sum(lanes, axis=1, keepdims=True), (1, norms.shape[1])
                )


def block(near, rows_in, gate_weight, up_weight, down_weight):
    units, width = down_weight.shape
    rows = rows_in[0].shape[0] * (1 if near else 2)
    count = units // 256 + (1 if units % 256 else 0)
    anywhere, here = pl.BlockSpec(memory_space=pl.ANY), pl.BlockSpec(memory_space=pltpu.VMEM)
    hidden = jax.ShapeDtypeStruct((rows, units), jnp.bfloat16)
    whole = jax.ShapeDtypeStruct((rows, width), jnp.bfloat16)
    grams = [pltpu.VMEM((2, rows // 2, rows // 2), jnp.float32)] * 2
    args = (*rows_in, gate_weight, up_weight, down_weight)
    more = [jax.ShapeDtypeStruct((rows // LEN, 128), jnp.float32)] if near else [whole] * 2
    return pl.pallas_call(
        functools.partial(block_kernel, near),
        out_shape=[hidden] * 3 + more,
        in_specs=[anywhere] * len(args),
        out_specs=[here] * (3 + len(more)),
        scratch_shapes=[pltpu.VMEM(array.shape, array.dtype) for array in args]
        + (grams if near else [])
        + [pltpu.SemaphoreType.DMA((3, count + 2))],
        compiler_params=pltpu.CompilerParams(vmem_limit_bytes=(44 if near else 50) << 20),
        cost_estimate=pl.CostEstimate(flops=0, bytes_accessed=0, transcendentals=0),
    )(*args)


def input_kernel(core, gate_w, up_w, d_gate, d_up, last, own, other):
    total = lax.dot_general(gate_w[...], d_gate[...], (((1,), (1,)), ((), ())), preferred_element_type=jnp.float32)
    total += lax.dot_general(up_w[...], d_up[...], (((1,), (1,)), ((), ())), preferred_element_type=jnp.float32)

    @pl.when(pl.program_id(1) == 0)
    def _():
        own[0] = total

    @pl.when(pl.program_id(1) == 1)
    def _():
        other[0] = total


def input_part(core, gate_weight, up_weight, d_gate, d_up, last):
    width, units = gate_weight.shape
    rows = d_gate.shape[0]
    whole = pl.BlockSpec((rows, units), lambda x, turn, core: (0, 0))
    part = pl.BlockSpec((width // 4, units), lambda x, turn, core: (x * 2 + lax.rem(turn + core[0], 2), 0))
    out = pl.BlockSpec((1, width // 4, rows), lambda x, turn, core: (x, 0, 0))
    shape = jax.ShapeDtypeStruct((2, width // 4, rows), jnp.float32)
    return pl.pallas_call(
        input_kernel,
        grid_spec=pltpu.PrefetchScalarGridSpec(
            num_scalar_prefetch=1,
            grid=(2, 2),
            in_specs=[part, part, whole, whole, pl.BlockSpec(memory_space=pl.ANY)],
            out_specs=[out, out],
        ),
        out_shape=[shape, shape],
        compiler_params=pltpu.CompilerParams(vmem_limit_bytes=32 << 20),
        cost_estimate=pl.CostEstimate(flops=0, bytes_accessed=0, transcendentals=0),
    )(core.reshape(1).astype(jnp.int32), gate_weight, up_weight, d_gate, d_up, last)


class Ring:
    def __init__(self, take, here, way, route, part=None):
        self.take, self.here, self.way, self.route = take, here, way, route
        self.hops = 3
        self.part = take((here + 3 * way) % 4) if part is None else part

    def step(self, *others):
        self.hops -= 1
        part = send(self.part, self.route) + self.take((self.here + self.hops * self.way) % 4)
        self.part = after(part, *others) if others else part


def flow_widths(units):
    tiles = 3 * units // 128
    return [(tiles + 3 - k) // 4 * 128 for k in range(4)]


def product_kernel(
    near_t, far_t, near_c, far_c, d_gate, far_gate, d_up, far_up, hidden, far_hidden, near_s, far_s, place_of, *refs
):
    outs, firsts, scaled = refs[:4], refs[4:8], refs[8:]
    rows = hidden.shape[0]
    seq_count = rows // LEN

    def spread(by_seq, shift_by, axis):
        shape = (rows, 1) if axis == 0 else (1, rows)
        row_seq = lax.broadcasted_iota(jnp.int32, shape, axis) // LEN + shift_by
        row_seq = jnp.where(row_seq >= seq_count, row_seq - seq_count, row_seq)
        weight = jnp.zeros(shape, jnp.float32)
        for seq in range(seq_count):
            weight = jnp.where(row_seq == seq, by_seq[seq], weight)
        return weight

    @pl.when(pl.program_id(0) == 0)
    def _():
        weights = [spread(near_s, 0, 0), spread(far_s, place_of[0], 0)]
        for rows_of, weight, into in zip((d_gate, far_gate, d_up, far_up), weights * 2, scaled):
            into[...] = (rows_of[...].astype(jnp.float32) * weight).astype(jnp.bfloat16)

    near_cot = (near_c[...].astype(jnp.float32) * spread(near_s, 0, 1)).astype(jnp.bfloat16)
    far_cot = (far_c[...].astype(jnp.float32) * spread(far_s, place_of[0], 1)).astype(jnp.bfloat16)
    units = hidden.shape[1]
    parts = []
    for lefts, rights in (
        ((near_t[...], far_t[...]), scaled[:2]),
        ((near_t[...], far_t[...]), scaled[2:]),
        ((near_cot, far_cot), (hidden, far_hidden)),
    ):
        total = jnp.dot(lefts[0], rights[0][...], preferred_element_type=jnp.float32)
        parts.append(total + jnp.dot(lefts[1], rights[1][...], preferred_element_type=jnp.float32))
    start = 0
    for out in outs:
        width = out.shape[1]
        for k, part in enumerate(parts):
            low, high = max(start, k * units), min(start + width, (k + 1) * units)
            if low < high:
                out[:, low - start : high - start] = part[:, low - k * units : high - k * units]
        start += width
    for out, first in ((outs[0], firsts[0]), (outs[2], firsts[2])):

        @pl.when(pl.program_id(0) == place_of[1])
        def _(out=out, first=first):
            first[...] = out[...]

    strip = outs[0].shape[0] // 4
    at_z = pl.ds(pl.multiple_of(place_of[2] * strip, strip), strip)
    for out, first in ((outs[1], firsts[1]), (outs[3], firsts[3])):
        first[...] = out[at_z, :]


def products(*args):
    count, rows = args[0].shape
    units = args[4].shape[1]
    left = pl.BlockSpec((count // 4, rows), lambda tile: (tile, 0))
    right = pl.BlockSpec((rows, units), lambda tile: (0, 0))
    scalars = pl.BlockSpec(memory_space=pltpu.SMEM)
    widths = flow_widths(units)
    return pl.pallas_call(
        product_kernel,
        grid=(4,),
        out_shape=[jax.ShapeDtypeStruct((count, width), jnp.float32) for width in widths]
        + [jax.ShapeDtypeStruct((count // 4, width), jnp.float32) for width in widths],
        in_specs=[left] * 4 + [right] * 6 + [scalars] * 3,
        out_specs=[pl.BlockSpec((count // 4, width), lambda tile: (tile, 0)) for width in widths]
        + [
            pl.BlockSpec((count // 4, width), lambda tile: (0, 0))
            if k % 2 == 0
            else pl.BlockSpec((count // 16, width), lambda tile: (tile, 0))
            for k, width in enumerate(widths)
        ],
        scratch_shapes=[pltpu.VMEM((rows, units), jnp.bfloat16)] * 4,
        compiler_params=pltpu.CompilerParams(vmem_limit_bytes=44 << 20),
        cost_estimate=pl.CostEstimate(flops=12 * rows * count * units, bytes_accessed=28 << 20, transcendentals=0),
    )(*args)


def per_device(tokens, cotangent, lengths, gate_weight, up_weight, down_weight):
    seq_count = lengths.shape[0]
    row_count, width = tokens.shape
    total_seqs = seq_count * lax.axis_size("dp")
    clip_bound = 0.5 * math.sqrt(D * FFW * LEN)
    dp, tensor = lax.axis_index("dp"), lax.axis_index("tensor")
    y, z, x_lo = dp // 8, (dp // 2) % 4, dp % 2
    x_hi, core = tensor // 2, tensor % 2
    way = 1 - 2 * core
    half = row_count // 2
    strip = width // 32

    positions = jnp.arange(LEN, dtype=jnp.int32)
    live = (positions[None, :] < lengths[:, None]).reshape(row_count)[:, None]
    masked = cotangent * live.astype(jnp.bfloat16)

    def own_half(rows, start):
        return lax.dynamic_slice_in_dim(rows, start, half, 0).astype(jnp.float32)

    lanes = jnp.broadcast_to(live.astype(jnp.bfloat16), (row_count, 128))
    token_half = send(jnp.concatenate([own_half(tokens, core * half), own_half(lanes, core * half)], axis=1), RING_X)

    cot_half = send(own_half(cotangent, core * half), RING_X)

    hidden_act, d_gate, d_up, norms = block(True, (tokens, masked), gate_weight, up_weight, down_weight)
    own_input, other_input = input_part(core, gate_weight, up_weight, d_gate, d_up, norms)
    norm_pair = norms[:, 0] + send(norms[:, 0], CORES)

    column_at = jnp.arange(width // 2, dtype=jnp.int32)
    source = (column_at // strip) * (2 * strip) + later(x_lo, norms) * strip + column_at % strip
    pick = (jnp.arange(width, dtype=jnp.int32)[:, None] == source[None, :]).astype(jnp.bfloat16)

    def picked(rows):
        return lax.dot_general(
            pick, rows, (((0,), (1,)), ((), ())), preferred_element_type=jnp.float32
        ).astype(jnp.bfloat16)

    near_tokens, near_cot = picked(tokens), picked(masked)

    token_half = after(token_half, near_tokens, near_cot, own_input)
    cot_half = after(cot_half, near_tokens, near_cot, own_input)
    token_rest, cot_rest = send(token_half, CORES), send(cot_half, CORES)
    far_hidden, far_gate, far_up, far_tokens, far_masked = block(
        False, (token_half, token_rest, cot_half, cot_rest), gate_weight, up_weight, down_weight
    )
    norm_pair = after(norm_pair, far_hidden)
    norm_sq = norm_pair + send(norm_pair, X_HI)
    clip_ratio = jnp.sqrt(norm_sq) / clip_bound
    clip_factor = 1.0 / jnp.maximum(1.0, clip_ratio)
    far_cols, far_cot = picked(far_tokens), picked(after(far_masked, clip_factor))

    def row_weight(by_seq, shift, axis):
        row_seq = (jnp.arange(row_count, dtype=jnp.int32) // LEN + shift) % seq_count
        seqs = jnp.arange(seq_count, dtype=jnp.int32)
        spread = jnp.expand_dims(row_seq, axis) == jnp.expand_dims(seqs, 1 - axis)
        return jnp.sum(jnp.where(spread, jnp.expand_dims(by_seq, 1 - axis), 0.0), axis=axis, keepdims=True)

    near_mean = clip_factor / total_seqs
    far_mean = send(near_mean, X_LO)
    shift = core * (seq_count // 2)
    grads = products(
        near_tokens, far_cols, near_cot, far_cot, d_gate, far_gate, d_up, far_up, hidden_act, far_hidden,
        near_mean, far_mean, jnp.stack([shift, (y + 3 * way) % 4, (z + 3 * way) % 4]),
    )
    units = d_gate.shape[1]
    parts = [first.reshape(4, strip, first.shape[1]) for first in grads[4:]]
    grads = [grad.reshape(4, 4, strip, grad.shape[1]) for grad in grads[:4]]

    def line(rows, axis=0):
        return lambda k: lax.dynamic_index_in_dim(rows, k, axis, keepdims=False)

    flows = [
        (line(grad, 0), y, RING_Y, z, RING_Z) if k % 2 == 0 else (line(grad, 1), z, RING_Z, y, RING_Y)
        for k, grad in enumerate(grads)
    ]
    rings = [Ring(take, here, way, route, part) for (take, here, route, _, _), part in zip(flows, parts)]

    part = own_input + send(other_input, CORES)
    across = after(lax.dynamic_index_in_dim(part, 1 - x_hi, 0, keepdims=False), far_mean)
    summed_input = send(across, X_HI)
    summed_input = summed_input + lax.dynamic_index_in_dim(part, x_hi, 0, keepdims=False)
    for _ in range(3):
        for ring in rings:
            ring.step()
    rows = together(*[ring.part for ring in rings])
    rings = [Ring(line(row), here, way, route) for row, (_, _, _, here, route) in zip(rows, flows)]
    for turn in range(3):
        for ring in rings:
            ring.step()
        if turn == 0:
            clip_late = after(clip_factor, *[ring.part for ring in rings])
    input_grad = (summed_input * row_weight(clip_late, 0, 0)).T.astype(jnp.bfloat16)
    sums = jnp.concatenate([ring.part for ring in rings], axis=1)
    grad_gate, grad_up = sums[:, :units], sums[:, units : 2 * units]
    grad_down = sums[:, 2 * units :].T
    return (input_grad, clip_ratio, grad_gate, grad_up, grad_down)


def solution(mesh):
    placed = (
        P("dp", None),
        P("dp", None),
        P("dp"),
        P(None, "tensor"),
        P(None, "tensor"),
        P("tensor", None),
    )
    return jax.shard_map(
        per_device,
        mesh=mesh,
        in_specs=placed,
        out_specs=(
            P("dp", "tensor"),
            P("dp"),
            P("dp", "tensor"),
            P("dp", "tensor"),
            P("tensor", "dp"),
        ),
        check_vma=False,
    )
```
